128 devices in a mesh: gx: 32 (over z, y, core), gy: 4 (over x).
Axes of the slice: x: 4, y: 4, z: 4, core: 2. Of those that a mesh axis runs over, the one named last changes fastest.
Arguments:
- source: float32 [512, 256, 128], P('gx', 'gy'), may hold values from -6 to 6
- density: float32 [512, 256, 128], P('gx', 'gy'), may hold values from 0.5 to 5
- darcy_drag: float32 [512, 256, 128], P('gx', 'gy'), may hold values from 1 to 30
- porous_rows: int32 [256], P('gy'), may hold values 0 or 1
Outputs:
- solution: float32 [512, 256, 128], P('gx', 'gy')
- residual: float32 [512, 256, 128], P('gx', 'gy')
The draws below stay inside these ranges and needn't reach their ends.
Inputs may be any that keep to these rules, and one draw needn't show every extreme that they name: `porous_rows`: 1 marks a wall-normal index inside the porous layer, 0 one outside.
All inputs are finite; a program needn't handle non-finite values. No bound on the sum of `porous_rows` on one device may be relied on, other than what follows from the above.
Results may differ from the reference program's by a relative error of at most 0.0003.
Values sent between devices are 32-bit elements; how exact they have to be, the bound alone decides.
No kernel may reach another device: no remote copies, remote signals or barrier semaphores. Data moves between devices by JAX's collectives and lax.ppermute only.
A program may use at most 192 MiB of HBM per device.

```python
import math
import jax
import jax.numpy as jnp

CZ = 128
LEVELS = 7
SWEEPS_COARSE = 16
NX = 512
NY = 256


def touch_ends(result, own_key, least, high):
    dims = result.shape
    index_at = [jax.random.randint(jax.random.fold_in(own_key, axis), (), 0, dims[axis]) for axis in range(len(dims))]
    result = result.at[tuple(index_at)].set(least)
    longest = dims.index(max(dims))
    index_at[longest] = (index_at[longest] + 1) % dims[longest]
    return result.at[tuple(index_at)].set(high)


def steps_of(key, dims, cuts, smallest, largest):
    level = 1.0
    for axis_at, shards_of in cuts:
        heights = jax.random.uniform(jax.random.fold_in(jax.random.fold_in(key, 6), axis_at), (shards_of,), jnp.float32, smallest / len(cuts), largest / len(cuts))
        level = level * jnp.repeat(jnp.exp(heights), dims[axis_at] // shards_of).reshape((-1,) + (1,) * (len(dims) - 1 - axis_at))
    return level


def gaussian(rng, shape, spread, reach, cuts=(), held_as=jnp.bfloat16):
    array = spread * jax.random.normal(rng, shape, jnp.float32)
    if cuts:
        array = array * steps_of(rng, shape, cuts, -0.22, 0.18)
    return jnp.clip(array, -reach, reach).astype(held_as)


def setup_inputs(seed: int = 0) -> dict:
    streams_of = jax.random.split(jax.random.key(seed), 5)
    return {
        "source": gaussian(streams_of[0], (NX, NY, CZ), 1.0, 6.0, ((0, 32), (1, 4)), jnp.float32),
        "density": jnp.clip(jnp.exp(math.log(5.0) - 2.3025851 * jax.random.uniform(streams_of[1], (NX, NY, CZ), jnp.float32) ** steps_of(streams_of[1], (NX, NY, CZ), ((0, 32), (1, 4)), -0.2, 0.2)), 0.5, 5.0),
        "darcy_drag": jnp.clip(jnp.exp(math.log(30.0) - 3.4011974 * jax.random.uniform(streams_of[2], (NX, NY, CZ), jnp.float32) ** steps_of(streams_of[2], (NX, NY, CZ), ((0, 32), (1, 4)), -0.2, 0.2)), 1.0, 30.0),
        "porous_rows": touch_ends((jax.random.randint(streams_of[3], (NY,), 0, 2) < 1).astype(jnp.int32), jax.random.fold_in(streams_of[3], 1), 0, 1),
    }


damping = 0.8
helmholtz_base = 2e-4


def zero_pad(values):
    return jnp.pad(values, ((1, 1), (1, 1), (0, 0)))


def face_coeffs(padded):
    centre = padded[1:-1, 1:-1, :]

    def harmonic(neighbour):
        return 2.0 * centre * neighbour / (centre + neighbour)

    return (harmonic(padded[2:, 1:-1, :]), harmonic(padded[:-2, 1:-1, :]),
            harmonic(padded[1:-1, 2:, :]), harmonic(padded[1:-1, :-2, :]),
            harmonic(jnp.roll(centre, -1, 2)), harmonic(jnp.roll(centre, 1, 2)))


def operate(padded, face_list, helmholtz):
    values = padded[1:-1, 1:-1, :]
    beside = (padded[2:, 1:-1, :], padded[:-2, 1:-1, :], padded[1:-1, 2:, :],
              padded[1:-1, :-2, :], jnp.roll(values, -1, 2), jnp.roll(values, 1, 2))
    applied = helmholtz * values
    for coeff, neighbour in zip(face_list, beside):
        applied = applied + coeff * (values - neighbour)
    return applied


def halving(shape):
    return tuple(2 if length % 2 == 0 and length > 1 else 1 for length in shape)


def coarsen(values):
    split_shape = []
    for length, stride in zip(values.shape, halving(values.shape)):
        split_shape += [length // stride, stride]
    return jnp.mean(values.reshape(split_shape), axis=(1, 3, 5))


def refine(values, factor):
    for axis_num, stride in enumerate(factor):
        values = jnp.repeat(values, stride, axis=axis_num)
    return values


def smooth_cycle(tier_index, source, conduct):
    face_list = face_coeffs(zero_pad(conduct))
    helmholtz = helmholtz_base * 4.0 ** tier_index
    diagonal = helmholtz + sum(face_list)

    def residual_of(current):
        return source - operate(zero_pad(current), face_list, helmholtz)

    if tier_index == LEVELS - 1:
        current = jnp.zeros_like(source)
        for _ in range(SWEEPS_COARSE):
            current = current + damping * residual_of(current) / diagonal
        return current
    current = damping * source / diagonal
    current = current + damping * residual_of(current) / diagonal
    remain = residual_of(current)
    factor = halving(source.shape)
    correction = smooth_cycle(tier_index + 1, 4.0 * coarsen(remain), coarsen(conduct))
    current = current + refine(correction, factor)
    for _ in range(2):
        current = current + damping * residual_of(current) / diagonal
    return current


def reference(source, density, darcy_drag, porous_rows):
    conduct = 1.0 / (density * (1.0 + darcy_drag * porous_rows.astype(jnp.float32)[None, :, None]))
    solution = smooth_cycle(0, source, conduct)
    face_list = face_coeffs(zero_pad(conduct))
    residual = source - operate(zero_pad(solution), face_list, helmholtz_base)
    return solution, residual
```

```python
import functools

import jax
import jax.numpy as jnp
from jax import lax
from jax.experimental import pallas as pl
from jax.experimental.pallas import tpu as pltpu
from jax.sharding import PartitionSpec as P

SWEEPS_COARSE = 16
DAMP = 0.8
KEEP = 1.0 - DAMP
H0 = 0.0002

NX, NY, NZ = 16, 64, 128
F32 = jnp.float32
VMEM = pl.BlockSpec(memory_space=pltpu.VMEM)


def call(body, outs, scratch, args, name, vmem):
    return pl.pallas_call(
        body,
        out_shape=[jax.ShapeDtypeStruct(s, F32) for s in outs],
        in_specs=[VMEM] * len(args),
        out_specs=[VMEM] * len(outs),
        scratch_shapes=[pltpu.VMEM(s, F32) for s in scratch],
        compiler_params=pltpu.CompilerParams(vmem_limit_bytes=vmem * 2**20),
        name=name,
    )(*args)


def recip(t):
    r = pl.reciprocal(t, approx=True)
    r = r * (2.0 - t * r)
    return r * (2.0 - t * r)


def harmonic(a, b):
    return (2.0 * a) * b * recip(jnp.maximum(a + b, 1e-30))


def lane(shape):
    return lax.broadcasted_iota(jnp.int32, shape, len(shape) - 1)


def lroll(v, shift):
    return pltpu.roll(v, shift % 128, v.ndim - 1)


def pair_lanes(v, s):
    first = (lane(v.shape) // s) % 2 == 0
    return v + jnp.where(first, lroll(v, -s), lroll(v, s))


def rows(lo, hi, body, unroll=1):
    def step(x, carry):
        body(x)
        return carry

    lax.fori_loop(lo, hi, step, 0, unroll=unroll)


def chunks(ys, ye, size):
    return [(y, min(size, ye - y)) for y in range(ys, ye, size)]


class Level:
    def __init__(self, depth, c, b, fx, fy, fz, fzm, w, ys, ye, size):
        self.h = H0 * 4.0**depth
        self.s = 2**depth
        self.c, self.b, self.fx, self.fy, self.fz, self.fzm, self.w = c, b, fx, fy, fz, fzm, w
        self.parts = chunks(ys, ye, size)

    def faces(self, lo, hi):
        def body(x):
            for y, n in self.parts:
                c = self.c[x, pl.ds(y, n), :]
                self.fx[x, pl.ds(y, n), :] = harmonic(c, self.c[x + 1, pl.ds(y, n), :])
                self.fy[x, pl.ds(y, n), :] = harmonic(c, self.c[x, pl.ds(y + 1, n), :])
                fz = harmonic(c, lroll(c, -self.s))
                self.fz[x, pl.ds(y, n), :] = fz
                self.fzm[x, pl.ds(y, n), :] = lroll(fz, self.s)

        rows(lo, hi, body)

    def weights(self, lo, hi, start=None):
        def body(x):
            for y, n in self.parts:
                here = pl.ds(y, n)
                d = self.fx[x, here, :] + self.fx[x - 1, here, :]
                d = d + self.fy[x, here, :] + self.fy[x, pl.ds(y - 1, n), :]
                d = d + self.fz[x, here, :] + self.fzm[x, here, :]
                w = DAMP * recip(self.h + d)
                self.w[x, here, :] = w
                if start is not None:
                    start[x, here, :] = w * self.b[x, here, :]

        rows(lo, hi, body)

    def flux(self, u, x, y, n):
        here = pl.ds(y, n)
        v = u[x, here, :]
        acc = self.fx[x, here, :] * u[x + 1, here, :]
        acc = acc + self.fx[x - 1, here, :] * u[x - 1, here, :]
        acc = acc + self.fy[x, here, :] * u[x, pl.ds(y + 1, n), :]
        acc = acc + self.fy[x, pl.ds(y - 1, n), :] * u[x, pl.ds(y - 1, n), :]
        acc = acc + self.fz[x, here, :] * lroll(v, -self.s)
        acc = acc + self.fzm[x, here, :] * lroll(v, self.s)
        return v, acc

    def sweep(self, u, out, lo, hi):
        def body(x):
            for y, n in self.parts:
                here = pl.ds(y, n)
                v, acc = self.flux(u, x, y, n)
                out[x, here, :] = KEEP * v + self.w[x, here, :] * (self.b[x, here, :] + acc)

        rows(lo, hi, body)

    def residual(self, u, x, y, n):
        here = pl.ds(y, n)
        v = u[x, here, :]
        r = self.b[x, here, :] - self.h * v
        r = r + self.fx[x, here, :] * (u[x + 1, here, :] - v)
        r = r + self.fx[x - 1, here, :] * (u[x - 1, here, :] - v)
        r = r + self.fy[x, here, :] * (u[x, pl.ds(y + 1, n), :] - v)
        r = r + self.fy[x, pl.ds(y - 1, n), :] * (u[x, pl.ds(y - 1, n), :] - v)
        r = r + self.fz[x, here, :] * (lroll(v, -self.s) - v)
        return r + self.fzm[x, here, :] * (lroll(v, self.s) - v)

    def restrict(self, u, tmp, out, count, x_from, x_to, rows_from):
        def body(k):
            x = x_from + 2 * k
            for y, n in self.parts:
                tmp[pl.ds(y, n), :] = self.residual(u, x, y, n) + self.residual(u, x + 1, y, n)
            half = tmp.shape[0] // 2
            t = tmp[pl.ds(0, half, stride=2), :] + tmp[pl.ds(1, half, stride=2), :]
            out[x_to + k, pl.ds(8, half), :] = 0.5 * pair_lanes(t, self.s)

        rows(0, count, body)

    def restrict_c(self, tmp, out, count, x_from, x_to):
        def body(k):
            x = x_from + 2 * k
            tmp[...] = self.c[x] + self.c[x + 1]
            half = tmp.shape[0] // 2
            t = tmp[pl.ds(0, half, stride=2), :] + tmp[pl.ds(1, half, stride=2), :]
            out[x_to + k, pl.ds(8, half), :] = 0.125 * pair_lanes(t, self.s)

        rows(0, count, body)


def odd(axis):
    return lax.axis_index(axis) % 2


def begin_kernel(source, density, drag, porous, cond, ypack0, ypack1):
    o = odd("gy")
    at0 = pl.multiple_of((1 - o) * (NY - 8), 8)
    at1 = pl.multiple_of(o * (NY - 8), 8)

    def body(x):
        c = recip(density[x] * (1.0 + drag[x] * porous[...]))
        cond[x] = c
        ypack0[x] = cond[x, pl.ds(at0, 8), :]
        ypack1[x] = cond[x, pl.ds(at1, 8), :]
        ypack0[NX + x] = source[x, pl.ds(at0, 8), :]
        ypack1[NX + x] = source[x, pl.ds(at1, 8), :]

    rows(0, NX, body)


def edge_kernel(cond, source, y0, y1, xpack0, xpack1):
    ox, oy = odd("gx"), odd("gy")
    at0 = pl.multiple_of((1 - oy) * (NY + 8), 8)
    at1 = pl.multiple_of(oy * (NY + 8), 8)

    def put(pack, row, field, x, base):
        pack[row, pl.ds(8, NY), :] = field[x]
        pack[row, pl.ds(at0, 8), :] = y0[base + x]
        pack[row, pl.ds(at1, 8), :] = y1[base + x]

    def body_c(k):
        put(xpack0, k, cond, k + (1 - ox) * (NX - 11), 0)
        put(xpack1, k, cond, k + ox * (NX - 11), 0)

    def body_b(k):
        put(xpack0, 11 + k, source, k + (1 - ox) * (NX - 10), NX)
        put(xpack1, 11 + k, source, k + ox * (NX - 10), NX)

    rows(0, 11, body_c)
    rows(0, 10, body_b)


X0, Y0 = 12, 16
X1, Y1 = 6, 16
X2, Y2 = 6, 16


def down_kernel(
    cond, source, y0, y1, x0, x1,
    c0_out, b0_out, u0_out, c1, b1, u1, c2, b2, ypack0, ypack1,
    c, b, fx, fy, fz, fzm, w, ua, ub, tmp, gx_, gy_, gz_, gzm_, gw_, ga_, tmp1,
):
    ox, oy = odd("gx"), odd("gy")
    at0 = pl.multiple_of(8 + (1 - oy) * (NY + 8), 8)
    at1 = pl.multiple_of(8 + oy * (NY + 8), 8)

    def own(x):
        c[X0 + x, pl.ds(Y0, NY), :] = cond[x]
        c[X0 + x, pl.ds(at0, 8), :] = y0[x]
        c[X0 + x, pl.ds(at1, 8), :] = y1[x]
        b[X0 + x, pl.ds(Y0, NY), :] = source[x]
        b[X0 + x, pl.ds(at0, 8), :] = y0[NX + x]
        b[X0 + x, pl.ds(at1, 8), :] = y1[NX + x]

    rows(0, NX, own)

    def halo_c(k):
        c[k + 1 + (1 - ox) * (11 + NX), pl.ds(8, 80), :] = x0[k]
        c[k + 1 + ox * (11 + NX), pl.ds(8, 80), :] = x1[k]

    def halo_b(k):
        b[k + 2 + (1 - ox) * (10 + NX), pl.ds(8, 80), :] = x0[11 + k]
        b[k + 2 + ox * (10 + NX), pl.ds(8, 80), :] = x1[11 + k]

    rows(0, 11, halo_c)
    rows(0, 10, halo_b)
    zero = jnp.zeros((8, NZ), F32)

    def pads(x):
        c[x, pl.ds(0, 8), :] = zero
        c[x, pl.ds(88, 8), :] = zero
        fy[x, pl.ds(0, 8), :] = zero

    rows(0, 40, pads)

    top = Level(0, c, b, fx, fy, fz, fzm, w, 8, 88, 40)
    top.faces(1, 39)
    top.weights(2, 38, ua)
    top.sweep(ua, ub, 3, 37)

    def clear1(x):
        for ref in (c1, b1, u1):
            ref[x] = jnp.zeros((64, NZ), F32)
        gy_[x, pl.ds(0, 8), :] = zero

    rows(0, 20, clear1)

    def clear2(x):
        for ref in (c2, b2):
            ref[x] = jnp.zeros((48, NZ), F32)

    rows(0, 16, clear2)
    tmp[pl.ds(0, 8), :] = zero
    tmp[pl.ds(88, 8), :] = zero
    tmp1[pl.ds(0, 8), :] = zero
    tmp1[pl.ds(56, 8), :] = zero
    top.restrict(ub, tmp, b1, 16, 4, 2, None)
    top.restrict_c(tmp, c1, 18, 2, 1)

    def keep(x):
        c0_out[x] = c[X0 - 4 + x]
        b0_out[x] = b[X0 - 4 + x]
        u0_out[x] = ub[X0 - 4 + x]

    rows(0, 24, keep)

    mid = Level(1, c1, b1, gx_, gy_, gz_, gzm_, gw_, 8, 56, 48)
    mid.faces(1, 19)
    mid.weights(2, 18, ga_)
    mid.sweep(ga_, u1, 3, 17)
    mid.restrict(u1, tmp1, b2, 6, 4, 5, None)
    mid.restrict_c(tmp1, c2, 8, 2, 4)

    high, low = 28, 0
    e0 = Y1 + (1 - oy) * high
    e1 = Y1 + oy * high

    def edge1(x):
        ypack0[x, pl.ds(0, 4), :] = u1[X1 + x, pl.ds(e0, 4), :]
        ypack1[x, pl.ds(0, 4), :] = u1[X1 + x, pl.ds(e1, 4), :]
        ypack0[x, pl.ds(4, 4), :] = b1[X1 + x, pl.ds(e0, 4), :]
        ypack1[x, pl.ds(4, 4), :] = b1[X1 + x, pl.ds(e1, 4), :]

    rows(0, 8, edge1)
    f0 = pl.multiple_of(Y2 + (1 - oy) * 8, 8)
    f1 = pl.multiple_of(Y2 + oy * 8, 8)
    for x in range(6):
        ypack0[8 + x] = b2[X2 - 1 + x, pl.ds(f0, 8), :]
        ypack1[8 + x] = b2[X2 - 1 + x, pl.ds(f1, 8), :]
    for x in range(8):
        ypack0[14 + x] = c2[X2 - 2 + x, pl.ds(f0, 8), :]
        ypack1[14 + x] = c2[X2 - 2 + x, pl.ds(f1, 8), :]


def set_y1(u1, b1, y0, y1, oy, lo, hi):
    a0 = Y1 - 4 + (1 - oy) * 36
    a1 = Y1 - 4 + oy * 36

    def body(x):
        u1[X1 + x, pl.ds(a0, 4), :] = y0[x, pl.ds(0, 4), :]
        u1[X1 + x, pl.ds(a1, 4), :] = y1[x, pl.ds(0, 4), :]
        if b1 is not None:
            b1[X1 + x, pl.ds(a0, 4), :] = y0[x, pl.ds(4, 4), :]
            b1[X1 + x, pl.ds(a1, 4), :] = y1[x, pl.ds(4, 4), :]

    rows(lo, hi, body)


def set_y2(c2, b2, y0, y1, oy):
    a0 = pl.multiple_of(Y2 - 8 + (1 - oy) * 24, 8)
    a1 = pl.multiple_of(Y2 - 8 + oy * 24, 8)
    for x in range(6):
        b2[X2 - 1 + x, pl.ds(a0, 8), :] = y0[8 + x]
        b2[X2 - 1 + x, pl.ds(a1, 8), :] = y1[8 + x]
    for x in range(8):
        c2[X2 - 2 + x, pl.ds(a0, 8), :] = y0[14 + x]
        c2[X2 - 2 + x, pl.ds(a1, 8), :] = y1[14 + x]


def edge2_kernel(u1_in, c2_in, b2_in, y0, y1, u1, c2, b2, xpack0, xpack1):
    ox, oy = odd("gx"), odd("gy")

    def copy1(x):
        u1[x] = u1_in[x]

    def copy2(x):
        c2[x] = c2_in[x]
        b2[x] = b2_in[x]

    rows(0, 20, copy1)
    rows(0, 16, copy2)
    set_y1(u1, None, y0, y1, oy, 0, 8)
    set_y2(c2, b2, y0, y1, oy)
    for pack, last in ((xpack0, 1 - ox), (xpack1, ox)):
        for k in range(4):
            pack[pl.ds(k * 48, 48), :] = u1[X1 + k + last * 4, pl.ds(8, 48), :]
        for k in range(5):
            pack[pl.ds(192 + k * 32, 32), :] = b2[X2 + k - last, pl.ds(8, 32), :]
        for k in range(6):
            pack[pl.ds(352 + k * 32, 32), :] = c2[X2 + k - 2 * last, pl.ds(8, 32), :]


def one_hot(shape, f):
    i = lax.broadcasted_iota(jnp.int32, shape, 0)
    j = lax.broadcasted_iota(jnp.int32, shape, 1)
    return jnp.where(f(i, j), 1.0, 0.0).astype(F32)


def exact_dot(a, b):
    return jnp.dot(a, b, precision=lax.Precision.HIGHEST, preferred_element_type=F32)


def level2_kernel(
    u1_in, c2_in, b2_in, x0, x1,
    u1, c2, b2, u2, gather,
    fx, fy, fz, fzm, w, ua, tmp, b3, c3,
):
    ox = odd("gx")
    zero = jnp.zeros((8, NZ), F32)

    def copy1(x):
        u1[x] = u1_in[x]

    def copy2(x):
        c2[x] = c2_in[x]
        b2[x] = b2_in[x]
        u2[x] = jnp.zeros((48, NZ), F32)
        fy[x, pl.ds(0, 8), :] = zero

    rows(0, 20, copy1)
    rows(0, 16, copy2)
    for pack, up in ((x0, 1 - ox), (x1, ox)):
        for k in range(4):
            u1[X1 - 4 + k + up * 12, pl.ds(8, 48), :] = pack[pl.ds(k * 48, 48), :]
        for k in range(5):
            b2[X2 - 5 + k + up * 9, pl.ds(8, 32), :] = pack[pl.ds(192 + k * 32, 32), :]
        for k in range(6):
            c2[X2 - 6 + k + up * 10, pl.ds(8, 32), :] = pack[pl.ds(352 + k * 32, 32), :]

    low = Level(2, c2, b2, fx, fy, fz, fzm, w, 8, 40, 32)
    low.faces(0, 15)
    low.weights(1, 15, ua)
    low.sweep(ua, u2, 2, 14)
    tmp[pl.ds(0, 8), :] = zero
    tmp[pl.ds(40, 8), :] = zero
    low.restrict(u2, tmp, b3, 2, X2, 0, None)
    low.restrict_c(tmp, c3, 2, X2, 0)
    both = jnp.concatenate(
        [b3[0, pl.ds(16, 8), :], b3[1, pl.ds(16, 8), :], c3[0, pl.ds(16, 8), :], c3[1, pl.ds(16, 8), :]], 0
    )
    spread = exact_dot(both, one_hot((NZ, NZ), lambda i, j: i == 8 * (j % 16)))
    shape = (8, NZ)
    mine = lane(shape) // 16 == lax.broadcasted_iota(jnp.int32, shape, 0)
    packed = [
        jnp.sum(jnp.where(mine, spread[8 * k : 8 * k + 8], 0.0), axis=0, keepdims=True) for k in range(4)
    ]
    eight = jnp.concatenate(packed + packed, 0)

    def body(k):
        gather[pl.ds(pl.multiple_of(8 * k, 8), 8), :] = eight

    rows(0, 64, body, 8)


class Whole:
    def __init__(self, depth, b, c):
        self.h = H0 * 4.0**depth
        self.s = 2 ** (depth - 3)
        self.st = 16 * self.s
        self.b = b
        n = c.shape[0]
        sub = lax.broadcasted_iota(jnp.int32, (1,) + c.shape[1:], 2)
        up = self.xp(c)
        end = jnp.where(sub == 7, 0.0, up[n - 1 :])
        up = jnp.concatenate([up[: n - 1], end], 0) if n > 1 else end
        self.fxp = harmonic(c, up)
        up = self.yp(c)
        last = up[:, 3:]
        last = jnp.where(lane(last.shape) >= 128 - self.st, 0.0, last)
        self.fyp = harmonic(c, jnp.concatenate([up[:, :3], last], 1))
        self.fzp = harmonic(c, self.zp(c))
        self.fxm, self.fym, self.fzm = self.xm(self.fxp), self.ym(self.fyp), self.zm(self.fzp)
        d = self.h + self.fxp + self.fxm + self.fyp + self.fym + self.fzp + self.fzm
        self.w = DAMP * recip(d)

    def xp(self, v):
        wrap = pltpu.roll(v[:1], 7, 2)
        return jnp.concatenate([v[1:], wrap], 0) if v.shape[0] > 1 else wrap

    def xm(self, v):
        n = v.shape[0]
        wrap = pltpu.roll(v[n - 1 :], 1, 2)
        return jnp.concatenate([wrap, v[: n - 1]], 0) if n > 1 else wrap

    def yp(self, v):
        w = v if self.st == 128 else lroll(v, -self.st)
        far = jnp.concatenate([w[:, 1:], w[:, :1]], 1)
        return far if self.st == 128 else jnp.where(lane(v.shape) < 128 - self.st, w, far)

    def ym(self, v):
        w = v if self.st == 128 else lroll(v, self.st)
        far = jnp.concatenate([w[:, 3:], w[:, :3]], 1)
        return far if self.st == 128 else jnp.where(lane(v.shape) >= self.st, w, far)

    def zp(self, v):
        s = self.s
        return jnp.where(lane(v.shape) % 16 < 16 - s, lroll(v, -s), lroll(v, 16 - s))

    def zm(self, v):
        s = self.s
        return self.zp(v) if s == 8 else jnp.where(lane(v.shape) % 16 >= s, lroll(v, s), lroll(v, s - 16))

    def flux(self, v):
        acc = self.fxp * self.xp(v) + self.fxm * self.xm(v)
        acc = acc + self.fyp * self.yp(v) + self.fym * self.ym(v)
        return acc + self.fzp * self.zp(v) + self.fzm * self.zm(v)

    def sweep(self, v):
        return KEEP * v + self.w * (self.b + self.flux(v))

    def residual(self, v):
        r = self.b - self.h * v
        r = r + self.fxp * (self.xp(v) - v) + self.fxm * (self.xm(v) - v)
        r = r + self.fyp * (self.yp(v) - v) + self.fym * (self.ym(v) - v)
        return r + self.fzp * (self.zp(v) - v) + self.fzm * (self.zm(v) - v)

    def coarse(self, v, scale):
        v = jnp.concatenate([v[2 * k : 2 * k + 1] + v[2 * k + 1 : 2 * k + 2] for k in range(v.shape[0] // 2)], 0)
        return scale * pair_lanes(pair_lanes(v, self.s), self.st)


def whole_cycle(depth, b, c):
    level = Whole(depth, b, c)
    v = level.w * b
    if depth == 6:
        for _ in range(SWEEPS_COARSE - 1):
            v = level.sweep(v)
        return v
    v = level.sweep(v)
    below = whole_cycle(depth + 1, level.coarse(level.residual(v), 0.5), level.coarse(c, 0.125))
    v = v + jnp.concatenate([below[k // 2 : k // 2 + 1] for k in range(v.shape[0])], 0)
    return level.sweep(level.sweep(v))


def up_kernel(
    gather, c2, b2, u2, c1, b1, u1_in, y0, y1, c0, b0, u0,
    out, res,
    s3, e2, e1, e0, hx, hy, hz, hzm, hw, ha, hb,
    gx_, gy_, gz_, gzm_, gw_, ga_, gb_, gr_,
    fx, fy, fz, fzm, w, ua, ub,
):
    ix, iy = lax.axis_index("gx"), lax.axis_index("gy")
    oy = iy % 2
    zero = jnp.zeros((8, NZ), F32)

    def field(k):
        return jnp.stack(
            [
                jnp.stack([gather[pl.ds(xq * 16 + g * 4 + k + xl, 8, stride=64), :] for g in range(4)], 0)
                for xq in range(4)
                for xl in range(2)
            ],
            0,
        )

    u3 = whole_cycle(3, field(0), field(2))
    s3[...] = jnp.zeros(s3.shape, F32)
    for xlo in range(8):
        for g in range(4):
            s3[g + 1, pl.ds(8 + xlo, 8, stride=8), :] = u3[xlo, g]
    shape = (8, NZ)
    mine = lane(shape) // 16 == lax.broadcasted_iota(jnp.int32, shape, 0)
    tiles = []
    for k in range(6):
        for g in range(3):
            row = s3[iy + g, pl.ds(2 * ix + 6 + k, 1), :]
            tiles.append(jnp.where(mine, jnp.broadcast_to(row, shape), 0.0))
    spread = exact_dot(jnp.concatenate(tiles, 0), one_hot((NZ, NZ), lambda i, j: i % 16 == j // 8))
    for k in range(6):
        t = spread[24 * k : 24 * k + 24]
        e2[k, pl.ds(0, 24, stride=2), :] = t
        e2[k, pl.ds(1, 24, stride=2), :] = t

    for x in range(16):
        hy[x, pl.ds(0, 8), :] = zero
        ha[x] = u2[x] + e2[(x - 2) // 2] if 2 <= x < 14 else jnp.zeros((48, NZ), F32)
    low = Level(2, c2, b2, hx, hy, hz, hzm, hw, 8, 40, 32)
    low.faces(0, 15)
    low.weights(1, 15)
    low.sweep(ha, hb, 3, 13)
    low.sweep(hb, ha, 4, 12)

    def grow1(k):
        t = ha[4 + k, pl.ds(8, 32), :]
        e1[k, pl.ds(0, 32, stride=2), :] = t
        e1[k, pl.ds(1, 32, stride=2), :] = t

    rows(0, 8, grow1)

    def copy1(x):
        ga_[x] = u1_in[x]
        gr_[x] = b1[x]
        gy_[x, pl.ds(0, 8), :] = zero

    rows(0, 20, copy1)
    set_y1(ga_, gr_, y0, y1, oy, 0, 8)

    def add1(x):
        ga_[x] = ga_[x] + e1[(x - 2) // 2]

    rows(2, 18, add1)
    mid = Level(1, c1, gr_, gx_, gy_, gz_, gzm_, gw_, 8, 56, 48)
    mid.faces(1, 19)
    mid.weights(2, 18)
    mid.sweep(ga_, gb_, 3, 17)
    mid.sweep(gb_, ga_, 4, 16)

    def grow0(k):
        t = ga_[4 + k, pl.ds(8, 48), :]
        e0[pl.ds(0, 48, stride=2), :] = t
        e0[pl.ds(1, 48, stride=2), :] = t
        for j in range(2):
            ua[2 * k + j] = u0[2 * k + j] + e0[...]

    rows(0, 12, grow0)

    def clear0(x):
        fy[x, pl.ds(0, 8), :] = zero

    rows(0, 24, clear0)
    top = Level(0, c0, b0, fx, fy, fz, fzm, w, 8, 88, 40)
    top.faces(1, 23)
    top.weights(2, 22)
    top.sweep(ua, ub, 2, 22)
    top.sweep(ub, ua, 3, 21)

    def finish(x):
        out[x] = ua[4 + x, pl.ds(Y0, NY), :]
        res[x, pl.ds(0, 32), :] = top.residual(ua, 4 + x, Y0, 32)
        res[x, pl.ds(32, 32), :] = top.residual(ua, 4 + x, Y0 + 32, 32)

    rows(0, NX, finish)


def swaps(axis, first, second):
    count = lax.axis_size(axis)

    def pairs(start):
        return [p for i in range(start, count - 1, 2) for p in ((i, i + 1), (i + 1, i))]

    late = lax.ppermute(second, axis, pairs(1))
    return lax.ppermute(first, axis, pairs(0)), late


def per_device(source, density, drag, porous_rows):
    porous = jnp.broadcast_to(porous_rows.astype(F32)[:, None], (NY, NZ))
    cond, p0, p1 = call(
        begin_kernel, [(NX, NY, NZ), (32, 8, NZ), (32, 8, NZ)], [], (source, density, drag, porous), "begin", 32
    )
    y0, y1 = swaps("gy", p0, p1)
    p0, p1 = call(edge_kernel, [(21, 80, NZ)] * 2, [], (cond, source, y0, y1), "edges", 32)
    x0, x1 = swaps("gx", p0, p1)
    one, two = (20, 64, NZ), (16, 48, NZ)
    keep = (24, 96, NZ)
    c0, b0, u0, c1, b1, u1, c2, b2, p0, p1 = call(
        down_kernel,
        [keep] * 3 + [one] * 3 + [two] * 2 + [(22, 8, NZ)] * 2,
        [(40, 96, NZ)] * 9 + [(96, NZ)] + [one] * 6 + [(64, NZ)],
        (cond, source, y0, y1, x0, x1),
        "down",
        56,
    )
    y0, y1 = swaps("gy", p0, p1)
    u1, c2, b2, p0, p1 = call(
        edge2_kernel, [one, two, two] + [(544, NZ)] * 2, [], (u1, c2, b2, y0, y1), "edges2", 32
    )
    x0, x1 = swaps("gx", p0, p1)
    u1, c2, b2, u2, packed = call(
        level2_kernel,
        [one, two, two, two, (512, NZ)],
        [two] * 6 + [(48, NZ)] + [(2, 48, NZ)] * 2,
        (u1, c2, b2, x0, x1),
        "level2",
        32,
    )
    whole = lax.all_to_all(packed, ("gx", "gy"), 0, 0, tiled=True)
    out, res = call(
        up_kernel,
        [(NX, NY, NZ)] * 2,
        [(6, 80, NZ), (6, 48, NZ), (8, 64, NZ), (96, NZ)] + [two] * 7 + [one] * 8 + [keep] * 7,
        (whole, c2, b2, u2, c1, b1, u1, y0, y1, c0, b0, u0),
        "up",
        56,
    )
    return out, res


def solution(mesh):
    return jax.shard_map(
        per_device,
        mesh=mesh,
        in_specs=(P("gx", "gy", None), P("gx", "gy", None), P("gx", "gy", None), P("gy")),
        out_specs=(P("gx", "gy", None), P("gx", "gy", None)),
        check_vma=False,
    )
```

```python
import functools

import jax
import jax.numpy as jnp
from jax import lax
from jax.experimental import pallas as pl
from jax.experimental.pallas import tpu as pltpu
from jax.sharding import PartitionSpec as P

SWEEPS_COARSE = 16
DAMP = 0.8
KEEP = 1.0 - DAMP
H0 = 0.0002

NX, NY, NZ = 16, 64, 128
F32 = jnp.float32
VMEM = pl.BlockSpec(memory_space=pltpu.VMEM)
HBM = pl.BlockSpec(memory_space=pltpu.HBM)


def call(body, outs, scratch, args, name, vmem, hbm=0):
    args = [pltpu.with_memory_space_constraint(a, pltpu.HBM) for a in args[:hbm]] + list(args[hbm:])
    return pl.pallas_call(
        body,
        out_shape=[jax.ShapeDtypeStruct(s, F32) for s in outs],
        in_specs=[HBM] * hbm + [VMEM] * (len(args) - hbm),
        out_specs=[VMEM] * len(outs),
        scratch_shapes=[pltpu.VMEM(s, F32) if isinstance(s, tuple) else s for s in scratch],
        compiler_params=pltpu.CompilerParams(vmem_limit_bytes=vmem * 2**20),
        name=name,
    )(*args)


def recip(t):
    return 1.0 / t


def harmonic(a, b):
    return (2.0 * a) * b / jnp.maximum(a + b, 1e-30)


def lane(shape):
    return lax.broadcasted_iota(jnp.int32, shape, len(shape) - 1)


def lroll(v, shift):
    return pltpu.roll(v, shift % 128, v.ndim - 1)


def pair_lanes(v, s):
    first = (lane(v.shape) // s) % 2 == 0
    return v + jnp.where(first, lroll(v, -s), lroll(v, s))


def pack_lanes(tiles):
    n = len(tiles)
    out = tiles[0]
    for k in range(1, n):
        out = jnp.where(lane(out.shape) % n == k, tiles[k], out)
    return out


def unpack_lanes(p, n):
    at = lane(p.shape) % n
    moved = {d: p if d == 0 else lroll(p, -d) for d in range(1 - n, n)}
    tiles = []
    for k in range(n):
        out = moved[k]
        for m in range(1, n):
            out = jnp.where(at == m, moved[k - m], out)
        tiles.append(out)
    return tiles


def rows(lo, hi, body, unroll=8):
    whole = (hi - lo) // unroll

    def step(k, carry):
        for j in range(unroll):
            body(lo + k * unroll + j)
        return carry

    if whole > 1:
        lax.fori_loop(0, whole, step, 0)
        lo = lo + whole * unroll
    for x in range(lo, hi):
        body(x)


def chunks(ys, ye, size):
    return [(y, min(size, ye - y)) for y in range(ys, ye, size)]


class Level:
    def __init__(self, depth, c, b, fx, fy, fz, fzm, w, ys, ye, size):
        self.h = H0 * 4.0**depth
        self.s = 2**depth
        self.c, self.b, self.fx, self.fy, self.fz, self.fzm, self.w = c, b, fx, fy, fz, fzm, w
        self.parts = chunks(ys, ye, size)

    def faces(self, lo, hi):
        def body(x):
            for y, n in self.parts:
                c = self.c[x, pl.ds(y, n), :]
                self.fx[x, pl.ds(y, n), :] = harmonic(c, self.c[x + 1, pl.ds(y, n), :])
                self.fy[x, pl.ds(y, n), :] = harmonic(c, self.c[x, pl.ds(y + 1, n), :])
                fz = harmonic(c, lroll(c, -self.s))
                self.fz[x, pl.ds(y, n), :] = fz
                self.fzm[x, pl.ds(y, n), :] = lroll(fz, self.s)

        rows(lo, hi, body)

    def weights(self, lo, hi, start=None):
        def body(x):
            for y, n in self.parts:
                here = pl.ds(y, n)
                d = self.fx[x, here, :] + self.fx[x - 1, here, :]
                d = d + self.fy[x, here, :] + self.fy[x, pl.ds(y - 1, n), :]
                d = d + self.fz[x, here, :] + self.fzm[x, here, :]
                w = DAMP * recip(self.h + d)
                self.w[x, here, :] = w
                if start is not None:
                    start[x, here, :] = w * self.b[x, here, :]

        rows(lo, hi, body)

    def flux(self, u, x, y, n):
        here = pl.ds(y, n)
        v = u[x, here, :]
        acc = self.fx[x, here, :] * u[x + 1, here, :]
        acc = acc + self.fx[x - 1, here, :] * u[x - 1, here, :]
        acc = acc + self.fy[x, here, :] * u[x, pl.ds(y + 1, n), :]
        acc = acc + self.fy[x, pl.ds(y - 1, n), :] * u[x, pl.ds(y - 1, n), :]
        acc = acc + self.fz[x, here, :] * lroll(v, -self.s)
        acc = acc + self.fzm[x, here, :] * lroll(v, self.s)
        return v, acc

    def sweep(self, u, out, lo, hi):
        def body(x):
            for y, n in self.parts:
                here = pl.ds(y, n)
                v, acc = self.flux(u, x, y, n)
                out[x, here, :] = KEEP * v + self.w[x, here, :] * (self.b[x, here, :] + acc)

        rows(lo, hi, body)

    def residual(self, u, x, y, n):
        here = pl.ds(y, n)
        v = u[x, here, :]
        r = self.b[x, here, :] - self.h * v
        r = r + self.fx[x, here, :] * (u[x + 1, here, :] - v)
        r = r + self.fx[x - 1, here, :] * (u[x - 1, here, :] - v)
        r = r + self.fy[x, here, :] * (u[x, pl.ds(y + 1, n), :] - v)
        r = r + self.fy[x, pl.ds(y - 1, n), :] * (u[x, pl.ds(y - 1, n), :] - v)
        r = r + self.fz[x, here, :] * (lroll(v, -self.s) - v)
        return r + self.fzm[x, here, :] * (lroll(v, self.s) - v)

    def halve(self, tmp, out, count, x_to, scale):
        half = tmp.shape[1] // 2

        def body(k):
            t = tmp[k, pl.ds(0, half, stride=2), :] + tmp[k, pl.ds(1, half, stride=2), :]
            out[x_to + k, pl.ds(8, half), :] = scale * pair_lanes(t, self.s)

        rows(0, count, body)

    def restrict(self, u, tmp, out, count, x_from, x_to):
        def body(k):
            x = x_from + 2 * k
            for y, n in self.parts:
                tmp[k, pl.ds(y, n), :] = self.residual(u, x, y, n) + self.residual(u, x + 1, y, n)

        rows(0, count, body, 4)
        self.halve(tmp, out, count, x_to, 0.5)

    def restrict_c(self, tmp, out, count, x_from, x_to):
        def body(k):
            x = x_from + 2 * k
            tmp[k] = self.c[x] + self.c[x + 1]

        rows(0, count, body)
        self.halve(tmp, out, count, x_to, 0.125)


def odd(axis):
    return lax.axis_index(axis) % 2


PARTS = 4


def begin_kernel(source, density, drag, porous, cond, rhs, ypack0, ypack1, dens, dra, por, sem, esem):
    o = odd("gy")
    at0 = pl.multiple_of((1 - o) * (NY - 8), 8)
    at1 = pl.multiple_of(o * (NY - 8), 8)
    part = NX // PARTS
    loads = []
    first = pltpu.make_async_copy(porous, por, esem.at[3])
    first.start()
    for k in range(PARTS):
        here = pl.ds(k * part, part)
        for j, (src, dst) in enumerate(((density, dens), (drag, dra))):
            loads.append(pltpu.make_async_copy(src.at[here], dst.at[here], sem.at[j, k]))
            loads[-1].start()
    edges = []
    for j, (at, pack) in enumerate(((at0, ypack0), (at1, ypack1))):
        edges.append(pltpu.make_async_copy(source.at[:, pl.ds(at, 8), :], pack.at[pl.ds(NX, NX)], esem.at[j]))
        edges[-1].start()
    edges.append(pltpu.make_async_copy(source, rhs, esem.at[2]))
    edges[-1].start()
    first.wait()
    shape = (NY, NZ)
    line = jnp.broadcast_to(por[...].astype(F32)[None], (NY, NY))
    same = lax.broadcasted_iota(jnp.int32, (NY, NY), 0) == lax.broadcasted_iota(jnp.int32, (NY, NY), 1)
    mask = jnp.broadcast_to(jnp.sum(jnp.where(same, line, 0.0), axis=1, keepdims=True), shape)
    for k in range(PARTS):
        loads[2 * k].wait()
        loads[2 * k + 1].wait()
        for x in range(k * part, k * part + part):
            cond[x] = recip(dens[x] * (1.0 + dra[x] * mask))
            ypack0[x] = cond[x, pl.ds(at0, 8), :]
            ypack1[x] = cond[x, pl.ds(at1, 8), :]
    for edge in edges:
        edge.wait()


def edge_kernel(cond, source, y0, y1, xpack0, xpack1):
    ox, oy = odd("gx"), odd("gy")
    at0 = pl.multiple_of((1 - oy) * (NY + 8), 8)
    at1 = pl.multiple_of(oy * (NY + 8), 8)

    def put(pack, row, field, x, base):
        pack[row, pl.ds(8, NY), :] = field[x]
        pack[row, pl.ds(at0, 8), :] = y0[base + x]
        pack[row, pl.ds(at1, 8), :] = y1[base + x]

    def body_c(k):
        put(xpack0, k, cond, k + (1 - ox) * (NX - 11), 0)
        put(xpack1, k, cond, k + ox * (NX - 11), 0)

    def body_b(k):
        put(xpack0, 11 + k, source, k + (1 - ox) * (NX - 10), NX)
        put(xpack1, 11 + k, source, k + ox * (NX - 10), NX)

    rows(0, 11, body_c)
    rows(0, 10, body_b)


X0, Y0 = 12, 16
X1, Y1 = 6, 16
X2, Y2 = 6, 16


def down_kernel(
    cond, source, y0, y1, x0, x1,
    fx, fy, fz, fzm, w, b, ub, gx_, gy_, gz_, gzm_, gw_, b1, u1, c2, b2, ypack0, ypack1,
    c, ua, tmp, c1, ga_, tmp1,
):
    ox, oy = odd("gx"), odd("gy")
    at0 = pl.multiple_of(8 + (1 - oy) * (NY + 8), 8)
    at1 = pl.multiple_of(8 + oy * (NY + 8), 8)

    def own(x):
        c[X0 + x, pl.ds(Y0, NY), :] = cond[x]
        c[X0 + x, pl.ds(at0, 8), :] = y0[x]
        c[X0 + x, pl.ds(at1, 8), :] = y1[x]
        b[X0 + x, pl.ds(Y0, NY), :] = source[x]
        b[X0 + x, pl.ds(at0, 8), :] = y0[NX + x]
        b[X0 + x, pl.ds(at1, 8), :] = y1[NX + x]

    rows(0, NX, own)

    def halo_c(k):
        c[k + 1 + (1 - ox) * (11 + NX), pl.ds(8, 80), :] = x0[k]
        c[k + 1 + ox * (11 + NX), pl.ds(8, 80), :] = x1[k]

    def halo_b(k):
        b[k + 2 + (1 - ox) * (10 + NX), pl.ds(8, 80), :] = x0[11 + k]
        b[k + 2 + ox * (10 + NX), pl.ds(8, 80), :] = x1[11 + k]

    rows(0, 11, halo_c)
    rows(0, 10, halo_b)
    zero = jnp.zeros((8, NZ), F32)

    def pads(x):
        c[x, pl.ds(0, 8), :] = zero
        c[x, pl.ds(88, 8), :] = zero
        fy[x, pl.ds(0, 8), :] = zero

    rows(0, 40, pads)

    top = Level(0, c, b, fx, fy, fz, fzm, w, 8, 88, 40)
    top.faces(1, 39)
    top.weights(2, 38, ua)
    top.sweep(ua, ub, 3, 37)

    def clear1(x):
        for ref in (c1, b1, u1):
            ref[x] = jnp.zeros((64, NZ), F32)
        gy_[x, pl.ds(0, 8), :] = zero

    rows(0, 20, clear1)

    def clear2(x):
        for ref in (c2, b2):
            ref[x] = jnp.zeros((48, NZ), F32)

    rows(0, 16, clear2)

    def clear_tmp(x):
        tmp[x, pl.ds(0, 8), :] = zero
        tmp[x, pl.ds(88, 8), :] = zero

    rows(0, 18, clear_tmp)
    for x in range(8):
        tmp1[x, pl.ds(0, 8), :] = zero
        tmp1[x, pl.ds(56, 8), :] = zero
    top.restrict(ub, tmp, b1, 16, 4, 2)
    top.restrict_c(tmp, c1, 18, 2, 1)

    mid = Level(1, c1, b1, gx_, gy_, gz_, gzm_, gw_, 8, 56, 48)
    mid.faces(1, 19)
    mid.weights(2, 18, ga_)
    mid.sweep(ga_, u1, 3, 17)
    mid.restrict(u1, tmp1, b2, 6, 4, 5)
    mid.restrict_c(tmp1, c2, 8, 2, 4)

    e0 = Y1 + (1 - oy) * 28
    e1 = Y1 + oy * 28
    f0 = pl.multiple_of(Y2 + (1 - oy) * 8, 8)
    f1 = pl.multiple_of(Y2 + oy * 8, 8)
    for pack, e, f in ((ypack0, e0, f0), (ypack1, e1, f1)):
        for k in range(4):
            x = X1 + 2 * k
            pack[k, pl.ds(0, 4), :] = pack_lanes([u1[x + j, pl.ds(e, 4), :] for j in range(2)])
            pack[k, pl.ds(4, 4), :] = pack_lanes([b1[x + j, pl.ds(e, 4), :] for j in range(2)])
        for k in range(2):
            pack[4 + k] = pack_lanes([b2[X2 - 1 + 4 * k + j, pl.ds(f, 8), :] for j in range(4)])
            pack[6 + k] = pack_lanes([c2[X2 - 2 + 4 * k + j, pl.ds(f, 8), :] for j in range(4)])


def set_y1(ref, y0, y1, oy, part):
    a0 = Y1 - 4 + (1 - oy) * 36
    a1 = Y1 - 4 + oy * 36
    for y, a in ((y0, a0), (y1, a1)):
        for k in range(4):
            for j, v in enumerate(unpack_lanes(y[k], 2)):
                ref[X1 + 2 * k + j, pl.ds(a, 4), :] = v[4 * part : 4 * part + 4]


def set_y2(c2, b2, y0, y1, oy):
    a0 = pl.multiple_of(Y2 - 8 + (1 - oy) * 24, 8)
    a1 = pl.multiple_of(Y2 - 8 + oy * 24, 8)
    for y, a in ((y0, a0), (y1, a1)):
        for k in range(2):
            for j, v in enumerate(unpack_lanes(y[4 + k], 4)):
                if 4 * k + j < 6:
                    b2[X2 - 1 + 4 * k + j, pl.ds(a, 8), :] = v
            for j, v in enumerate(unpack_lanes(y[6 + k], 4)):
                c2[X2 - 2 + 4 * k + j, pl.ds(a, 8), :] = v


def copy_rows(pairs, lo, hi):
    def body(x):
        for src, dst in pairs:
            dst[x] = src[x]

    rows(lo, hi, body)


def edge2_kernel(u1_in, c2_in, b2_in, y0, y1, xpack0, xpack1, u1, c2, b2):
    ox, oy = odd("gx"), odd("gy")
    copy_rows([(u1_in, u1)], X1, X1 + 8)
    copy_rows([(c2_in, c2), (b2_in, b2)], X2 - 2, X2 + 6)
    set_y1(u1, y0, y1, oy, 0)
    set_y2(c2, b2, y0, y1, oy)
    for pack, last in ((xpack0, 1 - ox), (xpack1, ox)):
        for k in range(2):
            x = X1 + 2 * k + last * 4
            pack[pl.ds(k * 48, 48), :] = pack_lanes([u1[x + j, pl.ds(8, 48), :] for j in range(2)])
        t = [c2[X2 + k - 2 * last, pl.ds(8, 32), :] for k in range(6)]
        t += [b2[X2 + k - last, pl.ds(8, 32), :] for k in range(5)]
        for k in range(3):
            pack[pl.ds(96 + k * 32, 32), :] = pack_lanes((t + t[:1])[4 * k : 4 * k + 4])


def one_hot(shape, f):
    i = lax.broadcasted_iota(jnp.int32, shape, 0)
    j = lax.broadcasted_iota(jnp.int32, shape, 1)
    return jnp.where(f(i, j), 1.0, 0.0).astype(F32)


def exact_dot(a, b):
    return jnp.dot(a, b, precision=lax.Precision.HIGHEST, preferred_element_type=F32)


def level2_kernel(
    u1_in, c2_in, b2_in, y0, y1, x0, x1,
    fx, fy, fz, fzm, w, b2, u2, u1, gather,
    c2, ua, tmp, b3, c3,
):
    ox, oy = odd("gx"), odd("gy")
    zero = jnp.zeros((8, NZ), F32)
    copy_rows([(u1_in, u1)], 0, 20)
    copy_rows([(c2_in, c2), (b2_in, b2)], 0, 16)
    for x in range(16):
        u2[x] = jnp.zeros((48, NZ), F32)
        fy[x, pl.ds(0, 8), :] = zero
    set_y1(u1, y0, y1, oy, 0)
    set_y2(c2, b2, y0, y1, oy)
    for pack, up in ((x0, 1 - ox), (x1, ox)):
        for k in range(2):
            for j, v in enumerate(unpack_lanes(pack[pl.ds(k * 48, 48), :], 2)):
                u1[X1 - 4 + 2 * k + j + up * 12, pl.ds(8, 48), :] = v
        t = []
        for k in range(3):
            t += unpack_lanes(pack[pl.ds(96 + k * 32, 32), :], 4)
        for k in range(6):
            c2[X2 - 6 + k + up * 10, pl.ds(8, 32), :] = t[k]
        for k in range(5):
            b2[X2 - 5 + k + up * 9, pl.ds(8, 32), :] = t[6 + k]

    low = Level(2, c2, b2, fx, fy, fz, fzm, w, 8, 40, 32)
    low.faces(0, 15)
    low.weights(1, 15, ua)
    low.sweep(ua, u2, 2, 14)
    for x in range(2):
        tmp[x, pl.ds(0, 8), :] = zero
        tmp[x, pl.ds(40, 8), :] = zero
    low.restrict(u2, tmp, b3, 2, X2, 0)
    low.restrict_c(tmp, c3, 2, X2, 0)
    both = jnp.concatenate(
        [b3[0, pl.ds(16, 8), :], b3[1, pl.ds(16, 8), :], c3[0, pl.ds(16, 8), :], c3[1, pl.ds(16, 8), :]], 0
    )
    spread = exact_dot(both, one_hot((NZ, NZ), lambda i, j: i == 8 * (j % 16)))
    shape = (8, NZ)
    mine = lane(shape) // 16 == lax.broadcasted_iota(jnp.int32, shape, 0)
    packed = [
        jnp.sum(jnp.where(mine, spread[8 * k : 8 * k + 8], 0.0), axis=0, keepdims=True) for k in range(4)
    ]
    eight = jnp.concatenate(packed + packed, 0)

    def body(k):
        gather[pl.ds(pl.multiple_of(8 * k, 8), 8), :] = eight

    rows(0, 64, body, 8)


class Whole:
    def __init__(self, depth, b, c):
        self.h = H0 * 4.0**depth
        self.s = 2 ** (depth - 3)
        self.st = 16 * self.s
        self.b = b
        n = c.shape[0]
        sub = lax.broadcasted_iota(jnp.int32, (1,) + c.shape[1:], 2)
        up = self.xp(c)
        end = jnp.where(sub == 7, 0.0, up[n - 1 :])
        up = jnp.concatenate([up[: n - 1], end], 0) if n > 1 else end
        self.fxp = harmonic(c, up)
        up = self.yp(c)
        last = up[:, 3:]
        last = jnp.where(lane(last.shape) >= 128 - self.st, 0.0, last)
        self.fyp = harmonic(c, jnp.concatenate([up[:, :3], last], 1))
        self.fzp = harmonic(c, self.zp(c))
        self.fxm, self.fym, self.fzm = self.xm(self.fxp), self.ym(self.fyp), self.zm(self.fzp)
        d = self.h + self.fxp + self.fxm + self.fyp + self.fym + self.fzp + self.fzm
        self.w = DAMP * recip(d)

    def xp(self, v):
        wrap = pltpu.roll(v[:1], 7, 2)
        return jnp.concatenate([v[1:], wrap], 0) if v.shape[0] > 1 else wrap

    def xm(self, v):
        n = v.shape[0]
        wrap = pltpu.roll(v[n - 1 :], 1, 2)
        return jnp.concatenate([wrap, v[: n - 1]], 0) if n > 1 else wrap

    def yp(self, v):
        w = v if self.st == 128 else lroll(v, -self.st)
        far = jnp.concatenate([w[:, 1:], w[:, :1]], 1)
        return far if self.st == 128 else jnp.where(lane(v.shape) < 128 - self.st, w, far)

    def ym(self, v):
        w = v if self.st == 128 else lroll(v, self.st)
        far = jnp.concatenate([w[:, 3:], w[:, :3]], 1)
        return far if self.st == 128 else jnp.where(lane(v.shape) >= self.st, w, far)

    def zp(self, v):
        s = self.s
        return jnp.where(lane(v.shape) % 16 < 16 - s, lroll(v, -s), lroll(v, 16 - s))

    def zm(self, v):
        s = self.s
        return self.zp(v) if s == 8 else jnp.where(lane(v.shape) % 16 >= s, lroll(v, s), lroll(v, s - 16))

    def flux(self, v):
        acc = self.fxp * self.xp(v) + self.fxm * self.xm(v)
        acc = acc + self.fyp * self.yp(v) + self.fym * self.ym(v)
        return acc + self.fzp * self.zp(v) + self.fzm * self.zm(v)

    def sweep(self, v):
        return KEEP * v + self.w * (self.b + self.flux(v))

    def residual(self, v):
        r = self.b - self.h * v
        r = r + self.fxp * (self.xp(v) - v) + self.fxm * (self.xm(v) - v)
        r = r + self.fyp * (self.yp(v) - v) + self.fym * (self.ym(v) - v)
        return r + self.fzp * (self.zp(v) - v) + self.fzm * (self.zm(v) - v)

    def coarse(self, v, scale):
        v = jnp.concatenate([v[2 * k : 2 * k + 1] + v[2 * k + 1 : 2 * k + 2] for k in range(v.shape[0] // 2)], 0)
        return scale * pair_lanes(pair_lanes(v, self.s), self.st)


def whole_cycle(depth, b, c):
    level = Whole(depth, b, c)
    v = level.w * b
    if depth == 6:
        for _ in range(SWEEPS_COARSE - 1):
            v = level.sweep(v)
        return v
    v = level.sweep(v)
    below = whole_cycle(depth + 1, level.coarse(level.residual(v), 0.5), level.coarse(c, 0.125))
    v = v + jnp.concatenate([below[k // 2 : k // 2 + 1] for k in range(v.shape[0])], 0)
    return level.sweep(level.sweep(v))


def up_kernel(
    gather, y0, y1,
    hx, hy, hz, hzm, hw, b2, u2,
    gx_, gy_, gz_, gzm_, gw_, b1_in, u1,
    fx, fy, fz, fzm, w, b, u0,
    out, res,
    s3, e2, e1, e0, ha, hb, b1, ga_, gb_, ua, ub,
):
    ix, iy = lax.axis_index("gx"), lax.axis_index("gy")
    oy = iy % 2
    zero = jnp.zeros((8, NZ), F32)

    def field(k):
        return jnp.stack(
            [
                jnp.stack([gather[pl.ds(xq * 16 + g * 4 + k + xl, 8, stride=64), :] for g in range(4)], 0)
                for xq in range(4)
                for xl in range(2)
            ],
            0,
        )

    u3 = whole_cycle(3, field(0), field(2))
    s3[...] = jnp.zeros(s3.shape, F32)
    for xlo in range(8):
        for g in range(4):
            s3[g + 1, pl.ds(8 + xlo, 8, stride=8), :] = u3[xlo, g]
    shape = (8, NZ)
    mine = lane(shape) // 16 == lax.broadcasted_iota(jnp.int32, shape, 0)
    tiles = []
    for k in range(6):
        for g in range(3):
            row = s3[iy + g, pl.ds(2 * ix + 6 + k, 1), :]
            tiles.append(jnp.where(mine, jnp.broadcast_to(row, shape), 0.0))
    spread = exact_dot(jnp.concatenate(tiles, 0), one_hot((NZ, NZ), lambda i, j: i % 16 == j // 8))
    for k in range(6):
        t = spread[24 * k : 24 * k + 24]
        e2[k, pl.ds(0, 24, stride=2), :] = t
        e2[k, pl.ds(1, 24, stride=2), :] = t

    for x in range(16):
        ha[x] = u2[x] + e2[(x - 2) // 2] if 2 <= x < 14 else jnp.zeros((48, NZ), F32)
    low = Level(2, None, b2, hx, hy, hz, hzm, hw, 8, 40, 32)
    low.sweep(ha, hb, 3, 13)
    low.sweep(hb, ha, 4, 12)

    def grow1(k):
        t = ha[4 + k, pl.ds(8, 32), :]
        e1[k, pl.ds(0, 32, stride=2), :] = t
        e1[k, pl.ds(1, 32, stride=2), :] = t

    rows(0, 8, grow1)

    copy_rows([(b1_in, b1)], 2, 18)
    set_y1(b1, y0, y1, oy, 1)

    def add1(k):
        for j in range(2):
            ga_[2 + 2 * k + j] = u1[2 + 2 * k + j] + e1[k]

    rows(0, 8, add1)
    mid = Level(1, None, b1, gx_, gy_, gz_, gzm_, gw_, 8, 56, 48)
    mid.sweep(ga_, gb_, 3, 17)
    mid.sweep(gb_, ga_, 4, 16)

    def grow0(k):
        t = ga_[4 + k, pl.ds(8, 48), :]
        e0[k, pl.ds(0, 48, stride=2), :] = t
        e0[k, pl.ds(1, 48, stride=2), :] = t

    def add0(k):
        for j in range(2):
            ua[8 + 2 * k + j] = u0[8 + 2 * k + j] + e0[k]

    rows(0, 12, grow0, 4)
    rows(0, 12, add0, 4)
    top = Level(0, None, b, fx, fy, fz, fzm, w, 8, 88, 40)
    top.sweep(ua, ub, 10, 30)
    top.sweep(ub, ua, 11, 29)

    def finish(x):
        out[x] = ua[X0 + x, pl.ds(Y0, NY), :]
        res[x] = top.residual(ua, X0 + x, Y0, NY)

    rows(0, NX, finish)


def swaps(axis, first, second):
    count = lax.axis_size(axis)

    def pairs(start):
        return [p for i in range(start, count - 1, 2) for p in ((i, i + 1), (i + 1, i))]

    late = lax.ppermute(second, axis, pairs(1))
    return lax.ppermute(first, axis, pairs(0)), late


def per_device(source, density, drag, porous_rows):
    sems = [pltpu.SemaphoreType.DMA((2, PARTS)), pltpu.SemaphoreType.DMA((4,))]
    block = (NX, NY, NZ)
    cond, source, p0, p1 = call(
        begin_kernel,
        [block, block, (32, 8, NZ), (32, 8, NZ)],
        [block, block, pltpu.VMEM((NY,), jnp.int32)] + sems,
        (source, density, drag, porous_rows),
        "begin",
        16,
        4,
    )
    y0, y1 = swaps("gy", p0, p1)
    p0, p1 = call(edge_kernel, [(21, 80, NZ)] * 2, [], (cond, source, y0, y1), "edges", 16)
    x0, x1 = swaps("gx", p0, p1)
    zero, one, two = (40, 96, NZ), (20, 64, NZ), (16, 48, NZ)
    down = call(
        down_kernel,
        [zero] * 7 + [one] * 7 + [two] * 2 + [(8, 8, NZ)] * 2,
        [zero] * 2 + [(18, 96, NZ)] + [one] * 2 + [(8, 64, NZ)],
        (cond, source, y0, y1, x0, x1),
        "down",
        36,
    )
    level0, level1 = down[:7], down[7:14]
    u1, c2, b2, p0, p1 = down[13:]
    y0, y1 = swaps("gy", p0, p1)
    p0, p1 = call(edge2_kernel, [(192, NZ)] * 2, [one, two, two], (u1, c2, b2, y0, y1), "edges2", 16)
    x0, x1 = swaps("gx", p0, p1)
    *level2, u1, packed = call(
        level2_kernel,
        [two] * 7 + [one, (512, NZ)],
        [two] * 2 + [(2, 48, NZ)] * 3,
        (u1, c2, b2, y0, y1, x0, x1),
        "level2",
        16,
    )
    whole = lax.all_to_all(packed, ("gx", "gy"), 0, 0, tiled=True)
    out, res = call(
        up_kernel,
        [block] * 2,
        [(6, 80, NZ), (6, 48, NZ), (8, 64, NZ), (12, 96, NZ)] + [two] * 2 + [one] * 3 + [zero] * 2,
        (whole, y0, y1, *level2, *level1[:6], u1, *level0),
        "up",
        36,
    )
    return out, res


def solution(mesh):
    return jax.shard_map(
        per_device,
        mesh=mesh,
        in_specs=(P("gx", "gy", None), P("gx", "gy", None), P("gx", "gy", None), P("gy")),
        out_specs=(P("gx", "gy", None), P("gx", "gy", None)),
        check_vma=False,
    )
```

```python
import functools

import jax
import jax.numpy as jnp
from jax import lax
from jax.experimental import pallas as pl
from jax.experimental.pallas import tpu as pltpu
from jax.sharding import PartitionSpec as P

SWEEPS_COARSE = 16
DAMP = 0.8
KEEP = 1.0 - DAMP
H0 = 0.0002

NX, NY, NZ = 16, 64, 128
F32 = jnp.float32
VMEM = pl.BlockSpec(memory_space=pltpu.VMEM)
HBM = pl.BlockSpec(memory_space=pltpu.HBM)


def call(body, outs, scratch, args, name, vmem, hbm=0, cost=0):
    args = [pltpu.with_memory_space_constraint(a, pltpu.HBM) for a in args[:hbm]] + list(args[hbm:])
    return pl.pallas_call(
        body,
        out_shape=[jax.ShapeDtypeStruct(s, F32) for s in outs],
        in_specs=[HBM] * hbm + [VMEM] * (len(args) - hbm),
        out_specs=[VMEM] * len(outs),
        scratch_shapes=[pltpu.VMEM(s, F32) if isinstance(s, tuple) else s for s in scratch],
        compiler_params=pltpu.CompilerParams(vmem_limit_bytes=vmem * 2**20),
        name=name,
        cost_estimate=pl.CostEstimate(flops=cost, bytes_accessed=0, transcendentals=0) if cost else None,
    )(*args)


def recip(t):
    return 1.0 / t


def harmonic(a, b):
    return (2.0 * a) * b / jnp.maximum(a + b, 1e-30)


def lane(shape):
    return lax.broadcasted_iota(jnp.int32, shape, len(shape) - 1)


def lroll(v, shift):
    return pltpu.roll(v, shift % 128, v.ndim - 1)


def pair_lanes(v, s):
    first = (lane(v.shape) // s) % 2 == 0
    return v + jnp.where(first, lroll(v, -s), lroll(v, s))


def pack_lanes(tiles):
    n = len(tiles)
    out = tiles[0]
    for k in range(1, n):
        out = jnp.where(lane(out.shape) % n == k, tiles[k], out)
    return out


def unpack_lanes(p, n):
    at = lane(p.shape) % n
    moved = {d: p if d == 0 else lroll(p, -d) for d in range(1 - n, n)}
    tiles = []
    for k in range(n):
        out = moved[k]
        for m in range(1, n):
            out = jnp.where(at == m, moved[k - m], out)
        tiles.append(out)
    return tiles


def rows(lo, hi, body, unroll=8):
    whole = (hi - lo) // unroll

    def step(k, carry):
        for j in range(unroll):
            body(lo + k * unroll + j)
        return carry

    if whole > 1:
        lax.fori_loop(0, whole, step, 0)
        lo = lo + whole * unroll
    for x in range(lo, hi):
        body(x)


class Level:
    def __init__(self, depth, c, b, fx, fy, fz, w, ys, ye):
        self.h = H0 * 4.0**depth
        self.s = 2**depth
        self.c, self.b, self.fx, self.fy, self.fz, self.w = c, b, fx, fy, fz, w
        self.ys, self.n = ys, ye - ys

    def faces(self, lo, hi):
        here, above = pl.ds(self.ys, self.n), pl.ds(self.ys + 1, self.n)

        def body(x):
            c = self.c[x, here, :]
            twice, safe = c + c, c + 1e-30

            def face(other):
                return twice * other / (safe + other)

            self.fx[x, here, :] = face(self.c[x + 1, here, :])
            self.fy[x, here, :] = face(self.c[x, above, :])
            self.fz[x, here, :] = face(lroll(c, -self.s))

        rows(lo, hi, body)

    def weights(self, lo, hi, start=None):
        here, below = pl.ds(self.ys, self.n), pl.ds(self.ys - 1, self.n)

        def body(x):
            fz = self.fz[x, here, :]
            d = self.fx[x, here, :] + self.fx[x - 1, here, :]
            d = d + (self.fy[x, here, :] + self.fy[x, below, :])
            d = d + (fz + lroll(fz, self.s))
            w = DAMP * recip(self.h + d)
            self.w[x, here, :] = w
            if start is not None:
                start[x, here, :] = w * self.b[x, here, :]

        rows(lo, hi, body)

    def start(self, out, lo, hi):
        here = pl.ds(self.ys, self.n)

        def body(x):
            out[x, here, :] = self.w[x, here, :] * self.b[x, here, :]

        rows(lo, hi, body)

    def sweep(self, u, out, lo, hi):
        here = pl.ds(self.ys, self.n)
        above, below = pl.ds(self.ys + 1, self.n), pl.ds(self.ys - 1, self.n)

        def body(x):
            v = u[x, here, :]
            fz = self.fz[x, here, :]
            acc = fz * lroll(v, -self.s) + lroll(fz * v, self.s)
            acc = acc + (self.fx[x, here, :] * u[x + 1, here, :] + self.fx[x - 1, here, :] * u[x - 1, here, :])
            acc = acc + (self.fy[x, here, :] * u[x, above, :] + self.fy[x, below, :] * u[x, below, :])
            out[x, here, :] = KEEP * v + self.w[x, here, :] * (self.b[x, here, :] + acc)

        rows(lo, hi, body)

    def residual(self, u, x, y, n):
        here, above, below = pl.ds(y, n), pl.ds(y + 1, n), pl.ds(y - 1, n)
        v = u[x, here, :]
        flow = self.fz[x, here, :] * (lroll(v, -self.s) - v)
        r = self.b[x, here, :] - self.h * v
        r = r + (flow - lroll(flow, self.s))
        r = r + self.fx[x, here, :] * (u[x + 1, here, :] - v)
        r = r + self.fx[x - 1, here, :] * (u[x - 1, here, :] - v)
        r = r + self.fy[x, here, :] * (u[x, above, :] - v)
        return r + self.fy[x, below, :] * (u[x, below, :] - v)

    def halve(self, tmp, out, lo, hi, x_to, scale):
        half = tmp.shape[1] // 2

        def body(k):
            t = tmp[k, pl.ds(0, half, stride=2), :] + tmp[k, pl.ds(1, half, stride=2), :]
            out[x_to + k, pl.ds(8, half), :] = scale * pair_lanes(t, self.s)

        rows(lo, hi, body)

    def restrict(self, u, tmp, out, lo, hi, x_from, x_to):
        def body(k):
            x = x_from + 2 * k
            both = self.residual(u, x, self.ys, self.n) + self.residual(u, x + 1, self.ys, self.n)
            tmp[k, pl.ds(self.ys, self.n), :] = both

        rows(lo, hi, body, 4)
        self.halve(tmp, out, lo, hi, x_to, 0.5)

    def restrict_c(self, tmp, out, lo, hi, x_from, x_to):
        def body(k):
            x = x_from + 2 * k
            tmp[k] = self.c[x] + self.c[x + 1]

        rows(lo, hi, body)
        self.halve(tmp, out, lo, hi, x_to, 0.125)


def odd(axis):
    return lax.axis_index(axis) % 2


PARTS = 4


def begin_kernel(source, density, drag, porous, cond, rhs, ypack0, ypack1, xpack0, xpack1, dens, dra, por, sem, esem):
    o = odd("gy")
    at0 = pl.multiple_of((1 - o) * (NY - 8), 8)
    at1 = pl.multiple_of(o * (NY - 8), 8)
    part = NX // PARTS
    loads = []
    first = pltpu.make_async_copy(porous, por, esem.at[3])
    first.start()
    for k in range(PARTS):
        here = pl.ds(k * part, part)
        for j, (src, dst) in enumerate(((density, dens), (drag, dra))):
            loads.append(pltpu.make_async_copy(src.at[here], dst.at[here], sem.at[j, k]))
            loads[-1].start()
    edges = []
    for j, (at, pack) in enumerate(((at0, ypack0), (at1, ypack1))):
        edges.append(pltpu.make_async_copy(source.at[:, pl.ds(at, 8), :], pack.at[pl.ds(NX, NX)], esem.at[j]))
        edges[-1].start()
    edges.append(pltpu.make_async_copy(source, rhs, esem.at[2]))
    edges[-1].start()
    ox = odd("gx")
    for j, (last, pack) in enumerate(((1 - ox, xpack0), (ox, xpack1))):
        rhs_rows = source.at[pl.ds(last * (NX - 10), 10)]
        edges.append(pltpu.make_async_copy(rhs_rows, pack.at[pl.ds(11, 10)], esem.at[4 + j]))
        edges[-1].start()
    first.wait()
    shape = (NY, NZ)
    line = jnp.broadcast_to(por[...].astype(F32)[None], (NY, NY))
    same = lax.broadcasted_iota(jnp.int32, (NY, NY), 0) == lax.broadcasted_iota(jnp.int32, (NY, NY), 1)
    mask = jnp.broadcast_to(jnp.sum(jnp.where(same, line, 0.0), axis=1, keepdims=True), shape)
    for k in range(PARTS):
        loads[2 * k].wait()
        loads[2 * k + 1].wait()
        for x in range(k * part, k * part + part):
            cond[x] = recip(dens[x] * (1.0 + dra[x] * mask))
            ypack0[x] = cond[x, pl.ds(at0, 8), :]
            ypack1[x] = cond[x, pl.ds(at1, 8), :]
    for last, pack in ((1 - ox, xpack0), (ox, xpack1)):
        for k in range(11):
            pack[k] = cond[k + last * (NX - 11)]
    for edge in edges:
        edge.wait()


def corner_kernel(y0, y1, xpack0, xpack1):
    ox, oy = odd("gx"), odd("gy")
    at0 = pl.multiple_of((1 - oy) * 8, 8)
    at1 = pl.multiple_of(oy * 8, 8)
    for pack, last in ((xpack0, 1 - ox), (xpack1, ox)):
        for k in range(21):
            x = k + last * (NX - 11) if k < 11 else NX + k - 11 + last * (NX - 10)
            pack[k, pl.ds(at0, 8), :] = y0[x]
            pack[k, pl.ds(at1, 8), :] = y1[x]


X0, Y0 = 12, 16
X1, Y1 = 6, 16
X2, Y2 = 6, 16


def levels_down(c, b, fx, fy, fz, w, c1, b1, gx_, gy_, gz_, gw_):
    top = Level(0, c, b, fx, fy, fz, w, 8, 88)
    return top, Level(1, c1, b1, gx_, gy_, gz_, gw_, 8, 56)


def inner_kernel(cond, source, y0, y1, c, b, fx, fy, fz, w, ua, ub, c1, b1, gx_, gy_, gz_, gw_, tmp):
    oy = odd("gy")
    at0 = pl.multiple_of(8 + (1 - oy) * (NY + 8), 8)
    at1 = pl.multiple_of(8 + oy * (NY + 8), 8)

    def own(x):
        c[1 + x, pl.ds(Y0, NY), :] = cond[x]
        c[1 + x, pl.ds(at0, 8), :] = y0[x]
        c[1 + x, pl.ds(at1, 8), :] = y1[x]
        b[1 + x, pl.ds(Y0, NY), :] = source[x]
        b[1 + x, pl.ds(at0, 8), :] = y0[NX + x]
        b[1 + x, pl.ds(at1, 8), :] = y1[NX + x]

    rows(0, NX, own)
    top, mid = levels_down(c, b, fx, fy, fz, w, c1, b1, gx_, gy_, gz_, gw_)
    top.faces(1, 17)
    top.weights(2, 16, ua)
    top.sweep(ua, ub, 3, 15)
    top.restrict_c(tmp, c1, 0, 8, 1, 1)
    top.restrict(ub, tmp, b1, 2, 6, 1, 1)
    mid.faces(1, 9)
    mid.weights(2, 8)


def down_kernel(
    x0, x1, k0, k1, c_in, b_in, fx_in, fy_in, fz_in, w_in, ua_in, ub_in, c1_in, b1_in, gx_in, gy_in, gz_in, gw_in,
    fx, fy, fz, w, b, ub, gx_, gy_, gz_, gw_, b1, u1, c2, b2, ypack0, ypack1,
    c, ua, c1, ga_, tmp, ctmp, tmp1,
):
    ox, oy = odd("gx"), odd("gy")
    here, here1 = pl.ds(8, 80), pl.ds(8, 48)

    def halo(ref, row, x, k, pack):
        ref[row, pl.ds(Y0, NY), :] = x[k]
        ref[row, pl.ds(8, 8), :] = pack[k, pl.ds(0, 8), :]
        ref[row, pl.ds(88 - 8, 8), :] = pack[k, pl.ds(8, 8), :]

    for x, pack, up in ((x0, k0, 1 - ox), (x1, k1, ox)):
        for k in range(11):
            halo(c, k + 1 + up * (11 + NX), x, k, pack)
        for k in range(10):
            halo(b, k + 2 + up * (10 + NX), x, 11 + k, pack)
    for x in (1, 16):
        c[x + 11, here, :] = c_in[x, here, :]
    for x in (2, 3, 14, 15):
        ua[x + 11, here, :] = ua_in[x, here, :]

    def fill(x):
        for ref, src in ((fx, fx_in), (fy, fy_in), (fz, fz_in), (w, w_in), (b, b_in), (ub, ub_in)):
            ref[x + 11, here, :] = src[x, here, :]

    rows(1, 17, fill)
    for x in range(1, 9):
        c1[x + 5, here1, :] = c1_in[x, here1, :]
        for ref, src in ((gx_, gx_in), (gy_, gy_in), (gz_, gz_in), (gw_, gw_in), (b1, b1_in)):
            ref[x + 5, here1, :] = src[x, here1, :]

    top, mid = levels_down(c, b, fx, fy, fz, w, c1, b1, gx_, gy_, gz_, gw_)
    top.faces(1, 12)
    top.faces(27, 39)
    top.weights(2, 13, ua)
    top.weights(27, 38, ua)
    top.sweep(ua, ub, 3, 14)
    top.sweep(ua, ub, 26, 37)
    top.restrict_c(ctmp, c1, 0, 5, 2, 1)
    top.restrict_c(ctmp, c1, 13, 18, 2, 1)
    top.restrict(ub, tmp, b1, 0, 6, 4, 2)
    top.restrict(ub, tmp, b1, 10, 16, 4, 2)

    mid.faces(1, 6)
    mid.faces(13, 19)
    mid.weights(2, 7)
    mid.weights(13, 18)
    mid.start(ga_, 2, 18)
    mid.sweep(ga_, u1, 3, 17)
    mid.restrict(u1, tmp1, b2, 0, 6, 4, 5)
    mid.restrict_c(tmp1, c2, 0, 8, 2, 4)

    e0 = Y1 + (1 - oy) * 28
    e1 = Y1 + oy * 28
    f0 = pl.multiple_of(Y2 + (1 - oy) * 8, 8)
    f1 = pl.multiple_of(Y2 + oy * 8, 8)
    for pack, e, f in ((ypack0, e0, f0), (ypack1, e1, f1)):
        for k in range(4):
            x = X1 + 2 * k
            pack[k, pl.ds(0, 4), :] = pack_lanes([u1[x + j, pl.ds(e, 4), :] for j in range(2)])
            pack[k, pl.ds(4, 4), :] = pack_lanes([b1[x + j, pl.ds(e, 4), :] for j in range(2)])
        for k in range(2):
            pack[4 + k] = pack_lanes([b2[X2 - 1 + 4 * k + j, pl.ds(f, 8), :] for j in range(4)])
            pack[6 + k] = pack_lanes([c2[X2 - 2 + 4 * k + j, pl.ds(f, 8), :] for j in range(4)])


def set_y1(ref, y0, y1, oy, part):
    a0 = Y1 - 4 + (1 - oy) * 36
    a1 = Y1 - 4 + oy * 36
    for y, a in ((y0, a0), (y1, a1)):
        for k in range(4):
            for j, v in enumerate(unpack_lanes(y[k], 2)):
                ref[X1 + 2 * k + j, pl.ds(a, 4), :] = v[4 * part : 4 * part + 4]


def set_y2(c2, b2, y0, y1, oy):
    a0 = pl.multiple_of(Y2 - 8 + (1 - oy) * 24, 8)
    a1 = pl.multiple_of(Y2 - 8 + oy * 24, 8)
    for y, a in ((y0, a0), (y1, a1)):
        for k in range(2):
            for j, v in enumerate(unpack_lanes(y[4 + k], 4)):
                if 4 * k + j < 6:
                    b2[X2 - 1 + 4 * k + j, pl.ds(a, 8), :] = v
            for j, v in enumerate(unpack_lanes(y[6 + k], 4)):
                c2[X2 - 2 + 4 * k + j, pl.ds(a, 8), :] = v


def copy_rows(pairs, lo, hi):
    def body(x):
        for src, dst in pairs:
            dst[x] = src[x]

    rows(lo, hi, body)


def edge2_kernel(u1_in, c2_in, b2_in, y0, y1, xpack0, xpack1, u1, c2, b2):
    ox, oy = odd("gx"), odd("gy")
    copy_rows([(u1_in, u1)], X1, X1 + 8)
    copy_rows([(c2_in, c2), (b2_in, b2)], X2 - 2, X2 + 6)
    set_y1(u1, y0, y1, oy, 0)
    set_y2(c2, b2, y0, y1, oy)
    for pack, last in ((xpack0, 1 - ox), (xpack1, ox)):
        for k in range(2):
            x = X1 + 2 * k + last * 4
            pack[pl.ds(k * 48, 48), :] = pack_lanes([u1[x + j, pl.ds(8, 48), :] for j in range(2)])
        t = [c2[X2 + k - 2 * last, pl.ds(8, 32), :] for k in range(6)]
        t += [b2[X2 + k - last, pl.ds(8, 32), :] for k in range(5)]
        for k in range(3):
            pack[pl.ds(96 + k * 32, 32), :] = pack_lanes((t + t[:1])[4 * k : 4 * k + 4])


def one_hot(shape, f):
    i = lax.broadcasted_iota(jnp.int32, shape, 0)
    j = lax.broadcasted_iota(jnp.int32, shape, 1)
    return jnp.where(f(i, j), 1.0, 0.0).astype(F32)


def exact_dot(a, b):
    return jnp.dot(a, b, precision=lax.Precision.HIGHEST, preferred_element_type=F32)


def level2_kernel(
    u1_in, c2_in, b2_in, y0, y1, x0, x1,
    fx, fy, fz, w, b2, u2, u1, gather,
    c2, ua, tmp, b3, c3,
):
    ox, oy = odd("gx"), odd("gy")
    copy_rows([(u1_in, u1)], X1, X1 + 8)
    copy_rows([(c2_in, c2), (b2_in, b2)], X2 - 2, X2 + 6)
    set_y1(u1, y0, y1, oy, 0)
    set_y2(c2, b2, y0, y1, oy)
    for pack, up in ((x0, 1 - ox), (x1, ox)):
        for k in range(2):
            for j, v in enumerate(unpack_lanes(pack[pl.ds(k * 48, 48), :], 2)):
                u1[X1 - 4 + 2 * k + j + up * 12, pl.ds(8, 48), :] = v
        t = []
        for k in range(3):
            t += unpack_lanes(pack[pl.ds(96 + k * 32, 32), :], 4)
        for k in range(6):
            c2[X2 - 6 + k + up * 10, pl.ds(8, 32), :] = t[k]
        for k in range(5):
            b2[X2 - 5 + k + up * 9, pl.ds(8, 32), :] = t[6 + k]

    low = Level(2, c2, b2, fx, fy, fz, w, 8, 40)
    low.faces(0, 15)
    low.weights(1, 15, ua)
    low.sweep(ua, u2, 2, 14)
    low.restrict(u2, tmp, b3, 0, 2, X2, 0)
    low.restrict_c(tmp, c3, 0, 2, X2, 0)
    both = jnp.concatenate(
        [b3[0, pl.ds(16, 8), :], b3[1, pl.ds(16, 8), :], c3[0, pl.ds(16, 8), :], c3[1, pl.ds(16, 8), :]], 0
    )
    spread = exact_dot(both, one_hot((NZ, NZ), lambda i, j: i == 8 * (j % 16)))
    shape = (8, NZ)
    mine = lane(shape) // 16 == lax.broadcasted_iota(jnp.int32, shape, 0)
    packed = [
        jnp.sum(jnp.where(mine, spread[8 * k : 8 * k + 8], 0.0), axis=0, keepdims=True) for k in range(4)
    ]
    eight = jnp.concatenate(packed + packed, 0)

    def body(k):
        gather[pl.ds(pl.multiple_of(8 * k, 8), 8), :] = eight

    rows(0, 64, body, 8)


class Whole:
    def __init__(self, depth, b, c):
        self.h = H0 * 4.0**depth
        self.s = 2 ** (depth - 3)
        self.st = 16 * self.s
        self.b = b
        n = c.shape[0]
        sub = lax.broadcasted_iota(jnp.int32, (1,) + c.shape[1:], 2)
        up = self.xp(c)
        end = jnp.where(sub == 7, 0.0, up[n - 1 :])
        up = jnp.concatenate([up[: n - 1], end], 0) if n > 1 else end
        self.fxp = harmonic(c, up)
        up = self.yp(c)
        last = up[:, 3:]
        last = jnp.where(lane(last.shape) >= 128 - self.st, 0.0, last)
        self.fyp = harmonic(c, jnp.concatenate([up[:, :3], last], 1))
        self.fzp = harmonic(c, self.zp(c))
        self.fxm, self.fym, self.fzm = self.xm(self.fxp), self.ym(self.fyp), self.zm(self.fzp)
        d = self.h + self.fxp + self.fxm + self.fyp + self.fym + self.fzp + self.fzm
        self.w = DAMP * recip(d)

    def xp(self, v):
        wrap = pltpu.roll(v[:1], 7, 2)
        return jnp.concatenate([v[1:], wrap], 0) if v.shape[0] > 1 else wrap

    def xm(self, v):
        n = v.shape[0]
        wrap = pltpu.roll(v[n - 1 :], 1, 2)
        return jnp.concatenate([wrap, v[: n - 1]], 0) if n > 1 else wrap

    def yp(self, v):
        w = v if self.st == 128 else lroll(v, -self.st)
        far = jnp.concatenate([w[:, 1:], w[:, :1]], 1)
        return far if self.st == 128 else jnp.where(lane(v.shape) < 128 - self.st, w, far)

    def ym(self, v):
        w = v if self.st == 128 else lroll(v, self.st)
        far = jnp.concatenate([w[:, 3:], w[:, :3]], 1)
        return far if self.st == 128 else jnp.where(lane(v.shape) >= self.st, w, far)

    def zp(self, v):
        s = self.s
        return jnp.where(lane(v.shape) % 16 < 16 - s, lroll(v, -s), lroll(v, 16 - s))

    def zm(self, v):
        s = self.s
        return self.zp(v) if s == 8 else jnp.where(lane(v.shape) % 16 >= s, lroll(v, s), lroll(v, s - 16))

    def flux(self, v):
        acc = self.fxp * self.xp(v) + self.fxm * self.xm(v)
        acc = acc + self.fyp * self.yp(v) + self.fym * self.ym(v)
        return acc + self.fzp * self.zp(v) + self.fzm * self.zm(v)

    def sweep(self, v):
        return KEEP * v + self.w * (self.b + self.flux(v))

    def residual(self, v):
        r = self.b - self.h * v
        r = r + self.fxp * (self.xp(v) - v) + self.fxm * (self.xm(v) - v)
        r = r + self.fyp * (self.yp(v) - v) + self.fym * (self.ym(v) - v)
        return r + self.fzp * (self.zp(v) - v) + self.fzm * (self.zm(v) - v)

    def coarse(self, v, scale):
        v = jnp.concatenate([v[2 * k : 2 * k + 1] + v[2 * k + 1 : 2 * k + 2] for k in range(v.shape[0] // 2)], 0)
        return scale * pair_lanes(pair_lanes(v, self.s), self.st)


def whole_cycle(depth, b, c):
    level = Whole(depth, b, c)
    v = level.w * b
    if depth == 6:
        for _ in range(SWEEPS_COARSE - 1):
            v = level.sweep(v)
        return v
    v = level.sweep(v)
    below = whole_cycle(depth + 1, level.coarse(level.residual(v), 0.5), level.coarse(c, 0.125))
    v = v + jnp.concatenate([below[k // 2 : k // 2 + 1] for k in range(v.shape[0])], 0)
    return level.sweep(level.sweep(v))


def up_kernel(
    gather, y0, y1,
    hx, hy, hz, hw, b2, u2,
    gx_, gy_, gz_, gw_, b1_in, u1,
    fx, fy, fz, w, b, u0,
    out, res,
    s3, e2, e1, e0, ha, hb, b1, ga_, gb_, ua, ub,
):
    ix, iy = lax.axis_index("gx"), lax.axis_index("gy")
    oy = iy % 2

    def field(k):
        return jnp.stack(
            [
                jnp.stack([gather[pl.ds(xq * 16 + g * 4 + k + xl, 8, stride=64), :] for g in range(4)], 0)
                for xq in range(4)
                for xl in range(2)
            ],
            0,
        )

    u3 = whole_cycle(3, field(0), field(2))
    s3[...] = jnp.zeros(s3.shape, F32)
    for xlo in range(8):
        for g in range(4):
            s3[g + 1, pl.ds(8 + xlo, 8, stride=8), :] = u3[xlo, g]
    shape = (8, NZ)
    mine = lane(shape) // 16 == lax.broadcasted_iota(jnp.int32, shape, 0)
    tiles = []
    for k in range(6):
        for g in range(3):
            row = s3[iy + g, pl.ds(2 * ix + 6 + k, 1), :]
            tiles.append(jnp.where(mine, jnp.broadcast_to(row, shape), 0.0))
    spread = exact_dot(jnp.concatenate(tiles, 0), one_hot((NZ, NZ), lambda i, j: i % 16 == j // 8))
    for k in range(6):
        t = spread[24 * k : 24 * k + 24]
        e2[k, pl.ds(0, 24, stride=2), :] = t
        e2[k, pl.ds(1, 24, stride=2), :] = t

    for x in range(2, 14):
        ha[x] = u2[x] + e2[(x - 2) // 2]
    low = Level(2, None, b2, hx, hy, hz, hw, 8, 40)
    low.sweep(ha, hb, 3, 13)
    low.sweep(hb, ha, 4, 12)

    def grow1(k):
        t = ha[4 + k, pl.ds(8, 32), :]
        e1[k, pl.ds(0, 32, stride=2), :] = t
        e1[k, pl.ds(1, 32, stride=2), :] = t

    rows(0, 8, grow1)

    copy_rows([(b1_in, b1)], 2, 18)
    set_y1(b1, y0, y1, oy, 1)

    def add1(k):
        for j in range(2):
            ga_[2 + 2 * k + j] = u1[2 + 2 * k + j] + e1[k]

    rows(0, 8, add1)
    mid = Level(1, None, b1, gx_, gy_, gz_, gw_, 8, 56)
    mid.sweep(ga_, gb_, 3, 17)
    mid.sweep(gb_, ga_, 4, 16)

    def grow0(k):
        t = ga_[4 + k, pl.ds(8, 48), :]
        e0[k, pl.ds(0, 48, stride=2), :] = t
        e0[k, pl.ds(1, 48, stride=2), :] = t

    def add0(k):
        for j in range(2):
            ua[8 + 2 * k + j] = u0[8 + 2 * k + j] + e0[k]

    rows(0, 12, grow0, 4)
    rows(0, 12, add0, 4)
    top = Level(0, None, b, fx, fy, fz, w, 8, 88)
    top.sweep(ua, ub, 10, 30)
    top.sweep(ub, ua, 11, 29)

    def finish(x):
        out[x] = ua[X0 + x, pl.ds(Y0, NY), :]
        res[x] = top.residual(ua, X0 + x, Y0, NY)

    rows(0, NX, finish)


def swaps(axis, first, second):
    count = lax.axis_size(axis)

    def pairs(start):
        return [p for i in range(start, count - 1, 2) for p in ((i, i + 1), (i + 1, i))]

    late = lax.ppermute(second, axis, pairs(1))
    return lax.ppermute(first, axis, pairs(0)), late


def per_device(source, density, drag, porous_rows):
    sems = [pltpu.SemaphoreType.DMA((2, PARTS)), pltpu.SemaphoreType.DMA((6,))]
    block = (NX, NY, NZ)
    cond, source, p0, p1, q0, q1 = call(
        begin_kernel,
        [block, block, (32, 8, NZ), (32, 8, NZ)] + [(21, NY, NZ)] * 2,
        [block, block, pltpu.VMEM((NY,), jnp.int32)] + sems,
        (source, density, drag, porous_rows),
        "begin",
        16,
        4,
    )
    x0, x1 = swaps("gx", q0, q1)
    y0, y1 = swaps("gy", p0, p1)
    p0, p1 = call(corner_kernel, [(21, 16, NZ)] * 2, [], (y0, y1), "corners", 16)
    k0, k1 = swaps("gx", p0, p1)
    zero, one, two = (40, 96, NZ), (20, 64, NZ), (16, 48, NZ)
    small, small1 = (18, 96, NZ), (10, 64, NZ)
    inner = call(
        inner_kernel, [small] * 8 + [small1] * 6, [(8, 96, NZ)], (cond, source, y0, y1), "inner", 16, 0, 10**7
    )
    down = call(
        down_kernel,
        [zero] * 6 + [one] * 6 + [two] * 2 + [(8, 8, NZ)] * 2,
        [zero] * 2 + [one] * 2 + [(16, 96, NZ), (18, 96, NZ), (8, 64, NZ)],
        (x0, x1, k0, k1, *inner),
        "down",
        24,
    )
    level0, level1 = down[:6], down[6:12]
    u1, c2, b2, p0, p1 = down[11:]
    y0, y1 = swaps("gy", p0, p1)
    p0, p1 = call(edge2_kernel, [(192, NZ)] * 2, [one, two, two], (u1, c2, b2, y0, y1), "edges2", 16)
    x0, x1 = swaps("gx", p0, p1)
    *level2, u1, packed = call(
        level2_kernel,
        [two] * 6 + [one, (512, NZ)],
        [two] * 2 + [(2, 48, NZ)] * 3,
        (u1, c2, b2, y0, y1, x0, x1),
        "level2",
        16,
    )
    whole = lax.all_to_all(packed, ("gx", "gy"), 0, 0, tiled=True)
    out, res = call(
        up_kernel,
        [block] * 2,
        [(6, 80, NZ), (6, 48, NZ), (8, 64, NZ), (12, 96, NZ)] + [two] * 2 + [one] * 3 + [zero] * 2,
        (whole, y0, y1, *level2, *level1[:5], u1, *level0),
        "up",
        24,
    )
    return out, res


def solution(mesh):
    return jax.shard_map(
        per_device,
        mesh=mesh,
        in_specs=(P("gx", "gy", None), P("gx", "gy", None), P("gx", "gy", None), P("gy")),
        out_specs=(P("gx", "gy", None), P("gx", "gy", None)),
        check_vma=False,
    )
```

```python
import functools

import jax
import jax.numpy as jnp
from jax import lax
from jax.experimental import pallas as pl
from jax.experimental.pallas import tpu as pltpu
from jax.sharding import PartitionSpec as P

SWEEPS_COARSE = 16
DAMP = 0.8
KEEP = 1.0 - DAMP
H0 = 0.0002

NX, NY, NZ = 16, 64, 128
F32 = jnp.float32
VMEM = pl.BlockSpec(memory_space=pltpu.VMEM)
HBM = pl.BlockSpec(memory_space=pltpu.HBM)


def call(body, outs, scratch, args, name, vmem, hbm=0, cost=0):
    args = [pltpu.with_memory_space_constraint(a, pltpu.HBM) for a in args[:hbm]] + list(args[hbm:])
    return pl.pallas_call(
        body,
        out_shape=[jax.ShapeDtypeStruct(s, F32) for s in outs],
        in_specs=[HBM] * hbm + [VMEM] * (len(args) - hbm),
        out_specs=[VMEM] * len(outs),
        scratch_shapes=[pltpu.VMEM(s, F32) if isinstance(s, tuple) else s for s in scratch],
        compiler_params=pltpu.CompilerParams(vmem_limit_bytes=vmem * 2**20),
        name=name,
        cost_estimate=pl.CostEstimate(flops=cost, bytes_accessed=0, transcendentals=0) if cost else None,
    )(*args)


def recip(t):
    return 1.0 / t


def harmonic(a, b):
    return (2.0 * a) * b / jnp.maximum(a + b, 1e-30)


def lane(shape):
    return lax.broadcasted_iota(jnp.int32, shape, len(shape) - 1)


def lroll(v, shift):
    return pltpu.roll(v, shift % 128, v.ndim - 1)


def pair_lanes(v, s):
    first = (lane(v.shape) // s) % 2 == 0
    return v + jnp.where(first, lroll(v, -s), lroll(v, s))


def pack_lanes(tiles):
    n = len(tiles)
    out = tiles[0]
    for k in range(1, n):
        out = jnp.where(lane(out.shape) % n == k, tiles[k], out)
    return out


def unpack_lanes(p, n):
    at = lane(p.shape) % n
    moved = {d: p if d == 0 else lroll(p, -d) for d in range(1 - n, n)}
    tiles = []
    for k in range(n):
        out = moved[k]
        for m in range(1, n):
            out = jnp.where(at == m, moved[k - m], out)
        tiles.append(out)
    return tiles


def rows(lo, hi, body, unroll=8):
    whole = (hi - lo) // unroll

    def step(k, carry):
        for j in range(unroll):
            body(lo + k * unroll + j)
        return carry

    if whole > 1:
        lax.fori_loop(0, whole, step, 0)
        lo = lo + whole * unroll
    for x in range(lo, hi):
        body(x)


class Level:
    def __init__(self, depth, c, b, fx, fy, fz, w, ys, ye):
        self.h = H0 * 4.0**depth
        self.s = 2**depth
        self.c, self.b, self.fx, self.fy, self.fz, self.w = c, b, fx, fy, fz, w
        self.ys, self.n = ys, ye - ys

    def faces(self, lo, hi):
        here, above = pl.ds(self.ys, self.n), pl.ds(self.ys + 1, self.n)

        def body(x):
            c = self.c[x, here, :]
            twice, safe = c + c, c + 1e-30

            def face(other):
                return twice * other / (safe + other)

            self.fx[x, here, :] = face(self.c[x + 1, here, :])
            self.fy[x, here, :] = face(self.c[x, above, :])
            self.fz[x, here, :] = face(lroll(c, -self.s))

        rows(lo, hi, body)

    def weights(self, lo, hi, start=None):
        here, below = pl.ds(self.ys, self.n), pl.ds(self.ys - 1, self.n)

        def body(x):
            fz = self.fz[x, here, :]
            d = self.fx[x, here, :] + self.fx[x - 1, here, :]
            d = d + (self.fy[x, here, :] + self.fy[x, below, :])
            d = d + (fz + lroll(fz, self.s))
            w = DAMP * recip(self.h + d)
            self.w[x, here, :] = w
            if start is not None:
                start[x, here, :] = w * self.b[x, here, :]

        rows(lo, hi, body)

    def start(self, out, lo, hi):
        here = pl.ds(self.ys, self.n)

        def body(x):
            out[x, here, :] = self.w[x, here, :] * self.b[x, here, :]

        rows(lo, hi, body)

    def sweep(self, u, out, lo, hi):
        here = pl.ds(self.ys, self.n)
        above, below = pl.ds(self.ys + 1, self.n), pl.ds(self.ys - 1, self.n)

        def body(x):
            v = u[x, here, :]
            fz = self.fz[x, here, :]
            acc = fz * lroll(v, -self.s) + lroll(fz * v, self.s)
            acc = acc + (self.fx[x, here, :] * u[x + 1, here, :] + self.fx[x - 1, here, :] * u[x - 1, here, :])
            acc = acc + (self.fy[x, here, :] * u[x, above, :] + self.fy[x, below, :] * u[x, below, :])
            out[x, here, :] = KEEP * v + self.w[x, here, :] * (self.b[x, here, :] + acc)

        rows(lo, hi, body)

    def residual(self, u, x, y, n):
        here, above, below = pl.ds(y, n), pl.ds(y + 1, n), pl.ds(y - 1, n)
        v = u[x, here, :]
        flow = self.fz[x, here, :] * (lroll(v, -self.s) - v)
        r = self.b[x, here, :] - self.h * v
        r = r + (flow - lroll(flow, self.s))
        r = r + self.fx[x, here, :] * (u[x + 1, here, :] - v)
        r = r + self.fx[x - 1, here, :] * (u[x - 1, here, :] - v)
        r = r + self.fy[x, here, :] * (u[x, above, :] - v)
        return r + self.fy[x, below, :] * (u[x, below, :] - v)

    def halve(self, tmp, out, lo, hi, x_to, scale):
        half = tmp.shape[1] // 2

        def body(k):
            t = tmp[k, pl.ds(0, half, stride=2), :] + tmp[k, pl.ds(1, half, stride=2), :]
            out[x_to + k, pl.ds(8, half), :] = scale * pair_lanes(t, self.s)

        rows(lo, hi, body)

    def restrict(self, u, tmp, out, lo, hi, x_from, x_to):
        def body(k):
            x = x_from + 2 * k
            both = self.residual(u, x, self.ys, self.n) + self.residual(u, x + 1, self.ys, self.n)
            tmp[k, pl.ds(self.ys, self.n), :] = both

        rows(lo, hi, body, 4)
        self.halve(tmp, out, lo, hi, x_to, 0.5)

    def restrict_c(self, tmp, out, lo, hi, x_from, x_to):
        def body(k):
            x = x_from + 2 * k
            tmp[k] = self.c[x] + self.c[x + 1]

        rows(lo, hi, body)
        self.halve(tmp, out, lo, hi, x_to, 0.125)


def odd(axis):
    return lax.axis_index(axis) % 2


PARTS = 4


def begin_kernel(source, density, drag, porous, cond, rhs, ypack0, ypack1, dens, dra, por, sem, esem):
    o = odd("gy")
    at0 = pl.multiple_of((1 - o) * (NY - 8), 8)
    at1 = pl.multiple_of(o * (NY - 8), 8)
    part = NX // PARTS
    loads = []
    first = pltpu.make_async_copy(porous, por, esem.at[3])
    first.start()
    for k in range(PARTS):
        here = pl.ds(k * part, part)
        for j, (src, dst) in enumerate(((density, dens), (drag, dra))):
            loads.append(pltpu.make_async_copy(src.at[here], dst.at[here], sem.at[j, k]))
            loads[-1].start()
    edges = []
    for j, (at, pack) in enumerate(((at0, ypack0), (at1, ypack1))):
        edges.append(pltpu.make_async_copy(source.at[:, pl.ds(at, 8), :], pack.at[pl.ds(NX, NX)], esem.at[j]))
        edges[-1].start()
    edges.append(pltpu.make_async_copy(source, rhs, esem.at[2]))
    edges[-1].start()
    first.wait()
    shape = (NY, NZ)
    line = jnp.broadcast_to(por[...].astype(F32)[None], (NY, NY))
    same = lax.broadcasted_iota(jnp.int32, (NY, NY), 0) == lax.broadcasted_iota(jnp.int32, (NY, NY), 1)
    mask = jnp.broadcast_to(jnp.sum(jnp.where(same, line, 0.0), axis=1, keepdims=True), shape)
    for k in range(PARTS):
        loads[2 * k].wait()
        loads[2 * k + 1].wait()
        for x in range(k * part, k * part + part):
            cond[x] = recip(dens[x] * (1.0 + dra[x] * mask))
            ypack0[x] = cond[x, pl.ds(at0, 8), :]
            ypack1[x] = cond[x, pl.ds(at1, 8), :]
    for edge in edges:
        edge.wait()


def edge_kernel(cond, source, xpack0, xpack1):
    ox = odd("gx")
    for last, pack in ((1 - ox, xpack0), (ox, xpack1)):
        for k in range(11):
            pack[k] = cond[k + last * (NX - 11)]
        for k in range(10):
            pack[11 + k] = source[k + last * (NX - 10)]


CORNERS = (
    [(0, d, d - 1, 0) for d in (1, 2, 3, 4, 5, 6, 7)]
    + [(0, 9, 4, 2), (0, 8, 5, 3), (0, 10, 6, 1)]
    + [(1, d, d + 6, 0) for d in (1, 2, 3, 4, 5, 6)]
    + [(1, 7, 11, 3), (1, 8, 12, 2), (1, 9, 10, 1)]
)
TILES = 13


def turn(v, by):
    return v if by == 0 else pltpu.roll(v, by % 8, 0)


def corner_kernel(y0, y1, xpack0, xpack1):
    ox, oy = odd("gx"), odd("gy")
    at0 = pl.multiple_of((1 - oy) * 8, 8)
    at1 = pl.multiple_of(oy * 8, 8)
    row = lax.broadcasted_iota(jnp.int32, (8, NZ), 0)
    for pack, last in ((xpack0, 1 - ox), (xpack1, ox)):
        for y, at, high in ((y0, at0, 1 - oy), (y1, at1, oy)):
            tiles = {}
            for field, d, t, by in CORNERS:
                v = y[field * NX + d - 1 + last * (NX + 1 - 2 * d)]
                if by == 0:
                    tiles[t] = v
                else:
                    low = jnp.where(row < by, turn(v, by), tiles[t])
                    top = jnp.where(row >= 8 - by, turn(v, -by), tiles[t])
                    tiles[t] = jnp.where(high == 1, top, low)
            for t in range(TILES):
                pack[t, pl.ds(at, 8), :] = tiles[t]


X0, Y0 = 12, 16
X1, Y1 = 6, 16
X2, Y2 = 6, 16


def levels_down(c, b, fx, fy, fz, w, c1, b1, gx_, gy_, gz_, gw_):
    top = Level(0, c, b, fx, fy, fz, w, 8, 88)
    return top, Level(1, c1, b1, gx_, gy_, gz_, gw_, 8, 56)


def inner_kernel(cond, source, y0, y1, c, b, fx, fy, fz, w, ua, ub, c1, b1, gx_, gy_, gz_, gw_, tmp):
    oy = odd("gy")
    at0 = pl.multiple_of(8 + (1 - oy) * (NY + 8), 8)
    at1 = pl.multiple_of(8 + oy * (NY + 8), 8)

    def own(x):
        c[1 + x, pl.ds(Y0, NY), :] = cond[x]
        c[1 + x, pl.ds(at0, 8), :] = y0[x]
        c[1 + x, pl.ds(at1, 8), :] = y1[x]
        b[1 + x, pl.ds(Y0, NY), :] = source[x]
        b[1 + x, pl.ds(at0, 8), :] = y0[NX + x]
        b[1 + x, pl.ds(at1, 8), :] = y1[NX + x]

    rows(0, NX, own)
    top, mid = levels_down(c, b, fx, fy, fz, w, c1, b1, gx_, gy_, gz_, gw_)
    top.faces(1, 17)
    top.weights(2, 16, ua)
    top.sweep(ua, ub, 3, 15)
    top.restrict_c(tmp, c1, 0, 8, 1, 1)
    top.restrict(ub, tmp, b1, 2, 6, 1, 1)
    mid.faces(1, 9)
    mid.weights(2, 8)


def down_kernel(
    x0, x1, k0, k1, c_in, b_in, fx_in, fy_in, fz_in, w_in, ua_in, ub_in, c1_in, b1_in, gx_in, gy_in, gz_in, gw_in,
    fx, fy, fz, w, b, ub, gx_, gy_, gz_, gw_, b1, u1, c2, b2, ypack0, ypack1,
    c, ua, c1, ga_, tmp, ctmp, tmp1,
):
    ox, oy = odd("gx"), odd("gy")
    here, here1 = pl.ds(8, 80), pl.ds(8, 48)

    for x, pack, up in ((x0, k0, 1 - ox), (x1, k1, ox)):
        for k in range(11):
            c[k + 1 + up * (11 + NX), pl.ds(Y0, NY), :] = x[k]
        for k in range(10):
            b[k + 2 + up * (10 + NX), pl.ds(Y0, NY), :] = x[11 + k]
        for field, d, t, by in CORNERS:
            ref = (c, b)[field]
            at = X0 - d + up * (NX - 1 + 2 * d)
            ref[at, pl.ds(8, 8), :] = turn(pack[t, pl.ds(0, 8), :], -by)
            ref[at, pl.ds(80, 8), :] = turn(pack[t, pl.ds(8, 8), :], by)
    for x in (1, 16):
        c[x + 11, here, :] = c_in[x, here, :]
    for x in (2, 3, 14, 15):
        ua[x + 11, here, :] = ua_in[x, here, :]

    def fill(x):
        for ref, src in ((fx, fx_in), (fy, fy_in), (fz, fz_in), (w, w_in), (b, b_in), (ub, ub_in)):
            ref[x + 11, here, :] = src[x, here, :]

    rows(1, 17, fill)
    for x in range(1, 9):
        c1[x + 5, here1, :] = c1_in[x, here1, :]
        for ref, src in ((gx_, gx_in), (gy_, gy_in), (gz_, gz_in), (gw_, gw_in), (b1, b1_in)):
            ref[x + 5, here1, :] = src[x, here1, :]

    top, mid = levels_down(c, b, fx, fy, fz, w, c1, b1, gx_, gy_, gz_, gw_)
    top.faces(1, 12)
    top.faces(27, 39)
    top.weights(2, 13, ua)
    top.weights(27, 38, ua)
    top.sweep(ua, ub, 3, 14)
    top.sweep(ua, ub, 26, 37)
    top.restrict_c(ctmp, c1, 0, 5, 2, 1)
    top.restrict_c(ctmp, c1, 13, 18, 2, 1)
    top.restrict(ub, tmp, b1, 0, 6, 4, 2)
    top.restrict(ub, tmp, b1, 10, 16, 4, 2)

    mid.faces(1, 6)
    mid.faces(13, 19)
    mid.weights(2, 7)
    mid.weights(13, 18)
    mid.start(ga_, 2, 18)
    mid.sweep(ga_, u1, 3, 17)
    mid.restrict(u1, tmp1, b2, 0, 6, 4, 5)
    mid.restrict_c(tmp1, c2, 0, 8, 2, 4)

    e0 = Y1 + (1 - oy) * 28
    e1 = Y1 + oy * 28
    f0 = pl.multiple_of(Y2 + (1 - oy) * 8, 8)
    f1 = pl.multiple_of(Y2 + oy * 8, 8)
    for pack, e, f in ((ypack0, e0, f0), (ypack1, e1, f1)):
        for k in range(4):
            x = X1 + 2 * k
            pack[k, pl.ds(0, 4), :] = pack_lanes([u1[x + j, pl.ds(e, 4), :] for j in range(2)])
            pack[k, pl.ds(4, 4), :] = pack_lanes([b1[x + j, pl.ds(e, 4), :] for j in range(2)])
        for k in range(2):
            pack[4 + k] = pack_lanes([b2[X2 - 1 + 4 * k + j, pl.ds(f, 8), :] for j in range(4)])
            pack[6 + k] = pack_lanes([c2[X2 - 2 + 4 * k + j, pl.ds(f, 8), :] for j in range(4)])


def set_y1(ref, y0, y1, oy, part):
    a0 = Y1 - 4 + (1 - oy) * 36
    a1 = Y1 - 4 + oy * 36
    for y, a in ((y0, a0), (y1, a1)):
        for k in range(4):
            for j, v in enumerate(unpack_lanes(y[k], 2)):
                ref[X1 + 2 * k + j, pl.ds(a, 4), :] = v[4 * part : 4 * part + 4]


def set_y2(c2, b2, y0, y1, oy):
    a0 = pl.multiple_of(Y2 - 8 + (1 - oy) * 24, 8)
    a1 = pl.multiple_of(Y2 - 8 + oy * 24, 8)
    for y, a in ((y0, a0), (y1, a1)):
        for k in range(2):
            for j, v in enumerate(unpack_lanes(y[4 + k], 4)):
                if 4 * k + j < 6:
                    b2[X2 - 1 + 4 * k + j, pl.ds(a, 8), :] = v
            for j, v in enumerate(unpack_lanes(y[6 + k], 4)):
                c2[X2 - 2 + 4 * k + j, pl.ds(a, 8), :] = v


def copy_rows(pairs, lo, hi):
    def body(x):
        for src, dst in pairs:
            dst[x] = src[x]

    rows(lo, hi, body)


def edge2_kernel(u1_in, c2_in, b2_in, y0, y1, xpack0, xpack1, u1, c2, b2):
    ox, oy = odd("gx"), odd("gy")
    copy_rows([(u1_in, u1)], X1, X1 + 8)
    copy_rows([(c2_in, c2), (b2_in, b2)], X2 - 2, X2 + 6)
    set_y1(u1, y0, y1, oy, 0)
    set_y2(c2, b2, y0, y1, oy)
    for pack, last in ((xpack0, 1 - ox), (xpack1, ox)):
        for k in range(2):
            x = X1 + 2 * k + last * 4
            pack[pl.ds(k * 48, 48), :] = pack_lanes([u1[x + j, pl.ds(8, 48), :] for j in range(2)])
        t = [c2[X2 + k - 2 * last, pl.ds(8, 32), :] for k in range(6)]
        t += [b2[X2 + k - last, pl.ds(8, 32), :] for k in range(5)]
        for k in range(3):
            pack[pl.ds(96 + k * 32, 32), :] = pack_lanes((t + t[:1])[4 * k : 4 * k + 4])


def one_hot(shape, f):
    i = lax.broadcasted_iota(jnp.int32, shape, 0)
    j = lax.broadcasted_iota(jnp.int32, shape, 1)
    return jnp.where(f(i, j), 1.0, 0.0).astype(F32)


def exact_dot(a, b):
    return jnp.dot(a, b, precision=lax.Precision.HIGHEST, preferred_element_type=F32)


def level2_kernel(
    u1_in, c2_in, b2_in, y0, y1, x0, x1,
    fx, fy, fz, w, b2, u2, u1, gather,
    c2, ua, tmp, b3, c3,
):
    ox, oy = odd("gx"), odd("gy")
    copy_rows([(u1_in, u1)], X1, X1 + 8)
    copy_rows([(c2_in, c2), (b2_in, b2)], X2 - 2, X2 + 6)
    set_y1(u1, y0, y1, oy, 0)
    set_y2(c2, b2, y0, y1, oy)
    for pack, up in ((x0, 1 - ox), (x1, ox)):
        for k in range(2):
            for j, v in enumerate(unpack_lanes(pack[pl.ds(k * 48, 48), :], 2)):
                u1[X1 - 4 + 2 * k + j + up * 12, pl.ds(8, 48), :] = v
        t = []
        for k in range(3):
            t += unpack_lanes(pack[pl.ds(96 + k * 32, 32), :], 4)
        for k in range(6):
            c2[X2 - 6 + k + up * 10, pl.ds(8, 32), :] = t[k]
        for k in range(5):
            b2[X2 - 5 + k + up * 9, pl.ds(8, 32), :] = t[6 + k]

    low = Level(2, c2, b2, fx, fy, fz, w, 8, 40)
    low.faces(0, 15)
    low.weights(1, 15, ua)
    low.sweep(ua, u2, 2, 14)
    low.restrict(u2, tmp, b3, 0, 2, X2, 0)
    low.restrict_c(tmp, c3, 0, 2, X2, 0)
    both = jnp.concatenate(
        [b3[0, pl.ds(16, 8), :], b3[1, pl.ds(16, 8), :], c3[0, pl.ds(16, 8), :], c3[1, pl.ds(16, 8), :]], 0
    )
    spread = exact_dot(both, one_hot((NZ, NZ), lambda i, j: i == 8 * (j % 16)))
    shape = (8, NZ)
    mine = lane(shape) // 16 == lax.broadcasted_iota(jnp.int32, shape, 0)
    packed = [
        jnp.sum(jnp.where(mine, spread[8 * k : 8 * k + 8], 0.0), axis=0, keepdims=True) for k in range(4)
    ]
    eight = jnp.concatenate(packed + packed, 0)

    def body(k):
        gather[pl.ds(pl.multiple_of(8 * k, 8), 8), :] = eight

    rows(0, 64, body, 8)


class Whole:
    def __init__(self, depth, b, c):
        self.h = H0 * 4.0**depth
        self.s = 2 ** (depth - 3)
        self.st = 16 * self.s
        self.b = b
        n = c.shape[0]
        sub = lax.broadcasted_iota(jnp.int32, (1,) + c.shape[1:], 2)
        up = self.xp(c)
        end = jnp.where(sub == 7, 0.0, up[n - 1 :])
        up = jnp.concatenate([up[: n - 1], end], 0) if n > 1 else end
        self.fxp = harmonic(c, up)
        up = self.yp(c)
        last = up[:, 3:]
        last = jnp.where(lane(last.shape) >= 128 - self.st, 0.0, last)
        self.fyp = harmonic(c, jnp.concatenate([up[:, :3], last], 1))
        self.fzp = harmonic(c, self.zp(c))
        self.fxm, self.fym, self.fzm = self.xm(self.fxp), self.ym(self.fyp), self.zm(self.fzp)
        d = self.h + self.fxp + self.fxm + self.fyp + self.fym + self.fzp + self.fzm
        self.w = DAMP * recip(d)

    def xp(self, v):
        wrap = pltpu.roll(v[:1], 7, 2)
        return jnp.concatenate([v[1:], wrap], 0) if v.shape[0] > 1 else wrap

    def xm(self, v):
        n = v.shape[0]
        wrap = pltpu.roll(v[n - 1 :], 1, 2)
        return jnp.concatenate([wrap, v[: n - 1]], 0) if n > 1 else wrap

    def yp(self, v):
        w = v if self.st == 128 else lroll(v, -self.st)
        far = jnp.concatenate([w[:, 1:], w[:, :1]], 1)
        return far if self.st == 128 else jnp.where(lane(v.shape) < 128 - self.st, w, far)

    def ym(self, v):
        w = v if self.st == 128 else lroll(v, self.st)
        far = jnp.concatenate([w[:, 3:], w[:, :3]], 1)
        return far if self.st == 128 else jnp.where(lane(v.shape) >= self.st, w, far)

    def zp(self, v):
        s = self.s
        return jnp.where(lane(v.shape) % 16 < 16 - s, lroll(v, -s), lroll(v, 16 - s))

    def zm(self, v):
        s = self.s
        return self.zp(v) if s == 8 else jnp.where(lane(v.shape) % 16 >= s, lroll(v, s), lroll(v, s - 16))

    def flux(self, v):
        acc = self.fxp * self.xp(v) + self.fxm * self.xm(v)
        acc = acc + self.fyp * self.yp(v) + self.fym * self.ym(v)
        return acc + self.fzp * self.zp(v) + self.fzm * self.zm(v)

    def sweep(self, v):
        return KEEP * v + self.w * (self.b + self.flux(v))

    def residual(self, v):
        r = self.b - self.h * v
        r = r + self.fxp * (self.xp(v) - v) + self.fxm * (self.xm(v) - v)
        r = r + self.fyp * (self.yp(v) - v) + self.fym * (self.ym(v) - v)
        return r + self.fzp * (self.zp(v) - v) + self.fzm * (self.zm(v) - v)

    def coarse(self, v, scale):
        v = jnp.concatenate([v[2 * k : 2 * k + 1] + v[2 * k + 1 : 2 * k + 2] for k in range(v.shape[0] // 2)], 0)
        return scale * pair_lanes(pair_lanes(v, self.s), self.st)


def whole_cycle(depth, b, c):
    level = Whole(depth, b, c)
    v = level.w * b
    if depth == 6:
        for _ in range(SWEEPS_COARSE - 1):
            v = level.sweep(v)
        return v
    v = level.sweep(v)
    below = whole_cycle(depth + 1, level.coarse(level.residual(v), 0.5), level.coarse(c, 0.125))
    v = v + jnp.concatenate([below[k // 2 : k // 2 + 1] for k in range(v.shape[0])], 0)
    return level.sweep(level.sweep(v))


def up_kernel(
    gather, y0, y1,
    hx, hy, hz, hw, b2, u2,
    gx_, gy_, gz_, gw_, b1_in, u1,
    fx, fy, fz, w, b, u0,
    out, res,
    s3, e2, e1, e0, ha, hb, b1, ga_, gb_, ua, ub,
):
    ix, iy = lax.axis_index("gx"), lax.axis_index("gy")
    oy = iy % 2

    def field(k):
        return jnp.stack(
            [
                jnp.stack([gather[pl.ds(xq * 16 + g * 4 + k + xl, 8, stride=64), :] for g in range(4)], 0)
                for xq in range(4)
                for xl in range(2)
            ],
            0,
        )

    u3 = whole_cycle(3, field(0), field(2))
    s3[...] = jnp.zeros(s3.shape, F32)
    for xlo in range(8):
        for g in range(4):
            s3[g + 1, pl.ds(8 + xlo, 8, stride=8), :] = u3[xlo, g]
    shape = (8, NZ)
    mine = lane(shape) // 16 == lax.broadcasted_iota(jnp.int32, shape, 0)
    tiles = []
    for k in range(6):
        for g in range(3):
            row = s3[iy + g, pl.ds(2 * ix + 6 + k, 1), :]
            tiles.append(jnp.where(mine, jnp.broadcast_to(row, shape), 0.0))
    spread = exact_dot(jnp.concatenate(tiles, 0), one_hot((NZ, NZ), lambda i, j: i % 16 == j // 8))
    for k in range(6):
        t = spread[24 * k : 24 * k + 24]
        e2[k, pl.ds(0, 24, stride=2), :] = t
        e2[k, pl.ds(1, 24, stride=2), :] = t

    for x in range(2, 14):
        ha[x] = u2[x] + e2[(x - 2) // 2]
    low = Level(2, None, b2, hx, hy, hz, hw, 8, 40)
    low.sweep(ha, hb, 3, 13)
    low.sweep(hb, ha, 4, 12)

    def grow1(k):
        t = ha[4 + k, pl.ds(8, 32), :]
        e1[k, pl.ds(0, 32, stride=2), :] = t
        e1[k, pl.ds(1, 32, stride=2), :] = t

    rows(0, 8, grow1)

    copy_rows([(b1_in, b1)], 2, 18)
    set_y1(b1, y0, y1, oy, 1)

    def add1(k):
        for j in range(2):
            ga_[2 + 2 * k + j] = u1[2 + 2 * k + j] + e1[k]

    rows(0, 8, add1)
    mid = Level(1, None, b1, gx_, gy_, gz_, gw_, 8, 56)
    mid.sweep(ga_, gb_, 3, 17)
    mid.sweep(gb_, ga_, 4, 16)

    def grow0(k):
        t = ga_[4 + k, pl.ds(8, 48), :]
        e0[k, pl.ds(0, 48, stride=2), :] = t
        e0[k, pl.ds(1, 48, stride=2), :] = t

    def add0(k):
        for j in range(2):
            ua[8 + 2 * k + j] = u0[8 + 2 * k + j] + e0[k]

    rows(0, 12, grow0, 4)
    rows(0, 12, add0, 4)
    top = Level(0, None, b, fx, fy, fz, w, 8, 88)
    top.sweep(ua, ub, 10, 30)
    top.sweep(ub, ua, 11, 29)

    def finish(x):
        out[x] = ua[X0 + x, pl.ds(Y0, NY), :]
        res[x] = top.residual(ua, X0 + x, Y0, NY)

    rows(0, NX, finish)


def swaps(axis, first, second):
    count = lax.axis_size(axis)

    def pairs(start):
        return [p for i in range(start, count - 1, 2) for p in ((i, i + 1), (i + 1, i))]

    late = lax.ppermute(second, axis, pairs(1))
    return lax.ppermute(first, axis, pairs(0)), late


def per_device(source, density, drag, porous_rows):
    sems = [pltpu.SemaphoreType.DMA((2, PARTS)), pltpu.SemaphoreType.DMA((4,))]
    block = (NX, NY, NZ)
    cond, source, p0, p1 = call(
        begin_kernel,
        [block, block, (32, 8, NZ), (32, 8, NZ)],
        [block, block, pltpu.VMEM((NY,), jnp.int32)] + sems,
        (source, density, drag, porous_rows),
        "begin",
        16,
        4,
    )
    y0, y1 = swaps("gy", p0, p1)
    q0, q1 = call(edge_kernel, [(21, NY, NZ)] * 2, [], (cond, source), "edges", 16, 0, 10**9)
    x0, x1 = swaps("gx", q0, q1)
    p0, p1 = call(corner_kernel, [(TILES, 16, NZ)] * 2, [], (y0, y1), "corners", 16)
    k0, k1 = swaps("gx", p0, p1)
    zero, one, two = (40, 96, NZ), (20, 64, NZ), (16, 48, NZ)
    small, small1 = (18, 96, NZ), (10, 64, NZ)
    inner = call(
        inner_kernel, [small] * 8 + [small1] * 6, [(8, 96, NZ)], (cond, source, y0, y1), "inner", 16, 0, 10**10
    )
    down = call(
        down_kernel,
        [zero] * 6 + [one] * 6 + [two] * 2 + [(8, 8, NZ)] * 2,
        [zero] * 2 + [one] * 2 + [(16, 96, NZ), (18, 96, NZ), (8, 64, NZ)],
        (x0, x1, k0, k1, *inner),
        "down",
        24,
    )
    level0, level1 = down[:6], down[6:12]
    u1, c2, b2, p0, p1 = down[11:]
    y0, y1 = swaps("gy", p0, p1)
    p0, p1 = call(edge2_kernel, [(192, NZ)] * 2, [one, two, two], (u1, c2, b2, y0, y1), "edges2", 16)
    x0, x1 = swaps("gx", p0, p1)
    *level2, u1, packed = call(
        level2_kernel,
        [two] * 6 + [one, (512, NZ)],
        [two] * 2 + [(2, 48, NZ)] * 3,
        (u1, c2, b2, y0, y1, x0, x1),
        "level2",
        16,
    )
    whole = lax.all_to_all(packed, ("gx", "gy"), 0, 0, tiled=True)
    out, res = call(
        up_kernel,
        [block] * 2,
        [(6, 80, NZ), (6, 48, NZ), (8, 64, NZ), (12, 96, NZ)] + [two] * 2 + [one] * 3 + [zero] * 2,
        (whole, y0, y1, *level2, *level1[:5], u1, *level0),
        "up",
        24,
    )
    return out, res


def solution(mesh):
    return jax.shard_map(
        per_device,
        mesh=mesh,
        in_specs=(P("gx", "gy", None), P("gx", "gy", None), P("gx", "gy", None), P("gy")),
        out_specs=(P("gx", "gy", None), P("gx", "gy", None)),
        check_vma=False,
    )
```

```python
import functools

import jax
import jax.numpy as jnp
from jax import lax
from jax.experimental import pallas as pl
from jax.experimental.pallas import tpu as pltpu
from jax.sharding import PartitionSpec as P

SWEEPS_COARSE = 16
DAMP = 0.8
KEEP = 1.0 - DAMP
H0 = 0.0002

NX, NY, NZ = 16, 64, 128
F32 = jnp.float32
VMEM = pl.BlockSpec(memory_space=pltpu.VMEM)
HBM = pl.BlockSpec(memory_space=pltpu.HBM)


def call(body, outs, scratch, args, name, vmem, hbm=0, cost=0):
    args = [pltpu.with_memory_space_constraint(a, pltpu.HBM) for a in args[:hbm]] + list(args[hbm:])
    return pl.pallas_call(
        body,
        out_shape=[jax.ShapeDtypeStruct(s, F32) for s in outs],
        in_specs=[HBM] * hbm + [VMEM] * (len(args) - hbm),
        out_specs=[VMEM] * len(outs),
        scratch_shapes=[pltpu.VMEM(s, F32) if isinstance(s, tuple) else s for s in scratch],
        compiler_params=pltpu.CompilerParams(vmem_limit_bytes=vmem * 2**20),
        name=name,
        cost_estimate=pl.CostEstimate(flops=cost, bytes_accessed=0, transcendentals=0) if cost else None,
    )(*args)


def recip(t):
    return 1.0 / t


def harmonic(a, b):
    return (2.0 * a) * b / jnp.maximum(a + b, 1e-30)


def lane(shape):
    return lax.broadcasted_iota(jnp.int32, shape, len(shape) - 1)


def lroll(v, shift):
    return pltpu.roll(v, shift % 128, v.ndim - 1)


def pair_lanes(v, s):
    first = (lane(v.shape) // s) % 2 == 0
    return v + jnp.where(first, lroll(v, -s), lroll(v, s))


def pack_lanes(tiles):
    n = len(tiles)
    out = tiles[0]
    for k in range(1, n):
        out = jnp.where(lane(out.shape) % n == k, tiles[k], out)
    return out


def unpack_lanes(p, n):
    at = lane(p.shape) % n
    moved = {d: p if d == 0 else lroll(p, -d) for d in range(1 - n, n)}
    tiles = []
    for k in range(n):
        out = moved[k]
        for m in range(1, n):
            out = jnp.where(at == m, moved[k - m], out)
        tiles.append(out)
    return tiles


def rows(lo, hi, body, unroll=8):
    whole = (hi - lo) // unroll

    def step(k, carry):
        for j in range(unroll):
            body(lo + k * unroll + j)
        return carry

    if whole > 1:
        lax.fori_loop(0, whole, step, 0)
        lo = lo + whole * unroll
    for x in range(lo, hi):
        body(x)


class Level:
    def __init__(self, depth, c, b, fx, fy, fz, w, ys, ye):
        self.h = H0 * 4.0**depth
        self.s = 2**depth
        self.c, self.b, self.fx, self.fy, self.fz, self.w = c, b, fx, fy, fz, w
        self.ys, self.n = ys, ye - ys

    def faces(self, lo, hi):
        here, above = pl.ds(self.ys, self.n), pl.ds(self.ys + 1, self.n)

        def body(x):
            c = self.c[x, here, :]
            twice, safe = c + c, c + 1e-30

            def face(other):
                return twice * other / (safe + other)

            self.fx[x, here, :] = face(self.c[x + 1, here, :])
            self.fy[x, here, :] = face(self.c[x, above, :])
            self.fz[x, here, :] = face(lroll(c, -self.s))

        rows(lo, hi, body)

    def weights(self, lo, hi, start=None):
        here, below = pl.ds(self.ys, self.n), pl.ds(self.ys - 1, self.n)

        def body(x):
            fz = self.fz[x, here, :]
            d = self.fx[x, here, :] + self.fx[x - 1, here, :]
            d = d + (self.fy[x, here, :] + self.fy[x, below, :])
            d = d + (fz + lroll(fz, self.s))
            w = DAMP * recip(self.h + d)
            self.w[x, here, :] = w
            if start is not None:
                start[x, here, :] = w * self.b[x, here, :]

        rows(lo, hi, body)

    def start(self, out, lo, hi):
        here = pl.ds(self.ys, self.n)

        def body(x):
            out[x, here, :] = self.w[x, here, :] * self.b[x, here, :]

        rows(lo, hi, body)

    def sweep(self, u, out, lo, hi):
        here = pl.ds(self.ys, self.n)
        above, below = pl.ds(self.ys + 1, self.n), pl.ds(self.ys - 1, self.n)

        def body(x):
            v = u[x, here, :]
            fz = self.fz[x, here, :]
            acc = fz * lroll(v, -self.s) + lroll(fz * v, self.s)
            acc = acc + (self.fx[x, here, :] * u[x + 1, here, :] + self.fx[x - 1, here, :] * u[x - 1, here, :])
            acc = acc + (self.fy[x, here, :] * u[x, above, :] + self.fy[x, below, :] * u[x, below, :])
            out[x, here, :] = KEEP * v + self.w[x, here, :] * (self.b[x, here, :] + acc)

        rows(lo, hi, body)

    def residual(self, u, x, y, n):
        here, above, below = pl.ds(y, n), pl.ds(y + 1, n), pl.ds(y - 1, n)
        v = u[x, here, :]
        flow = self.fz[x, here, :] * (lroll(v, -self.s) - v)
        r = self.b[x, here, :] - self.h * v
        r = r + (flow - lroll(flow, self.s))
        r = r + self.fx[x, here, :] * (u[x + 1, here, :] - v)
        r = r + self.fx[x - 1, here, :] * (u[x - 1, here, :] - v)
        r = r + self.fy[x, here, :] * (u[x, above, :] - v)
        return r + self.fy[x, below, :] * (u[x, below, :] - v)

    def halve(self, tmp, out, lo, hi, x_to, scale):
        half = tmp.shape[1] // 2

        def body(k):
            t = tmp[k, pl.ds(0, half, stride=2), :] + tmp[k, pl.ds(1, half, stride=2), :]
            out[x_to + k, pl.ds(8, half), :] = scale * pair_lanes(t, self.s)

        rows(lo, hi, body)

    def restrict(self, u, tmp, out, lo, hi, x_from, x_to):
        def body(k):
            x = x_from + 2 * k
            both = self.residual(u, x, self.ys, self.n) + self.residual(u, x + 1, self.ys, self.n)
            tmp[k, pl.ds(self.ys, self.n), :] = both

        rows(lo, hi, body, 4)
        self.halve(tmp, out, lo, hi, x_to, 0.5)

    def restrict_c(self, tmp, out, lo, hi, x_from, x_to):
        def body(k):
            x = x_from + 2 * k
            tmp[k] = self.c[x] + self.c[x + 1]

        rows(lo, hi, body)
        self.halve(tmp, out, lo, hi, x_to, 0.125)


def odd(axis):
    return lax.axis_index(axis) % 2


PARTS = 4


def stored(x):
    o = odd("gx")
    return o * (NX - 1) + (1 - 2 * o) * x


def begin_kernel(source, density, drag, porous, cond, rhs, ypack0, ypack1, dens, dra, src, por, sem, psem):
    o = odd("gy")
    at0 = pl.multiple_of((1 - o) * (NY - 8), 8)
    at1 = pl.multiple_of(o * (NY - 8), 8)
    part = NX // PARTS
    loads = []
    first = pltpu.make_async_copy(porous, por, psem)
    first.start()
    for k in range(PARTS):
        here = pl.ds(k * part, part)
        for j, (ref, dst) in enumerate(((density, dens), (drag, dra), (source, src))):
            loads.append(pltpu.make_async_copy(ref.at[here], dst.at[here], sem.at[j, k]))
            loads[-1].start()
    first.wait()
    line = jnp.broadcast_to(por[...].astype(F32)[None], (NY, NY))
    same = lax.broadcasted_iota(jnp.int32, (NY, NY), 0) == lax.broadcasted_iota(jnp.int32, (NY, NY), 1)
    mask = jnp.broadcast_to(jnp.sum(jnp.where(same, line, 0.0), axis=1, keepdims=True), (NY, NZ))
    for k in range(PARTS):
        for load in loads[3 * k : 3 * k + 3]:
            load.wait()
        for x in range(k * part, k * part + part):
            to = stored(x)
            cond[to] = recip(dens[x] * (1.0 + dra[x] * mask))
            rhs[to] = src[x]
            for pack, at in ((ypack0, at0), (ypack1, at1)):
                pack[to] = cond[to, pl.ds(at, 8), :]
                pack[NX + to] = src[x, pl.ds(at, 8), :]


HIGH_C, HIGH_B, LOW_C, LOW_B = 11, 10, 8, 6


def edge_kernel(cond, source, high, low):
    for d in range(HIGH_C):
        high[d] = cond[NX - 1 - d]
    for d in range(HIGH_B):
        high[HIGH_C + d] = source[NX - 1 - d]
    for d in range(LOW_C):
        low[d] = cond[d]
    for d in range(LOW_B):
        low[LOW_C + d] = source[d]


HIGH = (
    [(0, d, d - 1, 0) for d in (1, 2, 3, 4, 5, 6, 7)]
    + [(0, 9, 4, 2), (0, 8, 5, 3), (0, 10, 6, 1)]
    + [(1, d, d + 6, 0) for d in (1, 2, 3, 4, 5, 6)]
    + [(1, 7, 11, 3), (1, 8, 12, 2), (1, 9, 10, 1)]
)
LOW = [(0, 1, 0, 0), (0, 7, 0, 1), (0, 2, 1, 0), (0, 6, 1, 2), (0, 3, 2, 0), (0, 5, 2, 3), (0, 4, 3, 0)]
LOW += [(1, 5, 3, 1), (1, 1, 4, 0), (1, 3, 4, 3), (1, 2, 5, 0), (1, 4, 5, 2)]
HIGH_TILES, LOW_TILES = 13, 6


def turn(v, by):
    return v if by == 0 else pltpu.roll(v, by % 8, 0)


def corner_kernel(y0, y1, high, low):
    oy = odd("gy")
    at0 = pl.multiple_of((1 - oy) * 8, 8)
    at1 = pl.multiple_of(oy * 8, 8)
    row = lax.broadcasted_iota(jnp.int32, (8, NZ), 0)
    for pack, corners, count, side in ((high, HIGH, HIGH_TILES, 1), (low, LOW, LOW_TILES, 0)):
        for y, at, above in ((y0, at0, 1 - oy), (y1, at1, oy)):
            tiles = {}
            for field, d, t, by in corners:
                v = y[field * NX + (NX - d if side else d - 1)]
                if by == 0:
                    tiles[t] = v
                else:
                    under = jnp.where(row < by, turn(v, by), tiles[t])
                    over = jnp.where(row >= 8 - by, turn(v, -by), tiles[t])
                    tiles[t] = jnp.where(above == 1, over, under)
            for t in range(count):
                pack[t, pl.ds(at, 8), :] = tiles[t]


X0, Y0 = 9, 16
X1, Y1 = 5, 16
X2, Y2 = 6, 16


def levels_down(c, b, fx, fy, fz, w, c1, b1, gx_, gy_, gz_, gw_):
    top = Level(0, c, b, fx, fy, fz, w, 8, 88)
    return top, Level(1, c1, b1, gx_, gy_, gz_, gw_, 8, 56)


def inner_kernel(cond, source, y0, y1, c, b, fx, fy, fz, w, ua, ub, c1, b1, gx_, gy_, gz_, gw_, tmp):
    oy = odd("gy")
    at0 = pl.multiple_of(8 + (1 - oy) * (NY + 8), 8)
    at1 = pl.multiple_of(8 + oy * (NY + 8), 8)

    def own(x):
        c[1 + x, pl.ds(Y0, NY), :] = cond[x]
        c[1 + x, pl.ds(at0, 8), :] = y0[x]
        c[1 + x, pl.ds(at1, 8), :] = y1[x]
        b[1 + x, pl.ds(Y0, NY), :] = source[x]
        b[1 + x, pl.ds(at0, 8), :] = y0[NX + x]
        b[1 + x, pl.ds(at1, 8), :] = y1[NX + x]

    rows(0, NX, own)
    top, mid = levels_down(c, b, fx, fy, fz, w, c1, b1, gx_, gy_, gz_, gw_)
    top.faces(1, 17)
    top.weights(2, 16, ua)
    top.sweep(ua, ub, 3, 15)
    top.restrict_c(tmp, c1, 0, 8, 1, 1)
    top.restrict(ub, tmp, b1, 2, 6, 1, 1)
    mid.faces(1, 9)
    mid.weights(2, 8)


def down_kernel(
    x0, x1, k0, k1, c_in, b_in, fx_in, fy_in, fz_in, w_in, ua_in, ub_in, c1_in, b1_in, gx_in, gy_in, gz_in, gw_in,
    fx, fy, fz, w, b, ub, gx_, gy_, gz_, gw_, b1, u1, c2, b2, ypack0, ypack1,
    c, ua, c1, ga_, tmp, ctmp, tmp1,
):
    oy = odd("gy")
    here, here1 = pl.ds(8, 80), pl.ds(8, 48)
    sides = ((x0, k0, HIGH, HIGH_C, HIGH_B, X0 + NX - 1, 1), (x1, k1, LOW, LOW_C, LOW_B, X0, -1))
    for x, pack, corners, nc, nb, edge, sign in sides:
        for d in range(1, nc + 1):
            c[edge + sign * d, pl.ds(Y0, NY), :] = x[d - 1]
        for d in range(1, nb + 1):
            b[edge + sign * d, pl.ds(Y0, NY), :] = x[nc + d - 1]
        for field, d, t, by in corners:
            ref = (c, b)[field]
            ref[edge + sign * d, pl.ds(8, 8), :] = turn(pack[t, pl.ds(0, 8), :], -by)
            ref[edge + sign * d, pl.ds(80, 8), :] = turn(pack[t, pl.ds(8, 8), :], by)
    for x in (1, 16):
        c[x + 8, here, :] = c_in[x, here, :]
    for x in (2, 3, 14, 15):
        ua[x + 8, here, :] = ua_in[x, here, :]

    def fill(x):
        for ref, src in ((fx, fx_in), (fy, fy_in), (fz, fz_in), (w, w_in), (b, b_in), (ub, ub_in)):
            ref[x + 8, here, :] = src[x, here, :]

    rows(1, 17, fill)
    for x in range(1, 9):
        c1[x + 4, here1, :] = c1_in[x, here1, :]
        for ref, src in ((gx_, gx_in), (gy_, gy_in), (gz_, gz_in), (gw_, gw_in), (b1, b1_in)):
            ref[x + 4, here1, :] = src[x, here1, :]

    top, mid = levels_down(c, b, fx, fy, fz, w, c1, b1, gx_, gy_, gz_, gw_)
    top.faces(2, 9)
    top.faces(24, 35)
    top.weights(3, 10, ua)
    top.weights(24, 35, ua)
    top.sweep(ua, ub, 4, 11)
    top.sweep(ua, ub, 23, 34)
    top.restrict_c(ctmp, c1, 0, 4, 1, 1)
    top.restrict_c(ctmp, c1, 12, 17, 1, 1)
    top.restrict(ub, tmp, b1, 0, 4, 5, 3)
    top.restrict(ub, tmp, b1, 8, 14, 5, 3)

    mid.faces(1, 5)
    mid.faces(12, 17)
    mid.weights(2, 6)
    mid.weights(12, 17)
    mid.start(ga_, 3, 17)
    mid.sweep(ga_, u1, 4, 16)
    mid.restrict(u1, tmp1, b2, 0, 5, 5, X2)
    mid.restrict_c(tmp1, c2, 0, 8, 1, X2 - 2)

    e0 = Y1 + (1 - oy) * 28
    e1 = Y1 + oy * 28
    f0 = pl.multiple_of(Y2 + (1 - oy) * 8, 8)
    f1 = pl.multiple_of(Y2 + oy * 8, 8)
    for pack, e, f in ((ypack0, e0, f0), (ypack1, e1, f1)):
        for k in range(4):
            x = X1 + 2 * k
            pack[k, pl.ds(0, 4), :] = pack_lanes([u1[x + j, pl.ds(e, 4), :] for j in range(2)])
            pack[k, pl.ds(4, 4), :] = pack_lanes([b1[x + j, pl.ds(e, 4), :] for j in range(2)])
        for k in range(2):
            pack[4 + k] = pack_lanes([b2[X2 + min(4 * k + j, 4), pl.ds(f, 8), :] for j in range(4)])
            pack[6 + k] = pack_lanes([c2[X2 - 2 + 4 * k + j, pl.ds(f, 8), :] for j in range(4)])


def set_y1(ref, y0, y1, oy, part):
    a0 = Y1 - 4 + (1 - oy) * 36
    a1 = Y1 - 4 + oy * 36
    for y, a in ((y0, a0), (y1, a1)):
        for k in range(4):
            for j, v in enumerate(unpack_lanes(y[k], 2)):
                ref[X1 + 2 * k + j, pl.ds(a, 4), :] = v[4 * part : 4 * part + 4]


def set_y2(c2, b2, y0, y1, oy):
    a0 = pl.multiple_of(Y2 - 8 + (1 - oy) * 24, 8)
    a1 = pl.multiple_of(Y2 - 8 + oy * 24, 8)
    for y, a in ((y0, a0), (y1, a1)):
        for k in range(2):
            for j, v in enumerate(unpack_lanes(y[4 + k], 4)):
                if 4 * k + j < 5:
                    b2[X2 + 4 * k + j, pl.ds(a, 8), :] = v
            for j, v in enumerate(unpack_lanes(y[6 + k], 4)):
                c2[X2 - 2 + 4 * k + j, pl.ds(a, 8), :] = v


def copy_rows(pairs, lo, hi):
    def body(x):
        for src, dst in pairs:
            dst[x] = src[x]

    rows(lo, hi, body)


def edge2_kernel(u1_in, b1_in, c2_in, b2_in, y0, y1, high, low, u1, b1, c2, b2):
    oy = odd("gy")
    copy_rows([(u1_in, u1), (b1_in, b1)], X1, X1 + 8)
    copy_rows([(c2_in, c2)], X2 - 2, X2 + 6)
    copy_rows([(b2_in, b2)], X2, X2 + 5)
    set_y1(u1, y0, y1, oy, 0)
    set_y1(b1, y0, y1, oy, 1)
    set_y2(c2, b2, y0, y1, oy)
    for pack, edge1, edge2, sign in ((high, X1 + 7, X2 + 3, -1), (low, X1, X2, 1)):
        for k in range(2):
            t = [u1[edge1 + sign * (2 * k + j), pl.ds(12, 40), :] for j in range(2)]
            pack[pl.ds(k * 40, 40), :] = pack_lanes(t)
        t = [c2[edge2 + sign * d, pl.ds(8, 32), :] for d in range(6)]
        t += [b2[edge2 + sign * d, pl.ds(8, 32), :] for d in range(5 if sign == 1 else 4)]
        t += t[:1] * (12 - len(t))
        for k in range(3):
            pack[pl.ds(80 + k * 32, 32), :] = pack_lanes(t[4 * k : 4 * k + 4])
        t = [b1[edge1 + sign * j, pl.ds(12, 40), :] for j in range(2)]
        pack[pl.ds(176, 40), :] = pack_lanes(t)
        t = [b1[edge1 + sign * 2, pl.ds(16 + 16 * j, 16), :] for j in range(2)]
        pack[pl.ds(216, 16), :] = pack_lanes(t)


def one_hot(shape, f):
    i = lax.broadcasted_iota(jnp.int32, shape, 0)
    j = lax.broadcasted_iota(jnp.int32, shape, 1)
    return jnp.where(f(i, j), 1.0, 0.0).astype(F32)


def exact_dot(a, b):
    return jnp.dot(a, b, precision=lax.Precision.HIGHEST, preferred_element_type=F32)


def level2_kernel(
    u1_in, c2_in, b2_in, y0, y1, x0, x1, far,
    fx, fy, fz, w, b2, u2, u1, gather,
    c2, ua, tmp, b3, c3,
):
    ox, oy = odd("gx"), odd("gy")
    copy_rows([(u1_in, u1)], X1, X1 + 8)
    copy_rows([(c2_in, c2)], X2 - 2, X2 + 6)
    copy_rows([(b2_in, b2)], X2, X2 + 5)
    set_y1(u1, y0, y1, oy, 0)
    set_y2(c2, b2, y0, y1, oy)
    for pack, edge1, edge2, sign in ((x0, X1 + 7, X2 + 3, 1), (x1, X1, X2, -1)):
        for k in range(2):
            for j, v in enumerate(unpack_lanes(pack[pl.ds(k * 40, 40), :], 2)):
                u1[edge1 + sign * (2 * k + j + 1), pl.ds(12, 40), :] = v
        t = []
        for k in range(3):
            t += unpack_lanes(pack[pl.ds(80 + k * 32, 32), :], 4)
        for d in range(6):
            c2[edge2 + sign * (d + 1), pl.ds(8, 32), :] = t[d]
        for d in range(5 if sign == -1 else 4):
            b2[edge2 + sign * (d + 1), pl.ds(8, 32), :] = t[6 + d]
    b2[X2 + 8, pl.ds(8, 32), :] = unpack_lanes(far[pl.ds(112, 32), :], 4)[2]

    low = Level(2, c2, b2, fx, fy, fz, w, 8, 40)
    low.faces(0, 15)
    low.weights(1, 15, ua)
    low.sweep(ua, u2, 2, 14)
    low.restrict(u2, tmp, b3, 0, 2, X2, 0)
    low.restrict_c(tmp, c3, 0, 2, X2, 0)
    both = jnp.concatenate(
        [b3[0, pl.ds(16, 8), :], b3[1, pl.ds(16, 8), :], c3[0, pl.ds(16, 8), :], c3[1, pl.ds(16, 8), :]], 0
    )
    spread = exact_dot(both, one_hot((NZ, NZ), lambda i, j: i == 8 * (j % 16)))
    shape = (8, NZ)
    mine = lane(shape) // 16 == lax.broadcasted_iota(jnp.int32, shape, 0)
    packed = [
        jnp.sum(jnp.where(mine, spread[8 * k : 8 * k + 8], 0.0), axis=0, keepdims=True) for k in range(4)
    ]
    packed = [jnp.where(ox == 1, packed[k ^ 1], packed[k]) for k in range(4)]
    eight = jnp.concatenate(packed + packed, 0)

    def body(k):
        gather[pl.ds(pl.multiple_of(8 * k, 8), 8), :] = eight

    rows(0, 64, body, 8)


class Whole:
    def __init__(self, depth, b, c):
        self.h = H0 * 4.0**depth
        self.s = 2 ** (depth - 3)
        self.st = 16 * self.s
        self.b = b
        n = c.shape[0]
        sub = lax.broadcasted_iota(jnp.int32, (1,) + c.shape[1:], 2)
        up = self.xp(c)
        end = jnp.where(sub == 7, 0.0, up[n - 1 :])
        up = jnp.concatenate([up[: n - 1], end], 0) if n > 1 else end
        self.fxp = harmonic(c, up)
        up = self.yp(c)
        last = up[:, 3:]
        last = jnp.where(lane(last.shape) >= 128 - self.st, 0.0, last)
        self.fyp = harmonic(c, jnp.concatenate([up[:, :3], last], 1))
        self.fzp = harmonic(c, self.zp(c))
        self.fxm, self.fym, self.fzm = self.xm(self.fxp), self.ym(self.fyp), self.zm(self.fzp)
        d = self.h + self.fxp + self.fxm + self.fyp + self.fym + self.fzp + self.fzm
        self.w = DAMP * recip(d)

    def xp(self, v):
        wrap = pltpu.roll(v[:1], 7, 2)
        return jnp.concatenate([v[1:], wrap], 0) if v.shape[0] > 1 else wrap

    def xm(self, v):
        n = v.shape[0]
        wrap = pltpu.roll(v[n - 1 :], 1, 2)
        return jnp.concatenate([wrap, v[: n - 1]], 0) if n > 1 else wrap

    def yp(self, v):
        w = v if self.st == 128 else lroll(v, -self.st)
        far = jnp.concatenate([w[:, 1:], w[:, :1]], 1)
        return far if self.st == 128 else jnp.where(lane(v.shape) < 128 - self.st, w, far)

    def ym(self, v):
        w = v if self.st == 128 else lroll(v, self.st)
        far = jnp.concatenate([w[:, 3:], w[:, :3]], 1)
        return far if self.st == 128 else jnp.where(lane(v.shape) >= self.st, w, far)

    def zp(self, v):
        s = self.s
        return jnp.where(lane(v.shape) % 16 < 16 - s, lroll(v, -s), lroll(v, 16 - s))

    def zm(self, v):
        s = self.s
        return self.zp(v) if s == 8 else jnp.where(lane(v.shape) % 16 >= s, lroll(v, s), lroll(v, s - 16))

    def flux(self, v):
        acc = self.fxp * self.xp(v) + self.fxm * self.xm(v)
        acc = acc + self.fyp * self.yp(v) + self.fym * self.ym(v)
        return acc + self.fzp * self.zp(v) + self.fzm * self.zm(v)

    def sweep(self, v):
        return KEEP * v + self.w * (self.b + self.flux(v))

    def residual(self, v):
        r = self.b - self.h * v
        r = r + self.fxp * (self.xp(v) - v) + self.fxm * (self.xm(v) - v)
        r = r + self.fyp * (self.yp(v) - v) + self.fym * (self.ym(v) - v)
        return r + self.fzp * (self.zp(v) - v) + self.fzm * (self.zm(v) - v)

    def coarse(self, v, scale):
        v = jnp.concatenate([v[2 * k : 2 * k + 1] + v[2 * k + 1 : 2 * k + 2] for k in range(v.shape[0] // 2)], 0)
        return scale * pair_lanes(pair_lanes(v, self.s), self.st)


def whole_cycle(depth, b, c):
    level = Whole(depth, b, c)
    v = level.w * b
    if depth == 6:
        for _ in range(SWEEPS_COARSE - 1):
            v = level.sweep(v)
        return v
    v = level.sweep(v)
    below = whole_cycle(depth + 1, level.coarse(level.residual(v), 0.5), level.coarse(c, 0.125))
    v = v + jnp.concatenate([below[k // 2 : k // 2 + 1] for k in range(v.shape[0])], 0)
    return level.sweep(level.sweep(v))


def up_kernel(
    gather, y0, y1, x1,
    hx, hy, hz, hw, b2, u2,
    gx_, gy_, gz_, gw_, b1_in, u1,
    fx, fy, fz, w, b, u0,
    out, res,
    s3, e2, e1, e0, ha, hb, b1, ga_, gb_, ua, ub,
):
    ix, iy = lax.axis_index("gx"), lax.axis_index("gy")
    ox, oy = ix % 2, iy % 2

    def field(k):
        return jnp.stack(
            [
                jnp.stack([gather[pl.ds(xq * 16 + g * 4 + k + xl, 8, stride=64), :] for g in range(4)], 0)
                for xq in range(4)
                for xl in range(2)
            ],
            0,
        )

    u3 = whole_cycle(3, field(0), field(2))
    s3[...] = jnp.zeros(s3.shape, F32)
    for xlo in range(8):
        for g in range(4):
            s3[g + 1, pl.ds(8 + xlo, 8, stride=8), :] = u3[xlo, g]
    shape = (8, NZ)
    mine = lane(shape) // 16 == lax.broadcasted_iota(jnp.int32, shape, 0)
    tiles = []
    for k in range(6):
        for g in range(3):
            row = s3[iy + g, pl.ds(2 * ix + 6 + 5 * ox + (1 - 2 * ox) * k, 1), :]
            tiles.append(jnp.where(mine, jnp.broadcast_to(row, shape), 0.0))
    spread = exact_dot(jnp.concatenate(tiles, 0), one_hot((NZ, NZ), lambda i, j: i % 16 == j // 8))
    for k in range(6):
        t = spread[24 * k : 24 * k + 24]
        e2[k, pl.ds(0, 24, stride=2), :] = t
        e2[k, pl.ds(1, 24, stride=2), :] = t

    for x in range(2, 14):
        ha[x] = u2[x] + e2[(x - 2) // 2]
    low = Level(2, None, b2, hx, hy, hz, hw, 8, 40)
    low.sweep(ha, hb, 3, 13)
    low.sweep(hb, ha, 4, 12)

    def grow1(k):
        t = ha[4 + k, pl.ds(8, 32), :]
        e1[k, pl.ds(0, 32, stride=2), :] = t
        e1[k, pl.ds(1, 32, stride=2), :] = t

    rows(0, 8, grow1)

    copy_rows([(b1_in, b1)], 3, 17)
    set_y1(b1, y0, y1, oy, 1)
    for j, v in enumerate(unpack_lanes(x1[pl.ds(176, 40), :], 2)):
        b1[X1 - 1 - j, pl.ds(12, 40), :] = v
    for j, v in enumerate(unpack_lanes(x1[pl.ds(216, 16), :], 2)):
        b1[X1 - 3, pl.ds(16 + 16 * j, 16), :] = v

    def add1(k):
        for j in range(2):
            ga_[1 + 2 * k + j] = u1[1 + 2 * k + j] + e1[k]

    rows(0, 8, add1)
    mid = Level(1, None, b1, gx_, gy_, gz_, gw_, 8, 56)
    mid.sweep(ga_, gb_, 2, 16)
    mid.sweep(gb_, ga_, 3, 15)

    def grow0(k):
        t = ga_[3 + k, pl.ds(8, 48), :]
        e0[k, pl.ds(0, 48, stride=2), :] = t
        e0[k, pl.ds(1, 48, stride=2), :] = t

    def add0(k):
        for j in range(2):
            ua[5 + 2 * k + j] = u0[5 + 2 * k + j] + e0[k]

    rows(0, 12, grow0, 4)
    rows(0, 12, add0, 4)
    top = Level(0, None, b, fx, fy, fz, w, 8, 88)
    top.sweep(ua, ub, 7, 27)
    top.sweep(ub, ua, 8, 26)

    def finish(x):
        to = stored(x)
        out[to] = ua[X0 + x, pl.ds(Y0, NY), :]
        res[to] = top.residual(ua, X0 + x, Y0, NY)

    rows(0, NX, finish)


def swaps(axis, first, second=None):
    count = lax.axis_size(axis)

    def pairs(start):
        return [p for i in range(start, count - 1, 2) for p in ((i, i + 1), (i + 1, i))]

    if second is None:
        return lax.ppermute(first, axis, pairs(0))
    late = lax.ppermute(second, axis, pairs(1))
    return lax.ppermute(first, axis, pairs(0)), late


def per_device(source, density, drag, porous_rows):
    sems = [pltpu.SemaphoreType.DMA((3, PARTS)), pltpu.SemaphoreType.DMA]
    block = (NX, NY, NZ)
    cond, source, p0, p1 = call(
        begin_kernel,
        [block, block, (32, 8, NZ), (32, 8, NZ)],
        [block] * 3 + [pltpu.VMEM((NY,), jnp.int32)] + sems,
        (source, density, drag, porous_rows),
        "begin",
        16,
        4,
    )
    y0, y1 = swaps("gy", p0, p1)
    q0, q1 = call(edge_kernel, [(HIGH_C + HIGH_B, NY, NZ), (LOW_C + LOW_B, NY, NZ)], [], (cond, source), "edges", 16, 0, 10**9)
    x0, x1 = swaps("gx", q0, q1)
    p0, p1 = call(corner_kernel, [(HIGH_TILES, 16, NZ), (LOW_TILES, 16, NZ)], [], (y0, y1), "corners", 16)
    k0, k1 = swaps("gx", p0, p1)
    zero, one, two = (36, 96, NZ), (18, 64, NZ), (16, 48, NZ)
    small, small1 = (18, 96, NZ), (10, 64, NZ)
    inner = call(
        inner_kernel, [small] * 8 + [small1] * 6, [(8, 96, NZ)], (cond, source, y0, y1), "inner", 16, 0, 10**10
    )
    down = call(
        down_kernel,
        [zero] * 6 + [one] * 6 + [two] * 2 + [(8, 8, NZ)] * 2,
        [zero] * 2 + [one] * 2 + [(14, 96, NZ), (17, 96, NZ), (8, 64, NZ)],
        (x0, x1, k0, k1, *inner),
        "down",
        24,
    )
    level0, level1 = down[:6], down[6:12]
    u1, c2, b2, p0, p1 = down[11:]
    y0, y1 = swaps("gy", p0, p1)
    p0, p1 = call(edge2_kernel, [(232, NZ)] * 2, [one, one, two, two], (u1, level1[4], c2, b2, y0, y1), "edges2", 16)
    x0, x1 = swaps("gx", p0, p1)
    far = swaps("gx", x1)
    *level2, u1, packed = call(
        level2_kernel,
        [two] * 6 + [one, (512, NZ)],
        [two] * 2 + [(2, 48, NZ)] * 3,
        (u1, c2, b2, y0, y1, x0, x1, far),
        "level2",
        16,
    )
    whole = lax.all_to_all(packed, ("gx", "gy"), 0, 0, tiled=True)
    out, res = call(
        up_kernel,
        [block] * 2,
        [(6, 80, NZ), (6, 48, NZ), (8, 64, NZ), (12, 96, NZ)] + [two] * 2 + [one] * 3 + [zero] * 2,
        (whole, y0, y1, x1, *level2, *level1[:5], u1, *level0),
        "up",
        24,
    )
    return out, res


def solution(mesh):
    return jax.shard_map(
        per_device,
        mesh=mesh,
        in_specs=(P("gx", "gy", None), P("gx", "gy", None), P("gx", "gy", None), P("gy")),
        out_specs=(P("gx", "gy", None), P("gx", "gy", None)),
        check_vma=False,
    )
```

```python
import functools

import jax
import jax.numpy as jnp
from jax import lax
from jax.experimental import pallas as pl
from jax.experimental.pallas import tpu as pltpu
from jax.sharding import PartitionSpec as P

SWEEPS_COARSE = 16
DAMP = 0.8
KEEP = 1.0 - DAMP
H0 = 0.0002

NX, NY, NZ = 16, 64, 128
F32 = jnp.float32
VMEM = pl.BlockSpec(memory_space=pltpu.VMEM)
HBM = pl.BlockSpec(memory_space=pltpu.HBM)


def call(body, outs, scratch, args, name, vmem, hbm=0, cost=0):
    args = [pltpu.with_memory_space_constraint(a, pltpu.HBM) for a in args[:hbm]] + list(args[hbm:])
    return pl.pallas_call(
        body,
        out_shape=[jax.ShapeDtypeStruct(s, F32) for s in outs],
        in_specs=[HBM] * hbm + [VMEM] * (len(args) - hbm),
        out_specs=[VMEM] * len(outs),
        scratch_shapes=[pltpu.VMEM(s, F32) if isinstance(s, tuple) else s for s in scratch],
        compiler_params=pltpu.CompilerParams(vmem_limit_bytes=vmem * 2**20),
        name=name,
        cost_estimate=pl.CostEstimate(flops=cost, bytes_accessed=0, transcendentals=0) if cost else None,
    )(*args)


def recip(t):
    return 1.0 / t


def harmonic(a, b):
    return (2.0 * a) * b / jnp.maximum(a + b, 1e-30)


def lane(shape):
    return lax.broadcasted_iota(jnp.int32, shape, len(shape) - 1)


def lroll(v, shift):
    return pltpu.roll(v, shift % 128, v.ndim - 1)


def pair_lanes(v, s):
    first = (lane(v.shape) // s) % 2 == 0
    return v + jnp.where(first, lroll(v, -s), lroll(v, s))


def pack_lanes(tiles):
    n = len(tiles)
    out = tiles[0]
    for k in range(1, n):
        out = jnp.where(lane(out.shape) % n == k, tiles[k], out)
    return out


def unpack_lanes(p, n):
    at = lane(p.shape) % n
    moved = {d: p if d == 0 else lroll(p, -d) for d in range(1 - n, n)}
    tiles = []
    for k in range(n):
        out = moved[k]
        for m in range(1, n):
            out = jnp.where(at == m, moved[k - m], out)
        tiles.append(out)
    return tiles


def rows(lo, hi, body, unroll=8):
    whole = (hi - lo) // unroll

    def step(k, carry):
        for j in range(unroll):
            body(lo + k * unroll + j)
        return carry

    if whole > 1:
        lax.fori_loop(0, whole, step, 0)
        lo = lo + whole * unroll
    for x in range(lo, hi):
        body(x)


class Level:
    def __init__(self, depth, c, b, fx, fy, fz, w, ys, ye):
        self.h = H0 * 4.0**depth
        self.s = 2**depth
        self.c, self.b, self.fx, self.fy, self.fz, self.w = c, b, fx, fy, fz, w
        self.ys, self.n = ys, ye - ys

    def faces(self, lo, hi):
        here, above = pl.ds(self.ys, self.n), pl.ds(self.ys + 1, self.n)

        def body(x):
            c = self.c[x, here, :]
            twice, safe = c + c, c + 1e-30

            def face(other):
                return twice * other / (safe + other)

            self.fx[x, here, :] = face(self.c[x + 1, here, :])
            self.fy[x, here, :] = face(self.c[x, above, :])
            self.fz[x, here, :] = face(lroll(c, -self.s))

        rows(lo, hi, body)

    def weights(self, lo, hi, start=None):
        here, below = pl.ds(self.ys, self.n), pl.ds(self.ys - 1, self.n)

        def body(x):
            fz = self.fz[x, here, :]
            d = self.fx[x, here, :] + self.fx[x - 1, here, :]
            d = d + (self.fy[x, here, :] + self.fy[x, below, :])
            d = d + (fz + lroll(fz, self.s))
            w = DAMP * recip(self.h + d)
            self.w[x, here, :] = w
            if start is not None:
                start[x, here, :] = w * self.b[x, here, :]

        rows(lo, hi, body)

    def start(self, out, lo, hi):
        here = pl.ds(self.ys, self.n)

        def body(x):
            out[x, here, :] = self.w[x, here, :] * self.b[x, here, :]

        rows(lo, hi, body)

    def sweep(self, u, out, lo, hi):
        here = pl.ds(self.ys, self.n)
        above, below = pl.ds(self.ys + 1, self.n), pl.ds(self.ys - 1, self.n)

        def body(x):
            v = u[x, here, :]
            fz = self.fz[x, here, :]
            acc = fz * lroll(v, -self.s) + lroll(fz * v, self.s)
            acc = acc + (self.fx[x, here, :] * u[x + 1, here, :] + self.fx[x - 1, here, :] * u[x - 1, here, :])
            acc = acc + (self.fy[x, here, :] * u[x, above, :] + self.fy[x, below, :] * u[x, below, :])
            out[x, here, :] = KEEP * v + self.w[x, here, :] * (self.b[x, here, :] + acc)

        rows(lo, hi, body)

    def residual(self, u, x, y, n):
        here, above, below = pl.ds(y, n), pl.ds(y + 1, n), pl.ds(y - 1, n)
        v = u[x, here, :]
        flow = self.fz[x, here, :] * (lroll(v, -self.s) - v)
        r = self.b[x, here, :] - self.h * v
        r = r + (flow - lroll(flow, self.s))
        r = r + self.fx[x, here, :] * (u[x + 1, here, :] - v)
        r = r + self.fx[x - 1, here, :] * (u[x - 1, here, :] - v)
        r = r + self.fy[x, here, :] * (u[x, above, :] - v)
        return r + self.fy[x, below, :] * (u[x, below, :] - v)

    def halve(self, tmp, out, lo, hi, x_to, scale):
        half = tmp.shape[1] // 2

        def body(k):
            t = tmp[k, pl.ds(0, half, stride=2), :] + tmp[k, pl.ds(1, half, stride=2), :]
            out[x_to + k, pl.ds(8, half), :] = scale * pair_lanes(t, self.s)

        rows(lo, hi, body)

    def restrict(self, u, tmp, out, lo, hi, x_from, x_to):
        def body(k):
            x = x_from + 2 * k
            both = self.residual(u, x, self.ys, self.n) + self.residual(u, x + 1, self.ys, self.n)
            tmp[k, pl.ds(self.ys, self.n), :] = both

        rows(lo, hi, body, 4)
        self.halve(tmp, out, lo, hi, x_to, 0.5)

    def restrict_c(self, tmp, out, lo, hi, x_from, x_to):
        def body(k):
            x = x_from + 2 * k
            tmp[k] = self.c[x] + self.c[x + 1]

        rows(lo, hi, body)
        self.halve(tmp, out, lo, hi, x_to, 0.125)


def odd(axis):
    return lax.axis_index(axis) % 2


PARTS = 4


def stored(x):
    o = odd("gx")
    return o * (NX - 1) + (1 - 2 * o) * x


def begin_kernel(source, density, drag, porous, cond, rhs, ypack0, ypack1, dens, dra, src, por, sem, psem):
    o = odd("gy")
    at0 = pl.multiple_of((1 - o) * (NY - 8), 8)
    at1 = pl.multiple_of(o * (NY - 8), 8)
    part = NX // PARTS
    loads = []
    first = pltpu.make_async_copy(porous, por, psem)
    first.start()
    for k in range(PARTS):
        here = pl.ds(k * part, part)
        for j, (ref, dst) in enumerate(((density, dens), (drag, dra), (source, src))):
            loads.append(pltpu.make_async_copy(ref.at[here], dst.at[here], sem.at[j, k]))
            loads[-1].start()
    first.wait()
    line = jnp.broadcast_to(por[...].astype(F32)[None], (NY, NY))
    same = lax.broadcasted_iota(jnp.int32, (NY, NY), 0) == lax.broadcasted_iota(jnp.int32, (NY, NY), 1)
    mask = jnp.broadcast_to(jnp.sum(jnp.where(same, line, 0.0), axis=1, keepdims=True), (NY, NZ))
    for k in range(PARTS):
        for load in loads[3 * k : 3 * k + 3]:
            load.wait()
        for x in range(k * part, k * part + part):
            to = stored(x)
            cond[to] = recip(dens[x] * (1.0 + dra[x] * mask))
            rhs[to] = src[x]
            for pack, at in ((ypack0, at0), (ypack1, at1)):
                pack[to] = cond[to, pl.ds(at, 8), :]
                pack[NX + to] = src[x, pl.ds(at, 8), :]


HIGH_C, HIGH_B, LOW_C, LOW_B = 11, 10, 8, 6


def edge_kernel(cond, source, high, low):
    for d in range(HIGH_C):
        high[d] = cond[NX - 1 - d]
    for d in range(HIGH_B):
        high[HIGH_C + d] = source[NX - 1 - d]
    for d in range(LOW_C):
        low[d] = cond[d]
    for d in range(LOW_B):
        low[LOW_C + d] = source[d]


HIGH = (
    [(0, d, d - 1, 0) for d in (1, 2, 3, 4, 5, 6, 7)]
    + [(0, 9, 4, 2), (0, 8, 5, 3), (0, 10, 6, 1)]
    + [(1, d, d + 6, 0) for d in (1, 2, 3, 4, 5, 6)]
    + [(1, 7, 11, 3), (1, 8, 12, 2), (1, 9, 10, 1)]
)
LOW = [(0, 1, 0, 0), (0, 7, 0, 1), (0, 2, 1, 0), (0, 6, 1, 2), (0, 3, 2, 0), (0, 5, 2, 3), (0, 4, 3, 0)]
LOW += [(1, 5, 3, 1), (1, 1, 4, 0), (1, 3, 4, 3), (1, 2, 5, 0), (1, 4, 5, 2)]
HIGH_TILES, LOW_TILES = 13, 6


def turn(v, by):
    return v if by == 0 else pltpu.roll(v, by % 8, 0)


def corner_kernel(y0, y1, high, low):
    oy = odd("gy")
    at0 = pl.multiple_of((1 - oy) * 8, 8)
    at1 = pl.multiple_of(oy * 8, 8)
    row = lax.broadcasted_iota(jnp.int32, (8, NZ), 0)
    for pack, corners, count, side in ((high, HIGH, HIGH_TILES, 1), (low, LOW, LOW_TILES, 0)):
        for y, at, above in ((y0, at0, 1 - oy), (y1, at1, oy)):
            tiles = {}
            for field, d, t, by in corners:
                v = y[field * NX + (NX - d if side else d - 1)]
                if by == 0:
                    tiles[t] = v
                else:
                    under = jnp.where(row < by, turn(v, by), tiles[t])
                    over = jnp.where(row >= 8 - by, turn(v, -by), tiles[t])
                    tiles[t] = jnp.where(above == 1, over, under)
            for t in range(count):
                pack[t, pl.ds(at, 8), :] = tiles[t]


X0, Y0 = 9, 16
X1, Y1 = 5, 16
X2, Y2 = 6, 16


def levels_down(c, b, fx, fy, fz, w, c1, b1, gx_, gy_, gz_, gw_):
    top = Level(0, c, b, fx, fy, fz, w, 8, 88)
    return top, Level(1, c1, b1, gx_, gy_, gz_, gw_, 8, 56)


def inner_kernel(cond, source, y0, y1, c, b, fx, fy, fz, w, ua, ub, c1, b1, gx_, gy_, gz_, gw_, tmp):
    oy = odd("gy")
    at0 = pl.multiple_of(8 + (1 - oy) * (NY + 8), 8)
    at1 = pl.multiple_of(8 + oy * (NY + 8), 8)

    def own(x):
        c[1 + x, pl.ds(Y0, NY), :] = cond[x]
        c[1 + x, pl.ds(at0, 8), :] = y0[x]
        c[1 + x, pl.ds(at1, 8), :] = y1[x]
        b[1 + x, pl.ds(Y0, NY), :] = source[x]
        b[1 + x, pl.ds(at0, 8), :] = y0[NX + x]
        b[1 + x, pl.ds(at1, 8), :] = y1[NX + x]

    rows(0, NX, own)
    top, mid = levels_down(c, b, fx, fy, fz, w, c1, b1, gx_, gy_, gz_, gw_)
    top.faces(1, 17)
    top.weights(2, 16, ua)
    top.sweep(ua, ub, 3, 15)
    top.restrict_c(tmp, c1, 0, 8, 1, 1)
    top.restrict(ub, tmp, b1, 2, 6, 1, 1)
    mid.faces(1, 9)
    mid.weights(2, 8)


def down_kernel(
    x0, x1, k0, k1, c_in, b_in, fx_in, fy_in, fz_in, w_in, ua_in, ub_in, c1_in, b1_in, gx_in, gy_in, gz_in, gw_in,
    fx, fy, fz, w, b, ub, gx_, gy_, gz_, gw_, b1, u1, c2, b2, ypack0, ypack1,
    c, ua, c1, ga_, tmp, ctmp, tmp1,
):
    oy = odd("gy")
    here, here1 = pl.ds(8, 80), pl.ds(8, 48)
    sides = ((x0, k0, HIGH, HIGH_C, HIGH_B, X0 + NX - 1, 1), (x1, k1, LOW, LOW_C, LOW_B, X0, -1))
    for x, pack, corners, nc, nb, edge, sign in sides:
        for d in range(1, nc + 1):
            c[edge + sign * d, pl.ds(Y0, NY), :] = x[d - 1]
        for d in range(1, nb + 1):
            b[edge + sign * d, pl.ds(Y0, NY), :] = x[nc + d - 1]
        for field, d, t, by in corners:
            ref = (c, b)[field]
            ref[edge + sign * d, pl.ds(8, 8), :] = turn(pack[t, pl.ds(0, 8), :], -by)
            ref[edge + sign * d, pl.ds(80, 8), :] = turn(pack[t, pl.ds(8, 8), :], by)
    for x in (1, 16):
        c[x + 8, here, :] = c_in[x, here, :]
    for x in (2, 3, 14, 15):
        ua[x + 8, here, :] = ua_in[x, here, :]

    def fill(x):
        for ref, src in ((fx, fx_in), (fy, fy_in), (fz, fz_in), (w, w_in), (b, b_in), (ub, ub_in)):
            ref[x + 8, here, :] = src[x, here, :]

    rows(1, 17, fill)
    for x in range(1, 9):
        c1[x + 4, here1, :] = c1_in[x, here1, :]
        for ref, src in ((gx_, gx_in), (gy_, gy_in), (gz_, gz_in), (gw_, gw_in), (b1, b1_in)):
            ref[x + 4, here1, :] = src[x, here1, :]

    top, mid = levels_down(c, b, fx, fy, fz, w, c1, b1, gx_, gy_, gz_, gw_)
    top.faces(2, 9)
    top.faces(24, 35)
    top.weights(3, 10, ua)
    top.weights(24, 35, ua)
    top.sweep(ua, ub, 4, 11)
    top.sweep(ua, ub, 23, 34)
    top.restrict_c(ctmp, c1, 0, 4, 1, 1)
    top.restrict_c(ctmp, c1, 12, 17, 1, 1)
    top.restrict(ub, tmp, b1, 0, 4, 5, 3)
    top.restrict(ub, tmp, b1, 8, 14, 5, 3)

    mid.faces(1, 5)
    mid.faces(12, 17)
    mid.weights(2, 6)
    mid.weights(12, 17)
    mid.start(ga_, 3, 17)
    mid.sweep(ga_, u1, 4, 16)
    mid.restrict(u1, tmp1, b2, 0, 5, 5, X2)
    mid.restrict_c(tmp1, c2, 0, 8, 1, X2 - 2)

    e0 = Y1 + (1 - oy) * 28
    e1 = Y1 + oy * 28
    f0 = pl.multiple_of(Y2 + (1 - oy) * 8, 8)
    f1 = pl.multiple_of(Y2 + oy * 8, 8)
    for pack, e, f in ((ypack0, e0, f0), (ypack1, e1, f1)):
        for k in range(4):
            x = X1 + 2 * k
            pack[k, pl.ds(0, 4), :] = pack_lanes([u1[x + j, pl.ds(e, 4), :] for j in range(2)])
            pack[k, pl.ds(4, 4), :] = pack_lanes([b1[x + j, pl.ds(e, 4), :] for j in range(2)])
        for k in range(2):
            pack[4 + k] = pack_lanes([b2[X2 + min(4 * k + j, 4), pl.ds(f, 8), :] for j in range(4)])
            pack[6 + k] = pack_lanes([c2[X2 - 2 + 4 * k + j, pl.ds(f, 8), :] for j in range(4)])


def set_y1(ref, y0, y1, oy, part):
    a0 = Y1 - 4 + (1 - oy) * 36
    a1 = Y1 - 4 + oy * 36
    for y, a in ((y0, a0), (y1, a1)):
        for k in range(4):
            for j, v in enumerate(unpack_lanes(y[k], 2)):
                ref[X1 + 2 * k + j, pl.ds(a, 4), :] = v[4 * part : 4 * part + 4]


def set_y2(c2, b2, y0, y1, oy):
    a0 = pl.multiple_of(Y2 - 8 + (1 - oy) * 24, 8)
    a1 = pl.multiple_of(Y2 - 8 + oy * 24, 8)
    for y, a in ((y0, a0), (y1, a1)):
        for k in range(2):
            for j, v in enumerate(unpack_lanes(y[4 + k], 4)):
                if 4 * k + j < 5:
                    b2[X2 + 4 * k + j, pl.ds(a, 8), :] = v
            for j, v in enumerate(unpack_lanes(y[6 + k], 4)):
                c2[X2 - 2 + 4 * k + j, pl.ds(a, 8), :] = v


def copy_rows(pairs, lo, hi):
    def body(x):
        for src, dst in pairs:
            dst[x] = src[x]

    rows(lo, hi, body)


def edge2_kernel(u1_in, b1_in, c2_in, b2_in, y0, y1, high, low, u1, b1, c2, b2):
    oy = odd("gy")
    copy_rows([(u1_in, u1), (b1_in, b1)], X1, X1 + 8)
    copy_rows([(c2_in, c2)], X2 - 2, X2 + 6)
    copy_rows([(b2_in, b2)], X2, X2 + 5)
    set_y1(u1, y0, y1, oy, 0)
    set_y1(b1, y0, y1, oy, 1)
    set_y2(c2, b2, y0, y1, oy)
    for pack, edge1, edge2, sign in ((high, X1 + 7, X2 + 3, -1), (low, X1, X2, 1)):
        for k in range(2):
            t = [u1[edge1 + sign * (2 * k + j), pl.ds(12, 40), :] for j in range(2)]
            pack[pl.ds(k * 40, 40), :] = pack_lanes(t)
        t = [c2[edge2 + sign * d, pl.ds(8, 32), :] for d in range(6)]
        t += [b2[edge2 + sign * d, pl.ds(8, 32), :] for d in range(5 if sign == 1 else 4)]
        t += t[:1] * (12 - len(t))
        for k in range(3):
            pack[pl.ds(80 + k * 32, 32), :] = pack_lanes(t[4 * k : 4 * k + 4])
        t = [b1[edge1 + sign * j, pl.ds(12, 40), :] for j in range(2)]
        pack[pl.ds(176, 40), :] = pack_lanes(t)
        t = [b1[edge1 + sign * 2, pl.ds(16 + 16 * j, 16), :] for j in range(2)]
        pack[pl.ds(216, 16), :] = pack_lanes(t)


def one_hot(shape, f):
    i = lax.broadcasted_iota(jnp.int32, shape, 0)
    j = lax.broadcasted_iota(jnp.int32, shape, 1)
    return jnp.where(f(i, j), 1.0, 0.0).astype(F32)


def exact_dot(a, b):
    return jnp.dot(a, b, precision=lax.Precision.HIGHEST, preferred_element_type=F32)


def halves(v):
    high = v.astype(jnp.bfloat16)
    return high, (v - high.astype(F32)).astype(jnp.bfloat16)


def split_dot(a, b):
    (a1, a2), (b1, b2) = halves(a), halves(b)
    return jnp.dot(jnp.concatenate([a1, a2, a1], 1), jnp.concatenate([b1, b1, b2], 0), preferred_element_type=F32)


def level2_kernel(
    u1_in, c2_in, b2_in, y0, y1, x0, x1, far,
    fx, fy, fz, w, b2, u2, u1, gather,
    c2, ua, tmp, b3, c3,
):
    ox, oy = odd("gx"), odd("gy")
    copy_rows([(u1_in, u1)], X1, X1 + 8)
    copy_rows([(c2_in, c2)], X2 - 2, X2 + 6)
    copy_rows([(b2_in, b2)], X2, X2 + 5)
    set_y1(u1, y0, y1, oy, 0)
    set_y2(c2, b2, y0, y1, oy)
    for pack, edge1, edge2, sign in ((x0, X1 + 7, X2 + 3, 1), (x1, X1, X2, -1)):
        for k in range(2):
            for j, v in enumerate(unpack_lanes(pack[pl.ds(k * 40, 40), :], 2)):
                u1[edge1 + sign * (2 * k + j + 1), pl.ds(12, 40), :] = v
        t = []
        for k in range(3):
            t += unpack_lanes(pack[pl.ds(80 + k * 32, 32), :], 4)
        for d in range(6):
            c2[edge2 + sign * (d + 1), pl.ds(8, 32), :] = t[d]
        for d in range(5 if sign == -1 else 4):
            b2[edge2 + sign * (d + 1), pl.ds(8, 32), :] = t[6 + d]
    b2[X2 + 8, pl.ds(8, 32), :] = unpack_lanes(far[pl.ds(112, 32), :], 4)[2]

    low = Level(2, c2, b2, fx, fy, fz, w, 8, 40)
    low.faces(0, 15)
    low.weights(1, 15, ua)
    low.sweep(ua, u2, 2, 14)
    low.restrict(u2, tmp, b3, 0, 2, X2, 0)
    low.restrict_c(tmp, c3, 0, 2, X2, 0)
    both = jnp.concatenate(
        [b3[0, pl.ds(16, 8), :], b3[1, pl.ds(16, 8), :], c3[0, pl.ds(16, 8), :], c3[1, pl.ds(16, 8), :]], 0
    )
    spread = exact_dot(both, one_hot((NZ, NZ), lambda i, j: i == 8 * (j % 16)))
    shape = (8, NZ)
    mine = lane(shape) // 16 == lax.broadcasted_iota(jnp.int32, shape, 0)
    packed = [
        jnp.sum(jnp.where(mine, spread[8 * k : 8 * k + 8], 0.0), axis=0, keepdims=True) for k in range(4)
    ]
    packed = [jnp.where(ox == 1, packed[k ^ 1], packed[k]) for k in range(4)]
    eight = jnp.concatenate(packed + packed, 0)

    def body(k):
        gather[pl.ds(pl.multiple_of(8 * k, 8), 8), :] = eight

    rows(0, 64, body, 8)


class Whole:
    def __init__(self, depth, b, c):
        self.h = H0 * 4.0**depth
        self.s = 2 ** (depth - 3)
        self.st = 16 * self.s
        self.b = b
        n = c.shape[0]
        sub = lax.broadcasted_iota(jnp.int32, (1,) + c.shape[1:], 2)
        up = self.xp(c)
        end = jnp.where(sub == 7, 0.0, up[n - 1 :])
        up = jnp.concatenate([up[: n - 1], end], 0) if n > 1 else end
        self.fxp = harmonic(c, up)
        up = self.yp(c)
        last = up[:, 3:]
        last = jnp.where(lane(last.shape) >= 128 - self.st, 0.0, last)
        self.fyp = harmonic(c, jnp.concatenate([up[:, :3], last], 1))
        self.fzp = harmonic(c, self.zp(c))
        self.fxm, self.fym, self.fzm = self.xm(self.fxp), self.ym(self.fyp), self.zm(self.fzp)
        d = self.h + self.fxp + self.fxm + self.fyp + self.fym + self.fzp + self.fzm
        self.w = DAMP * recip(d)

    def xp(self, v):
        wrap = pltpu.roll(v[:1], 7, 2)
        return jnp.concatenate([v[1:], wrap], 0) if v.shape[0] > 1 else wrap

    def xm(self, v):
        n = v.shape[0]
        wrap = pltpu.roll(v[n - 1 :], 1, 2)
        return jnp.concatenate([wrap, v[: n - 1]], 0) if n > 1 else wrap

    def yp(self, v):
        w = v if self.st == 128 else lroll(v, -self.st)
        far = jnp.concatenate([w[:, 1:], w[:, :1]], 1)
        return far if self.st == 128 else jnp.where(lane(v.shape) < 128 - self.st, w, far)

    def ym(self, v):
        w = v if self.st == 128 else lroll(v, self.st)
        far = jnp.concatenate([w[:, 3:], w[:, :3]], 1)
        return far if self.st == 128 else jnp.where(lane(v.shape) >= self.st, w, far)

    def zp(self, v):
        s = self.s
        return jnp.where(lane(v.shape) % 16 < 16 - s, lroll(v, -s), lroll(v, 16 - s))

    def zm(self, v):
        s = self.s
        return self.zp(v) if s == 8 else jnp.where(lane(v.shape) % 16 >= s, lroll(v, s), lroll(v, s - 16))

    def flux(self, v):
        acc = self.fxp * self.xp(v) + self.fxm * self.xm(v)
        acc = acc + self.fyp * self.yp(v) + self.fym * self.ym(v)
        return acc + self.fzp * self.zp(v) + self.fzm * self.zm(v)

    def sweep(self, v):
        return KEEP * v + self.w * (self.b + self.flux(v))

    def residual(self, v):
        r = self.b - self.h * v
        r = r + self.fxp * (self.xp(v) - v) + self.fxm * (self.xm(v) - v)
        r = r + self.fyp * (self.yp(v) - v) + self.fym * (self.ym(v) - v)
        return r + self.fzp * (self.zp(v) - v) + self.fzm * (self.zm(v) - v)

    def coarse(self, v, scale):
        v = jnp.concatenate([v[2 * k : 2 * k + 1] + v[2 * k + 1 : 2 * k + 2] for k in range(v.shape[0] // 2)], 0)
        return scale * pair_lanes(pair_lanes(v, self.s), self.st)


def coarsest(level, g):
    def column(v):
        v = v.reshape(32, NZ)
        low = lane(v.shape) % 16 < 8
        return jnp.concatenate([jnp.where(low, v, lroll(v, 8)), jnp.where(low, lroll(v, -8), v)], 0)

    shape = (64, NZ)
    i, j = lax.broadcasted_iota(jnp.int32, shape, 0), lane(shape)

    def pad(v):
        return jnp.concatenate([v, jnp.zeros(shape, F32)], 0)

    m = jnp.where(i == j, KEEP, 0.0)
    w = level.w
    for coef, at in (
        (w * level.fxp, i + 1),
        (w * level.fxm, i - 1),
        (w * level.fyp, i + 8),
        (w * level.fym, i - 8),
        (w * (level.fzp + level.fzm), i ^ 32),
    ):
        m = m + jnp.where(j == at, column(coef), 0.0)
    total = m + jnp.where(i == j, 1.0, 0.0)
    for _ in range(3):
        m = split_dot(m, pad(m))
        total = total + split_dot(m, pad(total))
    u = split_dot(total, pad(column(g)))
    low = lane((32, NZ)) % 16 < 8
    return jnp.where(low, u[:32], u[32:]).reshape(g.shape)


def whole_cycle(depth, b, c):
    level = Whole(depth, b, c)
    v = level.w * b
    if depth == 6:
        return coarsest(level, v)
    v = level.sweep(v)
    below = whole_cycle(depth + 1, level.coarse(level.residual(v), 0.5), level.coarse(c, 0.125))
    v = v + jnp.concatenate([below[k // 2 : k // 2 + 1] for k in range(v.shape[0])], 0)
    return level.sweep(level.sweep(v))


def up_kernel(
    gather, y0, y1, x1,
    hx, hy, hz, hw, b2, u2,
    gx_, gy_, gz_, gw_, b1_in, u1,
    fx, fy, fz, w, b, u0,
    out, res,
    s3, e2, e1, e0, ha, hb, b1, ga_, gb_, ua, ub,
):
    ix, iy = lax.axis_index("gx"), lax.axis_index("gy")
    ox, oy = ix % 2, iy % 2

    def field(k):
        return jnp.stack(
            [
                jnp.stack([gather[pl.ds(xq * 16 + g * 4 + k + xl, 8, stride=64), :] for g in range(4)], 0)
                for xq in range(4)
                for xl in range(2)
            ],
            0,
        )

    u3 = whole_cycle(3, field(0), field(2))
    s3[...] = jnp.zeros(s3.shape, F32)
    for xlo in range(8):
        for g in range(4):
            s3[g + 1, pl.ds(8 + xlo, 8, stride=8), :] = u3[xlo, g]
    shape = (8, NZ)
    mine = lane(shape) // 16 == lax.broadcasted_iota(jnp.int32, shape, 0)
    tiles = []
    for k in range(6):
        for g in range(3):
            row = s3[iy + g, pl.ds(2 * ix + 6 + 5 * ox + (1 - 2 * ox) * k, 1), :]
            tiles.append(jnp.where(mine, jnp.broadcast_to(row, shape), 0.0))
    spread = exact_dot(jnp.concatenate(tiles, 0), one_hot((NZ, NZ), lambda i, j: i % 16 == j // 8))
    for k in range(6):
        t = spread[24 * k : 24 * k + 24]
        e2[k, pl.ds(0, 24, stride=2), :] = t
        e2[k, pl.ds(1, 24, stride=2), :] = t

    for x in range(2, 14):
        ha[x] = u2[x] + e2[(x - 2) // 2]
    low = Level(2, None, b2, hx, hy, hz, hw, 8, 40)
    low.sweep(ha, hb, 3, 13)
    low.sweep(hb, ha, 4, 12)

    def grow1(k):
        t = ha[4 + k, pl.ds(8, 32), :]
        e1[k, pl.ds(0, 32, stride=2), :] = t
        e1[k, pl.ds(1, 32, stride=2), :] = t

    rows(0, 8, grow1)

    copy_rows([(b1_in, b1)], 2, 18)
    set_y1(b1, y0, y1, oy, 1)
    for j, v in enumerate(unpack_lanes(x1[pl.ds(176, 40), :], 2)):
        b1[X1 - 1 - j, pl.ds(12, 40), :] = v
    for j, v in enumerate(unpack_lanes(x1[pl.ds(216, 16), :], 2)):
        b1[X1 - 3, pl.ds(16 + 16 * j, 16), :] = v

    def add1(k):
        for j in range(2):
            ga_[1 + 2 * k + j] = u1[1 + 2 * k + j] + e1[k]

    rows(0, 8, add1)
    mid = Level(1, None, b1, gx_, gy_, gz_, gw_, 8, 56)
    mid.sweep(ga_, gb_, 2, 16)
    mid.sweep(gb_, ga_, 3, 15)

    def grow0(k):
        t = ga_[3 + k, pl.ds(8, 48), :]
        e0[k, pl.ds(0, 48, stride=2), :] = t
        e0[k, pl.ds(1, 48, stride=2), :] = t

    def add0(k):
        for j in range(2):
            ua[5 + 2 * k + j] = u0[5 + 2 * k + j] + e0[k]

    rows(0, 12, grow0, 4)
    rows(0, 12, add0, 4)
    top = Level(0, None, b, fx, fy, fz, w, 8, 88)
    top.sweep(ua, ub, 7, 27)
    top.sweep(ub, ua, 8, 26)

    def finish(x):
        to = stored(x)
        out[to] = ua[X0 + x, pl.ds(Y0, NY), :]
        res[to] = top.residual(ua, X0 + x, Y0, NY)

    rows(0, NX, finish)


def swaps(axis, first, second=None):
    count = lax.axis_size(axis)

    def pairs(start):
        return [p for i in range(start, count - 1, 2) for p in ((i, i + 1), (i + 1, i))]

    if second is None:
        return lax.ppermute(first, axis, pairs(0))
    late = lax.ppermute(second, axis, pairs(1))
    return lax.ppermute(first, axis, pairs(0)), late


def per_device(source, density, drag, porous_rows):
    sems = [pltpu.SemaphoreType.DMA((3, PARTS)), pltpu.SemaphoreType.DMA]
    block = (NX, NY, NZ)
    cond, source, p0, p1 = call(
        begin_kernel,
        [block, block, (32, 8, NZ), (32, 8, NZ)],
        [block] * 3 + [pltpu.VMEM((NY,), jnp.int32)] + sems,
        (source, density, drag, porous_rows),
        "begin",
        16,
        4,
    )
    y0, y1 = swaps("gy", p0, p1)
    q0, q1 = call(edge_kernel, [(HIGH_C + HIGH_B, NY, NZ), (LOW_C + LOW_B, NY, NZ)], [], (cond, source), "edges", 16, 0, 10**9)
    x0, x1 = swaps("gx", q0, q1)
    p0, p1 = call(corner_kernel, [(HIGH_TILES, 16, NZ), (LOW_TILES, 16, NZ)], [], (y0, y1), "corners", 16)
    k0, k1 = swaps("gx", p0, p1)
    zero, one, two = (36, 96, NZ), (18, 64, NZ), (16, 48, NZ)
    small, small1 = (18, 96, NZ), (10, 64, NZ)
    inner = call(
        inner_kernel, [small] * 8 + [small1] * 6, [(8, 96, NZ)], (cond, source, y0, y1), "inner", 16, 0, 10**10
    )
    down = call(
        down_kernel,
        [zero] * 6 + [one] * 6 + [two] * 2 + [(8, 8, NZ)] * 2,
        [zero] * 2 + [one] * 2 + [(14, 96, NZ), (17, 96, NZ), (8, 64, NZ)],
        (x0, x1, k0, k1, *inner),
        "down",
        24,
    )
    level0, level1 = down[:6], down[6:12]
    u1, c2, b2, p0, p1 = down[11:]
    y0, y1 = swaps("gy", p0, p1)
    p0, p1 = call(edge2_kernel, [(232, NZ)] * 2, [one, one, two, two], (u1, level1[4], c2, b2, y0, y1), "edges2", 16)
    x0, x1 = swaps("gx", p0, p1)
    far = swaps("gx", x1)
    *level2, u1, packed = call(
        level2_kernel,
        [two] * 6 + [one, (512, NZ)],
        [two] * 2 + [(2, 48, NZ)] * 3,
        (u1, c2, b2, y0, y1, x0, x1, far),
        "level2",
        16,
    )
    whole = lax.all_to_all(packed, ("gx", "gy"), 0, 0, tiled=True)
    out, res = call(
        up_kernel,
        [block] * 2,
        [(6, 80, NZ), (6, 48, NZ), (8, 64, NZ), (12, 96, NZ)] + [two] * 2 + [one] * 3 + [zero] * 2,
        (whole, y0, y1, x1, *level2, *level1[:5], u1, *level0),
        "up",
        24,
    )
    return out, res


def solution(mesh):
    return jax.shard_map(
        per_device,
        mesh=mesh,
        in_specs=(P("gx", "gy", None), P("gx", "gy", None), P("gx", "gy", None), P("gy")),
        out_specs=(P("gx", "gy", None), P("gx", "gy", None)),
        check_vma=False,
    )
```

```python
import functools

import jax
import jax.numpy as jnp
from jax import lax
from jax.experimental import pallas as pl
from jax.experimental.pallas import tpu as pltpu
from jax.sharding import PartitionSpec as P

SWEEPS_COARSE = 16
DAMP = 0.8
KEEP = 1.0 - DAMP
H0 = 0.0002

NX, NY, NZ = 16, 64, 128
F32 = jnp.float32
VMEM = pl.BlockSpec(memory_space=pltpu.VMEM)
HBM = pl.BlockSpec(memory_space=pltpu.HBM)


def call(body, outs, scratch, args, name, vmem, hbm=0, cost=0):
    args = [pltpu.with_memory_space_constraint(a, pltpu.HBM) for a in args[:hbm]] + list(args[hbm:])
    return pl.pallas_call(
        body,
        out_shape=[jax.ShapeDtypeStruct(s, F32) for s in outs],
        in_specs=[HBM] * hbm + [VMEM] * (len(args) - hbm),
        out_specs=[VMEM] * len(outs),
        scratch_shapes=[pltpu.VMEM(s, F32) if isinstance(s, tuple) else s for s in scratch],
        compiler_params=pltpu.CompilerParams(vmem_limit_bytes=vmem * 2**20),
        name=name,
        cost_estimate=pl.CostEstimate(flops=cost, bytes_accessed=0, transcendentals=0) if cost else None,
    )(*args)


def recip(t):
    return 1.0 / t


def harmonic(a, b):
    return (2.0 * a) * b / jnp.maximum(a + b, 1e-30)


def lane(shape):
    return lax.broadcasted_iota(jnp.int32, shape, len(shape) - 1)


def lroll(v, shift):
    return pltpu.roll(v, shift % 128, v.ndim - 1)


def pair_lanes(v, s):
    first = (lane(v.shape) // s) % 2 == 0
    return v + jnp.where(first, lroll(v, -s), lroll(v, s))


def pack_lanes(tiles):
    n = len(tiles)
    out = tiles[0]
    for k in range(1, n):
        out = jnp.where(lane(out.shape) % n == k, tiles[k], out)
    return out


def unpack_lanes(p, n):
    at = lane(p.shape) % n
    moved = {d: p if d == 0 else lroll(p, -d) for d in range(1 - n, n)}
    tiles = []
    for k in range(n):
        out = moved[k]
        for m in range(1, n):
            out = jnp.where(at == m, moved[k - m], out)
        tiles.append(out)
    return tiles


def rows(lo, hi, body, unroll=8):
    whole = (hi - lo) // unroll

    def step(k, carry):
        for j in range(unroll):
            body(lo + k * unroll + j)
        return carry

    if whole > 1:
        lax.fori_loop(0, whole, step, 0)
        lo = lo + whole * unroll
    for x in range(lo, hi):
        body(x)


class Level:
    def __init__(self, depth, c, b, fx, fy, fz, w, ys, ye):
        self.h = H0 * 4.0**depth
        self.s = 2**depth
        self.c, self.b, self.fx, self.fy, self.fz, self.w = c, b, fx, fy, fz, w
        self.ys, self.n = ys, ye - ys

    def faces(self, lo, hi):
        here, above = pl.ds(self.ys, self.n), pl.ds(self.ys + 1, self.n)

        def body(x):
            c = self.c[x, here, :]
            twice, safe = c + c, c + 1e-30

            def face(other):
                return twice * other / (safe + other)

            self.fx[x, here, :] = face(self.c[x + 1, here, :])
            self.fy[x, here, :] = face(self.c[x, above, :])
            self.fz[x, here, :] = face(lroll(c, -self.s))

        rows(lo, hi, body)

    def weights(self, lo, hi, start=None):
        here, below = pl.ds(self.ys, self.n), pl.ds(self.ys - 1, self.n)

        def body(x):
            fz = self.fz[x, here, :]
            d = self.fx[x, here, :] + self.fx[x - 1, here, :]
            d = d + (self.fy[x, here, :] + self.fy[x, below, :])
            d = d + (fz + lroll(fz, self.s))
            w = DAMP * recip(self.h + d)
            self.w[x, here, :] = w
            if start is not None:
                start[x, here, :] = w * self.b[x, here, :]

        rows(lo, hi, body)

    def start(self, out, lo, hi):
        here = pl.ds(self.ys, self.n)

        def body(x):
            out[x, here, :] = self.w[x, here, :] * self.b[x, here, :]

        rows(lo, hi, body)

    def sweep(self, u, out, lo, hi):
        here = pl.ds(self.ys, self.n)
        above, below = pl.ds(self.ys + 1, self.n), pl.ds(self.ys - 1, self.n)

        def body(x):
            v = u[x, here, :]
            fz = self.fz[x, here, :]
            acc = fz * lroll(v, -self.s) + lroll(fz * v, self.s)
            acc = acc + (self.fx[x, here, :] * u[x + 1, here, :] + self.fx[x - 1, here, :] * u[x - 1, here, :])
            acc = acc + (self.fy[x, here, :] * u[x, above, :] + self.fy[x, below, :] * u[x, below, :])
            out[x, here, :] = KEEP * v + self.w[x, here, :] * (self.b[x, here, :] + acc)

        rows(lo, hi, body)

    def residual(self, u, x, y, n):
        here, above, below = pl.ds(y, n), pl.ds(y + 1, n), pl.ds(y - 1, n)
        v = u[x, here, :]
        flow = self.fz[x, here, :] * (lroll(v, -self.s) - v)
        r = self.b[x, here, :] - self.h * v
        r = r + (flow - lroll(flow, self.s))
        r = r + self.fx[x, here, :] * (u[x + 1, here, :] - v)
        r = r + self.fx[x - 1, here, :] * (u[x - 1, here, :] - v)
        r = r + self.fy[x, here, :] * (u[x, above, :] - v)
        return r + self.fy[x, below, :] * (u[x, below, :] - v)

    def halve(self, tmp, out, lo, hi, x_to, scale):
        half = tmp.shape[1] // 2

        def body(k):
            t = tmp[k, pl.ds(0, half, stride=2), :] + tmp[k, pl.ds(1, half, stride=2), :]
            out[x_to + k, pl.ds(8, half), :] = scale * pair_lanes(t, self.s)

        rows(lo, hi, body)

    def restrict(self, u, tmp, out, lo, hi, x_from, x_to):
        def body(k):
            x = x_from + 2 * k
            both = self.residual(u, x, self.ys, self.n) + self.residual(u, x + 1, self.ys, self.n)
            tmp[k, pl.ds(self.ys, self.n), :] = both

        rows(lo, hi, body, 4)
        self.halve(tmp, out, lo, hi, x_to, 0.5)

    def restrict_c(self, tmp, out, lo, hi, x_from, x_to):
        def body(k):
            x = x_from + 2 * k
            tmp[k] = self.c[x] + self.c[x + 1]

        rows(lo, hi, body)
        self.halve(tmp, out, lo, hi, x_to, 0.125)


def odd(axis):
    return lax.axis_index(axis) % 2


PARTS = 4


def stored(x):
    o = odd("gx")
    return o * (NX - 1) + (1 - 2 * o) * x


def begin_kernel(source, density, drag, porous, cond, rhs, ypack0, ypack1, dens, dra, src, por, sem, psem):
    o = odd("gy")
    at0 = pl.multiple_of((1 - o) * (NY - 8), 8)
    at1 = pl.multiple_of(o * (NY - 8), 8)
    part = NX // PARTS
    loads = []
    first = pltpu.make_async_copy(porous, por, psem)
    first.start()
    for k in range(PARTS):
        here = pl.ds(k * part, part)
        for j, (ref, dst) in enumerate(((density, dens), (drag, dra), (source, src))):
            loads.append(pltpu.make_async_copy(ref.at[here], dst.at[here], sem.at[j, k]))
            loads[-1].start()
    first.wait()
    line = jnp.broadcast_to(por[...].astype(F32)[None], (NY, NY))
    same = lax.broadcasted_iota(jnp.int32, (NY, NY), 0) == lax.broadcasted_iota(jnp.int32, (NY, NY), 1)
    mask = jnp.broadcast_to(jnp.sum(jnp.where(same, line, 0.0), axis=1, keepdims=True), (NY, NZ))
    for k in range(PARTS):
        for load in loads[3 * k : 3 * k + 3]:
            load.wait()
        for x in range(k * part, k * part + part):
            to = stored(x)
            cond[to] = recip(dens[x] * (1.0 + dra[x] * mask))
            rhs[to] = src[x]
            for pack, at in ((ypack0, at0), (ypack1, at1)):
                pack[to] = cond[to, pl.ds(at, 8), :]
                pack[NX + to] = src[x, pl.ds(at, 8), :]


HIGH_C, HIGH_B, LOW_C, LOW_B = 11, 10, 8, 6


def edge_kernel(cond, source, high, low):
    for d in range(HIGH_C):
        high[d] = cond[NX - 1 - d]
    for d in range(HIGH_B):
        high[HIGH_C + d] = source[NX - 1 - d]
    for d in range(LOW_C):
        low[d] = cond[d]
    for d in range(LOW_B):
        low[LOW_C + d] = source[d]


HIGH = (
    [(0, d, d - 1, 0) for d in (1, 2, 3, 4, 5, 6, 7)]
    + [(0, 9, 4, 2), (0, 8, 5, 3), (0, 10, 6, 1)]
    + [(1, d, d + 6, 0) for d in (1, 2, 3, 4, 5, 6)]
    + [(1, 7, 11, 3), (1, 8, 12, 2), (1, 9, 10, 1)]
)
LOW = [(0, 1, 0, 0), (0, 7, 0, 1), (0, 2, 1, 0), (0, 6, 1, 2), (0, 3, 2, 0), (0, 5, 2, 3), (0, 4, 3, 0)]
LOW += [(1, 5, 3, 1), (1, 1, 4, 0), (1, 3, 4, 3), (1, 2, 5, 0), (1, 4, 5, 2)]
HIGH_TILES, LOW_TILES = 13, 6


def turn(v, by):
    return v if by == 0 else pltpu.roll(v, by % 8, 0)


def corner_kernel(y0, y1, high, low):
    oy = odd("gy")
    at0 = pl.multiple_of((1 - oy) * 8, 8)
    at1 = pl.multiple_of(oy * 8, 8)
    row = lax.broadcasted_iota(jnp.int32, (8, NZ), 0)
    for pack, corners, count, side in ((high, HIGH, HIGH_TILES, 1), (low, LOW, LOW_TILES, 0)):
        for y, at, above in ((y0, at0, 1 - oy), (y1, at1, oy)):
            tiles = {}
            for field, d, t, by in corners:
                v = y[field * NX + (NX - d if side else d - 1)]
                if by == 0:
                    tiles[t] = v
                else:
                    under = jnp.where(row < by, turn(v, by), tiles[t])
                    over = jnp.where(row >= 8 - by, turn(v, -by), tiles[t])
                    tiles[t] = jnp.where(above == 1, over, under)
            for t in range(count):
                pack[t, pl.ds(at, 8), :] = tiles[t]


X0, Y0 = 9, 16
X1, Y1 = 5, 16
X2, Y2 = 6, 16


def levels_down(c, b, fx, fy, fz, w, c1, b1, gx_, gy_, gz_, gw_):
    top = Level(0, c, b, fx, fy, fz, w, 8, 88)
    return top, Level(1, c1, b1, gx_, gy_, gz_, gw_, 8, 56)


def inner_kernel(cond, source, y0, y1, c, b, fx, fy, fz, w, ua, ub, c1, b1, gx_, gy_, gz_, gw_, tmp):
    oy = odd("gy")
    at0 = pl.multiple_of(8 + (1 - oy) * (NY + 8), 8)
    at1 = pl.multiple_of(8 + oy * (NY + 8), 8)

    def own(x):
        c[1 + x, pl.ds(Y0, NY), :] = cond[x]
        c[1 + x, pl.ds(at0, 8), :] = y0[x]
        c[1 + x, pl.ds(at1, 8), :] = y1[x]
        b[1 + x, pl.ds(Y0, NY), :] = source[x]
        b[1 + x, pl.ds(at0, 8), :] = y0[NX + x]
        b[1 + x, pl.ds(at1, 8), :] = y1[NX + x]

    rows(0, NX, own)
    top, mid = levels_down(c, b, fx, fy, fz, w, c1, b1, gx_, gy_, gz_, gw_)
    top.faces(1, 17)
    top.weights(2, 16, ua)
    top.sweep(ua, ub, 3, 15)
    top.restrict_c(tmp, c1, 0, 8, 1, 1)
    top.restrict(ub, tmp, b1, 2, 6, 1, 1)
    mid.faces(1, 9)
    mid.weights(2, 8)


def down_kernel(
    x0, x1, k0, k1, c_in, b_in, fx_in, fy_in, fz_in, w_in, ua_in, ub_in, c1_in, b1_in, gx_in, gy_in, gz_in, gw_in,
    fx, fy, fz, w, b, ub, gx_, gy_, gz_, gw_, b1, u1, c2, b2, ypack0, ypack1,
    c, ua, c1, ga_, tmp, ctmp, tmp1,
):
    oy = odd("gy")
    here, here1 = pl.ds(8, 80), pl.ds(8, 48)
    sides = ((x0, k0, HIGH, HIGH_C, HIGH_B, X0 + NX - 1, 1), (x1, k1, LOW, LOW_C, LOW_B, X0, -1))
    for x, pack, corners, nc, nb, edge, sign in sides:
        for d in range(1, nc + 1):
            c[edge + sign * d, pl.ds(Y0, NY), :] = x[d - 1]
        for d in range(1, nb + 1):
            b[edge + sign * d, pl.ds(Y0, NY), :] = x[nc + d - 1]
        for field, d, t, by in corners:
            ref = (c, b)[field]
            ref[edge + sign * d, pl.ds(8, 8), :] = turn(pack[t, pl.ds(0, 8), :], -by)
            ref[edge + sign * d, pl.ds(80, 8), :] = turn(pack[t, pl.ds(8, 8), :], by)
    for x in (1, 16):
        c[x + 8, here, :] = c_in[x, here, :]
    for x in (2, 3, 14, 15):
        ua[x + 8, here, :] = ua_in[x, here, :]

    def fill(x):
        for ref, src in ((fx, fx_in), (fy, fy_in), (fz, fz_in), (w, w_in), (b, b_in), (ub, ub_in)):
            ref[x + 8, here, :] = src[x, here, :]

    rows(1, 17, fill)
    for x in range(1, 9):
        c1[x + 4, here1, :] = c1_in[x, here1, :]
        for ref, src in ((gx_, gx_in), (gy_, gy_in), (gz_, gz_in), (gw_, gw_in), (b1, b1_in)):
            ref[x + 4, here1, :] = src[x, here1, :]

    top, mid = levels_down(c, b, fx, fy, fz, w, c1, b1, gx_, gy_, gz_, gw_)
    top.faces(2, 9)
    top.faces(24, 35)
    top.weights(3, 10, ua)
    top.weights(24, 35, ua)
    top.sweep(ua, ub, 4, 11)
    top.sweep(ua, ub, 23, 34)
    top.restrict_c(ctmp, c1, 0, 4, 1, 1)
    top.restrict_c(ctmp, c1, 12, 17, 1, 1)
    top.restrict(ub, tmp, b1, 0, 4, 5, 3)
    top.restrict(ub, tmp, b1, 8, 14, 5, 3)

    mid.faces(1, 5)
    mid.faces(12, 17)
    mid.weights(2, 6)
    mid.weights(12, 17)
    mid.start(ga_, 3, 17)
    mid.sweep(ga_, u1, 4, 16)
    mid.restrict(u1, tmp1, b2, 0, 5, 5, X2)
    mid.restrict_c(tmp1, c2, 0, 8, 1, X2 - 2)

    e0 = Y1 + (1 - oy) * 28
    e1 = Y1 + oy * 28
    f0 = pl.multiple_of(Y2 + (1 - oy) * 8, 8)
    f1 = pl.multiple_of(Y2 + oy * 8, 8)
    for pack, e, f in ((ypack0, e0, f0), (ypack1, e1, f1)):
        for k in range(4):
            x = X1 + 2 * k
            pack[k, pl.ds(0, 4), :] = pack_lanes([u1[x + j, pl.ds(e, 4), :] for j in range(2)])
            pack[k, pl.ds(4, 4), :] = pack_lanes([b1[x + j, pl.ds(e, 4), :] for j in range(2)])
        for k in range(2):
            pack[4 + k] = pack_lanes([b2[X2 + min(4 * k + j, 4), pl.ds(f, 8), :] for j in range(4)])
            pack[6 + k] = pack_lanes([c2[X2 - 2 + 4 * k + j, pl.ds(f, 8), :] for j in range(4)])


def set_y1(ref, y0, y1, oy, part):
    a0 = Y1 - 4 + (1 - oy) * 36
    a1 = Y1 - 4 + oy * 36
    for y, a in ((y0, a0), (y1, a1)):
        for k in range(4):
            for j, v in enumerate(unpack_lanes(y[k], 2)):
                ref[X1 + 2 * k + j, pl.ds(a, 4), :] = v[4 * part : 4 * part + 4]


def set_y2(c2, b2, y0, y1, oy):
    a0 = pl.multiple_of(Y2 - 8 + (1 - oy) * 24, 8)
    a1 = pl.multiple_of(Y2 - 8 + oy * 24, 8)
    for y, a in ((y0, a0), (y1, a1)):
        for k in range(2):
            for j, v in enumerate(unpack_lanes(y[4 + k], 4)):
                if 4 * k + j < 5:
                    b2[X2 + 4 * k + j, pl.ds(a, 8), :] = v
            for j, v in enumerate(unpack_lanes(y[6 + k], 4)):
                c2[X2 - 2 + 4 * k + j, pl.ds(a, 8), :] = v


def copy_rows(pairs, lo, hi):
    def body(x):
        for src, dst in pairs:
            dst[x] = src[x]

    rows(lo, hi, body)


def edge2_kernel(u1_in, b1_in, c2_in, b2_in, y0, y1, high, low, u1, b1, c2, b2):
    oy = odd("gy")
    copy_rows([(u1_in, u1), (b1_in, b1)], X1, X1 + 8)
    copy_rows([(c2_in, c2)], X2 - 2, X2 + 6)
    copy_rows([(b2_in, b2)], X2, X2 + 5)
    set_y1(u1, y0, y1, oy, 0)
    set_y1(b1, y0, y1, oy, 1)
    set_y2(c2, b2, y0, y1, oy)
    for pack, edge1, edge2, sign in ((high, X1 + 7, X2 + 3, -1), (low, X1, X2, 1)):
        for k in range(2):
            t = [u1[edge1 + sign * (2 * k + j), pl.ds(12, 40), :] for j in range(2)]
            pack[pl.ds(k * 40, 40), :] = pack_lanes(t)
        t = [c2[edge2 + sign * d, pl.ds(10, 28), :] for d in range(6)]
        t += [b2[edge2 + sign * d, pl.ds(10, 28), :] for d in range(5 if sign == 1 else 4)]
        t += t[:1] * (12 - len(t))
        for k in range(3):
            pack[pl.ds(80 + k * 28, 28), :] = pack_lanes(t[4 * k : 4 * k + 4])
        for n, y in enumerate((12, 48)):
            t = [b1[edge1 + sign * j, pl.ds(y, 4), :] for j in range(2)]
            pack[pl.ds(164 + 4 * n, 4), :] = pack_lanes(t)
        t = [b1[edge1 + sign * 2, pl.ds(16 + 16 * j, 16), :] for j in range(2)]
        pack[pl.ds(172, 16), :] = pack_lanes(t)


def one_hot(shape, f):
    i = lax.broadcasted_iota(jnp.int32, shape, 0)
    j = lax.broadcasted_iota(jnp.int32, shape, 1)
    return jnp.where(f(i, j), 1.0, 0.0).astype(F32)


def exact_dot(a, b):
    return jnp.dot(a, b, precision=lax.Precision.HIGHEST, preferred_element_type=F32)


def halves(v):
    high = v.astype(jnp.bfloat16)
    return high, (v - high.astype(F32)).astype(jnp.bfloat16)


def split_dot(a, b):
    (a1, a2), (b1, b2) = halves(a), halves(b)
    return jnp.dot(jnp.concatenate([a1, a2, a1], 1), jnp.concatenate([b1, b1, b2], 0), preferred_element_type=F32)


def level2_kernel(
    u1_in, c2_in, b2_in, y0, y1, x0, x1,
    fx, fy, fz, w, b2, u2, u1, gather,
    c2, ua, tmp, b3, c3,
):
    ox, oy = odd("gx"), odd("gy")
    copy_rows([(u1_in, u1)], X1, X1 + 8)
    copy_rows([(c2_in, c2)], X2 - 2, X2 + 6)
    copy_rows([(b2_in, b2)], X2, X2 + 5)
    set_y1(u1, y0, y1, oy, 0)
    set_y2(c2, b2, y0, y1, oy)
    for pack, edge1, edge2, sign in ((x0, X1 + 7, X2 + 3, 1), (x1, X1, X2, -1)):
        for k in range(2):
            for j, v in enumerate(unpack_lanes(pack[pl.ds(k * 40, 40), :], 2)):
                u1[edge1 + sign * (2 * k + j + 1), pl.ds(12, 40), :] = v
        t = []
        for k in range(3):
            t += unpack_lanes(pack[pl.ds(80 + k * 28, 28), :], 4)
        for d in range(6):
            c2[edge2 + sign * (d + 1), pl.ds(10, 28), :] = t[d]
        for d in range(5 if sign == -1 else 4):
            b2[edge2 + sign * (d + 1), pl.ds(10, 28), :] = t[6 + d]

    low = Level(2, c2, b2, fx, fy, fz, w, 8, 40)
    low.faces(0, 15)
    low.weights(1, 15, ua)
    low.sweep(ua, u2, 2, 14)
    low.restrict(u2, tmp, b3, 0, 2, X2, 0)
    low.restrict_c(tmp, c3, 0, 2, X2, 0)
    both = jnp.concatenate(
        [b3[0, pl.ds(16, 8), :], b3[1, pl.ds(16, 8), :], c3[0, pl.ds(16, 8), :], c3[1, pl.ds(16, 8), :]], 0
    )
    spread = exact_dot(both, one_hot((NZ, NZ), lambda i, j: i == 8 * (j % 16)))
    shape = (8, NZ)
    mine = lane(shape) // 16 == lax.broadcasted_iota(jnp.int32, shape, 0)
    packed = [
        jnp.sum(jnp.where(mine, spread[8 * k : 8 * k + 8], 0.0), axis=0, keepdims=True) for k in range(4)
    ]
    packed = [jnp.where(ox == 1, packed[k ^ 1], packed[k]) for k in range(4)]
    eight = jnp.concatenate(packed + packed, 0)

    def body(k):
        gather[pl.ds(pl.multiple_of(8 * k, 8), 8), :] = eight

    rows(0, 64, body, 8)


class Whole:
    def __init__(self, depth, b, c):
        self.h = H0 * 4.0**depth
        self.s = 2 ** (depth - 3)
        self.st = 16 * self.s
        self.b = b
        n = c.shape[0]
        sub = lax.broadcasted_iota(jnp.int32, (1,) + c.shape[1:], 2)
        up = self.xp(c)
        end = jnp.where(sub == 7, 0.0, up[n - 1 :])
        up = jnp.concatenate([up[: n - 1], end], 0) if n > 1 else end
        self.fxp = harmonic(c, up)
        up = self.yp(c)
        last = up[:, 3:]
        last = jnp.where(lane(last.shape) >= 128 - self.st, 0.0, last)
        self.fyp = harmonic(c, jnp.concatenate([up[:, :3], last], 1))
        self.fzp = harmonic(c, self.zp(c))
        self.fxm, self.fym, self.fzm = self.xm(self.fxp), self.ym(self.fyp), self.zm(self.fzp)
        d = self.h + self.fxp + self.fxm + self.fyp + self.fym + self.fzp + self.fzm
        self.w = DAMP * recip(d)

    def xp(self, v):
        wrap = pltpu.roll(v[:1], 7, 2)
        return jnp.concatenate([v[1:], wrap], 0) if v.shape[0] > 1 else wrap

    def xm(self, v):
        n = v.shape[0]
        wrap = pltpu.roll(v[n - 1 :], 1, 2)
        return jnp.concatenate([wrap, v[: n - 1]], 0) if n > 1 else wrap

    def yp(self, v):
        w = v if self.st == 128 else lroll(v, -self.st)
        far = jnp.concatenate([w[:, 1:], w[:, :1]], 1)
        return far if self.st == 128 else jnp.where(lane(v.shape) < 128 - self.st, w, far)

    def ym(self, v):
        w = v if self.st == 128 else lroll(v, self.st)
        far = jnp.concatenate([w[:, 3:], w[:, :3]], 1)
        return far if self.st == 128 else jnp.where(lane(v.shape) >= self.st, w, far)

    def zp(self, v):
        s = self.s
        return jnp.where(lane(v.shape) % 16 < 16 - s, lroll(v, -s), lroll(v, 16 - s))

    def zm(self, v):
        s = self.s
        return self.zp(v) if s == 8 else jnp.where(lane(v.shape) % 16 >= s, lroll(v, s), lroll(v, s - 16))

    def flux(self, v):
        acc = self.fxp * self.xp(v) + self.fxm * self.xm(v)
        acc = acc + self.fyp * self.yp(v) + self.fym * self.ym(v)
        return acc + self.fzp * self.zp(v) + self.fzm * self.zm(v)

    def sweep(self, v):
        return KEEP * v + self.w * (self.b + self.flux(v))

    def residual(self, v):
        r = self.b - self.h * v
        r = r + self.fxp * (self.xp(v) - v) + self.fxm * (self.xm(v) - v)
        r = r + self.fyp * (self.yp(v) - v) + self.fym * (self.ym(v) - v)
        return r + self.fzp * (self.zp(v) - v) + self.fzm * (self.zm(v) - v)

    def coarse(self, v, scale):
        v = jnp.concatenate([v[2 * k : 2 * k + 1] + v[2 * k + 1 : 2 * k + 2] for k in range(v.shape[0] // 2)], 0)
        return scale * pair_lanes(pair_lanes(v, self.s), self.st)


def coarsest(level, g):
    def column(v):
        v = v.reshape(32, NZ)
        low = lane(v.shape) % 16 < 8
        return jnp.concatenate([jnp.where(low, v, lroll(v, 8)), jnp.where(low, lroll(v, -8), v)], 0)

    shape = (64, NZ)
    i, j = lax.broadcasted_iota(jnp.int32, shape, 0), lane(shape)

    def pad(v):
        return jnp.concatenate([v, jnp.zeros(shape, F32)], 0)

    m = jnp.where(i == j, KEEP, 0.0)
    w = level.w
    for coef, at in (
        (w * level.fxp, i + 1),
        (w * level.fxm, i - 1),
        (w * level.fyp, i + 8),
        (w * level.fym, i - 8),
        (w * (level.fzp + level.fzm), i ^ 32),
    ):
        m = m + jnp.where(j == at, column(coef), 0.0)
    total = m + jnp.where(i == j, 1.0, 0.0)
    for _ in range(3):
        m = split_dot(m, pad(m))
        total = total + split_dot(m, pad(total))
    u = split_dot(total, pad(column(g)))
    low = lane((32, NZ)) % 16 < 8
    return jnp.where(low, u[:32], u[32:]).reshape(g.shape)


def whole_cycle(depth, b, c):
    level = Whole(depth, b, c)
    v = level.w * b
    if depth == 6:
        return coarsest(level, v)
    v = level.sweep(v)
    below = whole_cycle(depth + 1, level.coarse(level.residual(v), 0.5), level.coarse(c, 0.125))
    v = v + jnp.concatenate([below[k // 2 : k // 2 + 1] for k in range(v.shape[0])], 0)
    return level.sweep(level.sweep(v))


def up_kernel(
    gather, y0, y1, x1, far,
    hx, hy, hz, hw, b2, u2,
    gx_, gy_, gz_, gw_, b1_in, u1,
    fx, fy, fz, w, b, u0,
    out, res,
    s3, e2, e1, e0, ha, hb, b1, ga_, gb_, ua, ub,
):
    ix, iy = lax.axis_index("gx"), lax.axis_index("gy")
    ox, oy = ix % 2, iy % 2
    low = Level(2, None, b2, hx, hy, hz, hw, 8, 40)
    wide = pl.ds(8, 32)
    low.start(ha, X2 + 6, X2 + 8)
    ha[X2 + 8, pl.ds(10, 28), :] = hw[X2 + 8, pl.ds(10, 28), :] * unpack_lanes(far[pl.ds(108, 28), :], 4)[2]
    low.sweep(ha, hb, X2 + 7, X2 + 8)

    def field(k):
        return jnp.stack(
            [
                jnp.stack([gather[pl.ds(xq * 16 + g * 4 + k + xl, 8, stride=64), :] for g in range(4)], 0)
                for xq in range(4)
                for xl in range(2)
            ],
            0,
        )

    u3 = whole_cycle(3, field(0), field(2))
    s3[...] = jnp.zeros(s3.shape, F32)
    for xlo in range(8):
        for g in range(4):
            s3[g + 1, pl.ds(8 + xlo, 8, stride=8), :] = u3[xlo, g]
    shape = (8, NZ)
    mine = lane(shape) // 16 == lax.broadcasted_iota(jnp.int32, shape, 0)
    tiles = []
    for k in range(6):
        for g in range(3):
            row = s3[iy + g, pl.ds(2 * ix + 6 + 5 * ox + (1 - 2 * ox) * k, 1), :]
            tiles.append(jnp.where(mine, jnp.broadcast_to(row, shape), 0.0))
    spread = exact_dot(jnp.concatenate(tiles, 0), one_hot((NZ, NZ), lambda i, j: i % 16 == j // 8))
    for k in range(6):
        t = spread[24 * k : 24 * k + 24]
        e2[k, pl.ds(0, 24, stride=2), :] = t
        e2[k, pl.ds(1, 24, stride=2), :] = t

    for x in range(2, 14):
        ha[x, wide, :] = (hb if x == X2 + 7 else u2)[x, wide, :] + e2[(x - 2) // 2, wide, :]
    low.sweep(ha, hb, 3, 13)
    low.sweep(hb, ha, 4, 12)

    def grow1(k):
        t = ha[4 + k, pl.ds(8, 32), :]
        e1[k, pl.ds(0, 32, stride=2), :] = t
        e1[k, pl.ds(1, 32, stride=2), :] = t

    rows(0, 8, grow1)

    copy_rows([(b1_in, b1)], 2, 18)
    set_y1(b1, y0, y1, oy, 1)
    for j, v in enumerate(unpack_lanes(x1[pl.ds(164, 8), :], 2)):
        b1[X1 - 1 - j, pl.ds(12, 4), :] = v[0:4]
        b1[X1 - 1 - j, pl.ds(48, 4), :] = v[4:8]
    for j, v in enumerate(unpack_lanes(x1[pl.ds(172, 16), :], 2)):
        b1[X1 - 3, pl.ds(16 + 16 * j, 16), :] = v

    def add1(k):
        for j in range(2):
            ga_[1 + 2 * k + j] = u1[1 + 2 * k + j] + e1[k]

    rows(0, 8, add1)
    mid = Level(1, None, b1, gx_, gy_, gz_, gw_, 8, 56)
    mid.sweep(ga_, gb_, 2, 16)
    mid.sweep(gb_, ga_, 3, 15)

    def grow0(k):
        t = ga_[3 + k, pl.ds(8, 48), :]
        e0[k, pl.ds(0, 48, stride=2), :] = t
        e0[k, pl.ds(1, 48, stride=2), :] = t

    def add0(k):
        for j in range(2):
            ua[5 + 2 * k + j] = u0[5 + 2 * k + j] + e0[k]

    rows(0, 12, grow0, 4)
    rows(0, 12, add0, 4)
    top = Level(0, None, b, fx, fy, fz, w, 8, 88)
    top.sweep(ua, ub, 7, 27)
    top.sweep(ub, ua, 8, 26)

    def finish(x):
        to = stored(x)
        out[to] = ua[X0 + x, pl.ds(Y0, NY), :]
        res[to] = top.residual(ua, X0 + x, Y0, NY)

    rows(0, NX, finish)


def swaps(axis, first, second=None):
    count = lax.axis_size(axis)

    def pairs(start):
        return [p for i in range(start, count - 1, 2) for p in ((i, i + 1), (i + 1, i))]

    if second is None:
        return lax.ppermute(first, axis, pairs(0))
    late = lax.ppermute(second, axis, pairs(1))
    return lax.ppermute(first, axis, pairs(0)), late


def per_device(source, density, drag, porous_rows):
    sems = [pltpu.SemaphoreType.DMA((3, PARTS)), pltpu.SemaphoreType.DMA]
    block = (NX, NY, NZ)
    cond, source, p0, p1 = call(
        begin_kernel,
        [block, block, (32, 8, NZ), (32, 8, NZ)],
        [block] * 3 + [pltpu.VMEM((NY,), jnp.int32)] + sems,
        (source, density, drag, porous_rows),
        "begin",
        16,
        4,
    )
    y0, y1 = swaps("gy", p0, p1)
    q0, q1 = call(edge_kernel, [(HIGH_C + HIGH_B, NY, NZ), (LOW_C + LOW_B, NY, NZ)], [], (cond, source), "edges", 16, 0, 10**9)
    x0, x1 = swaps("gx", q0, q1)
    p0, p1 = call(corner_kernel, [(HIGH_TILES, 16, NZ), (LOW_TILES, 16, NZ)], [], (y0, y1), "corners", 16)
    k0, k1 = swaps("gx", p0, p1)
    zero, one, two = (36, 96, NZ), (18, 64, NZ), (16, 48, NZ)
    small, small1 = (18, 96, NZ), (10, 64, NZ)
    inner = call(
        inner_kernel, [small] * 8 + [small1] * 6, [(8, 96, NZ)], (cond, source, y0, y1), "inner", 16, 0, 10**10
    )
    down = call(
        down_kernel,
        [zero] * 6 + [one] * 6 + [two] * 2 + [(8, 8, NZ)] * 2,
        [zero] * 2 + [one] * 2 + [(14, 96, NZ), (17, 96, NZ), (8, 64, NZ)],
        (x0, x1, k0, k1, *inner),
        "down",
        24,
    )
    level0, level1 = down[:6], down[6:12]
    u1, c2, b2, p0, p1 = down[11:]
    y0, y1 = swaps("gy", p0, p1)
    p0, p1 = call(edge2_kernel, [(192, NZ)] * 2, [one, one, two, two], (u1, level1[4], c2, b2, y0, y1), "edges2", 16)
    x0, x1 = swaps("gx", p0, p1)
    far = swaps("gx", x1)
    *level2, u1, packed = call(
        level2_kernel,
        [two] * 6 + [one, (512, NZ)],
        [two] * 2 + [(2, 48, NZ)] * 3,
        (u1, c2, b2, y0, y1, x0, x1),
        "level2",
        16,
    )
    packed, far = lax.optimization_barrier((packed, far))
    whole = lax.all_to_all(packed, ("gx", "gy"), 0, 0, tiled=True)
    out, res = call(
        up_kernel,
        [block] * 2,
        [(6, 80, NZ), (6, 48, NZ), (8, 64, NZ), (12, 96, NZ)] + [two] * 2 + [one] * 3 + [zero] * 2,
        (whole, y0, y1, x1, far, *level2, *level1[:5], u1, *level0),
        "up",
        24,
    )
    return out, res


def solution(mesh):
    return jax.shard_map(
        per_device,
        mesh=mesh,
        in_specs=(P("gx", "gy", None), P("gx", "gy", None), P("gx", "gy", None), P("gy")),
        out_specs=(P("gx", "gy", None), P("gx", "gy", None)),
        check_vma=False,
    )
```

```python
import functools

import jax
import jax.numpy as jnp
from jax import lax
from jax.experimental import pallas as pl
from jax.experimental.pallas import tpu as pltpu
from jax.sharding import PartitionSpec as P

SWEEPS_COARSE = 16
DAMP = 0.8
KEEP = 1.0 - DAMP
H0 = 0.0002

NX, NY, NZ = 16, 64, 128
F32 = jnp.float32
VMEM = pl.BlockSpec(memory_space=pltpu.VMEM)
HBM = pl.BlockSpec(memory_space=pltpu.HBM)


def call(body, outs, scratch, args, name, vmem, hbm=0, cost=0):
    args = [pltpu.with_memory_space_constraint(a, pltpu.HBM) for a in args[:hbm]] + list(args[hbm:])
    return pl.pallas_call(
        body,
        out_shape=[jax.ShapeDtypeStruct(s, F32) for s in outs],
        in_specs=[HBM] * hbm + [VMEM] * (len(args) - hbm),
        out_specs=[VMEM] * len(outs),
        scratch_shapes=[pltpu.VMEM(s, F32) if isinstance(s, tuple) else s for s in scratch],
        compiler_params=pltpu.CompilerParams(vmem_limit_bytes=vmem * 2**20),
        name=name,
        cost_estimate=pl.CostEstimate(flops=cost, bytes_accessed=0, transcendentals=0) if cost else None,
    )(*args)


def recip(t):
    return 1.0 / t


def harmonic(a, b):
    return (2.0 * a) * b / jnp.maximum(a + b, 1e-30)


def lane(shape):
    return lax.broadcasted_iota(jnp.int32, shape, len(shape) - 1)


def lroll(v, shift):
    return pltpu.roll(v, shift % 128, v.ndim - 1)


def pair_lanes(v, s):
    first = (lane(v.shape) // s) % 2 == 0
    return v + jnp.where(first, lroll(v, -s), lroll(v, s))


def pack_lanes(tiles):
    n = len(tiles)
    out = tiles[0]
    for k in range(1, n):
        out = jnp.where(lane(out.shape) % n == k, tiles[k], out)
    return out


def unpack_lanes(p, n):
    at = lane(p.shape) % n
    moved = {d: p if d == 0 else lroll(p, -d) for d in range(1 - n, n)}
    tiles = []
    for k in range(n):
        out = moved[k]
        for m in range(1, n):
            out = jnp.where(at == m, moved[k - m], out)
        tiles.append(out)
    return tiles


def rows(lo, hi, body, unroll=8):
    whole = (hi - lo) // unroll

    def step(k, carry):
        for j in range(unroll):
            body(lo + k * unroll + j)
        return carry

    if whole > 1:
        lax.fori_loop(0, whole, step, 0)
        lo = lo + whole * unroll
    for x in range(lo, hi):
        body(x)


class Level:
    def __init__(self, depth, c, b, fx, fy, fz, w, ys, ye):
        self.h = H0 * 4.0**depth
        self.s = 2**depth
        self.c, self.b, self.fx, self.fy, self.fz, self.w = c, b, fx, fy, fz, w
        self.ys, self.n = ys, ye - ys

    def faces(self, lo, hi):
        here, above = pl.ds(self.ys, self.n), pl.ds(self.ys + 1, self.n)

        def body(x):
            c = self.c[x, here, :]
            twice, safe = c + c, c + 1e-30

            def face(other):
                return twice * other / (safe + other)

            self.fx[x, here, :] = face(self.c[x + 1, here, :])
            self.fy[x, here, :] = face(self.c[x, above, :])
            self.fz[x, here, :] = face(lroll(c, -self.s))

        rows(lo, hi, body)

    def weights(self, lo, hi, start=None):
        here, below = pl.ds(self.ys, self.n), pl.ds(self.ys - 1, self.n)

        def body(x):
            fz = self.fz[x, here, :]
            d = self.fx[x, here, :] + self.fx[x - 1, here, :]
            d = d + (self.fy[x, here, :] + self.fy[x, below, :])
            d = d + (fz + lroll(fz, self.s))
            w = DAMP * recip(self.h + d)
            self.w[x, here, :] = w
            if start is not None:
                start[x, here, :] = w * self.b[x, here, :]

        rows(lo, hi, body)

    def start(self, out, lo, hi):
        here = pl.ds(self.ys, self.n)

        def body(x):
            out[x, here, :] = self.w[x, here, :] * self.b[x, here, :]

        rows(lo, hi, body)

    def sweep(self, u, out, lo, hi):
        here = pl.ds(self.ys, self.n)
        above, below = pl.ds(self.ys + 1, self.n), pl.ds(self.ys - 1, self.n)

        def body(x):
            v = u[x, here, :]
            fz = self.fz[x, here, :]
            acc = fz * lroll(v, -self.s) + lroll(fz * v, self.s)
            acc = acc + (self.fx[x, here, :] * u[x + 1, here, :] + self.fx[x - 1, here, :] * u[x - 1, here, :])
            acc = acc + (self.fy[x, here, :] * u[x, above, :] + self.fy[x, below, :] * u[x, below, :])
            out[x, here, :] = KEEP * v + self.w[x, here, :] * (self.b[x, here, :] + acc)

        rows(lo, hi, body)

    def residual(self, u, x, y, n):
        here, above, below = pl.ds(y, n), pl.ds(y + 1, n), pl.ds(y - 1, n)
        v = u[x, here, :]
        flow = self.fz[x, here, :] * (lroll(v, -self.s) - v)
        r = self.b[x, here, :] - self.h * v
        r = r + (flow - lroll(flow, self.s))
        r = r + self.fx[x, here, :] * (u[x + 1, here, :] - v)
        r = r + self.fx[x - 1, here, :] * (u[x - 1, here, :] - v)
        r = r + self.fy[x, here, :] * (u[x, above, :] - v)
        return r + self.fy[x, below, :] * (u[x, below, :] - v)

    def halve(self, tmp, out, lo, hi, x_to, scale):
        half = tmp.shape[1] // 2

        def body(k):
            t = tmp[k, pl.ds(0, half, stride=2), :] + tmp[k, pl.ds(1, half, stride=2), :]
            out[x_to + k, pl.ds(8, half), :] = scale * pair_lanes(t, self.s)

        rows(lo, hi, body)

    def restrict(self, u, tmp, out, lo, hi, x_from, x_to):
        def body(k):
            x = x_from + 2 * k
            both = self.residual(u, x, self.ys, self.n) + self.residual(u, x + 1, self.ys, self.n)
            tmp[k, pl.ds(self.ys, self.n), :] = both

        rows(lo, hi, body, 4)
        self.halve(tmp, out, lo, hi, x_to, 0.5)

    def restrict_c(self, tmp, out, lo, hi, x_from, x_to):
        def body(k):
            x = x_from + 2 * k
            tmp[k] = self.c[x] + self.c[x + 1]

        rows(lo, hi, body)
        self.halve(tmp, out, lo, hi, x_to, 0.125)


def odd(axis):
    return lax.axis_index(axis) % 2


PARTS = 2


def stored(x):
    o = odd("gx")
    return o * (NX - 1) + (1 - 2 * o) * x


def begin_kernel(source, density, drag, porous, cond, rhs, ypack0, ypack1, dens, dra, src, por, sem, psem):
    o = odd("gy")
    at0 = pl.multiple_of((1 - o) * (NY - 8), 8)
    at1 = pl.multiple_of(o * (NY - 8), 8)
    part = NX // PARTS
    loads = []
    first = pltpu.make_async_copy(porous, por, psem)
    first.start()
    for k in range(PARTS):
        here = pl.ds(k * part, part)
        for j, (ref, dst) in enumerate(((density, dens), (drag, dra), (source, src))):
            loads.append(pltpu.make_async_copy(ref.at[here], dst.at[here], sem.at[j, k]))
            loads[-1].start()
    first.wait()
    line = jnp.broadcast_to(por[...].astype(F32)[None], (NY, NY))
    same = lax.broadcasted_iota(jnp.int32, (NY, NY), 0) == lax.broadcasted_iota(jnp.int32, (NY, NY), 1)
    mask = jnp.broadcast_to(jnp.sum(jnp.where(same, line, 0.0), axis=1, keepdims=True), (NY, NZ))
    for k in range(PARTS):
        for load in loads[3 * k : 3 * k + 3]:
            load.wait()
        for x in range(k * part, k * part + part):
            to = stored(x)
            cond[to] = recip(dens[x] * (1.0 + dra[x] * mask))
            rhs[to] = src[x]
            for pack, at in ((ypack0, at0), (ypack1, at1)):
                pack[to] = cond[to, pl.ds(at, 8), :]
                pack[NX + to] = src[x, pl.ds(at, 8), :]


HIGH_C, HIGH_B, LOW_C, LOW_B = 11, 10, 8, 6


def edge_kernel(cond, source, high, low):
    for d in range(HIGH_C):
        high[d] = cond[NX - 1 - d]
    for d in range(HIGH_B):
        high[HIGH_C + d] = source[NX - 1 - d]
    for d in range(LOW_C):
        low[d] = cond[d]
    for d in range(LOW_B):
        low[LOW_C + d] = source[d]


HIGH = (
    [(0, d, d - 1, 0) for d in (1, 2, 3, 4, 5, 6, 7)]
    + [(0, 9, 4, 2), (0, 8, 5, 3), (0, 10, 6, 1)]
    + [(1, d, d + 6, 0) for d in (1, 2, 3, 4, 5, 6)]
    + [(1, 7, 11, 3), (1, 8, 12, 2), (1, 9, 10, 1)]
)
LOW = [(0, 1, 0, 0), (0, 7, 0, 1), (0, 2, 1, 0), (0, 6, 1, 2), (0, 3, 2, 0), (0, 5, 2, 3), (0, 4, 3, 0)]
LOW += [(1, 5, 3, 1), (1, 1, 4, 0), (1, 3, 4, 3), (1, 2, 5, 0), (1, 4, 5, 2)]
HIGH_TILES, LOW_TILES = 13, 6


def turn(v, by):
    return v if by == 0 else pltpu.roll(v, by % 8, 0)


def corner_kernel(y0, y1, high, low):
    oy = odd("gy")
    at0 = pl.multiple_of((1 - oy) * 8, 8)
    at1 = pl.multiple_of(oy * 8, 8)
    row = lax.broadcasted_iota(jnp.int32, (8, NZ), 0)
    for pack, corners, count, side in ((high, HIGH, HIGH_TILES, 1), (low, LOW, LOW_TILES, 0)):
        for y, at, above in ((y0, at0, 1 - oy), (y1, at1, oy)):
            tiles = {}
            for field, d, t, by in corners:
                v = y[field * NX + (NX - d if side else d - 1)]
                if by == 0:
                    tiles[t] = v
                else:
                    under = jnp.where(row < by, turn(v, by), tiles[t])
                    over = jnp.where(row >= 8 - by, turn(v, -by), tiles[t])
                    tiles[t] = jnp.where(above == 1, over, under)
            for t in range(count):
                pack[t, pl.ds(at, 8), :] = tiles[t]


X0, Y0 = 9, 16
X1, Y1 = 5, 16
X2, Y2 = 6, 16


def levels_down(c, b, fx, fy, fz, w, c1, b1, gx_, gy_, gz_, gw_):
    top = Level(0, c, b, fx, fy, fz, w, 8, 88)
    return top, Level(1, c1, b1, gx_, gy_, gz_, gw_, 12, 52)


def inner_kernel(cond, source, y0, y1, c, b, fx, fy, fz, w, ua, ub, c1, b1, gx_, gy_, gz_, gw_, tmp):
    oy = odd("gy")
    at0 = pl.multiple_of(8 + (1 - oy) * (NY + 8), 8)
    at1 = pl.multiple_of(8 + oy * (NY + 8), 8)

    def own(x):
        c[1 + x, pl.ds(Y0, NY), :] = cond[x]
        c[1 + x, pl.ds(at0, 8), :] = y0[x]
        c[1 + x, pl.ds(at1, 8), :] = y1[x]
        b[1 + x, pl.ds(Y0, NY), :] = source[x]
        b[1 + x, pl.ds(at0, 8), :] = y0[NX + x]
        b[1 + x, pl.ds(at1, 8), :] = y1[NX + x]

    rows(0, NX, own)
    top, mid = levels_down(c, b, fx, fy, fz, w, c1, b1, gx_, gy_, gz_, gw_)
    top.faces(1, 17)
    top.weights(2, 16, ua)
    top.sweep(ua, ub, 3, 15)
    top.restrict_c(tmp, c1, 0, 8, 1, 1)
    top.restrict(ub, tmp, b1, 2, 6, 1, 1)
    mid.faces(1, 9)
    mid.weights(2, 8)


def down_kernel(
    x0, x1, k0, k1, c_in, b_in, fx_in, fy_in, fz_in, w_in, ua_in, ub_in, c1_in, b1_in, gx_in, gy_in, gz_in, gw_in,
    fx, fy, fz, w, b, ub, gx_, gy_, gz_, gw_, b1, u1, c2, b2, ypack0, ypack1,
    c, ua, c1, ga_, tmp, ctmp, tmp1,
):
    oy = odd("gy")
    here, here1 = pl.ds(8, 80), pl.ds(8, 48)
    sides = ((x0, k0, HIGH, HIGH_C, HIGH_B, X0 + NX - 1, 1), (x1, k1, LOW, LOW_C, LOW_B, X0, -1))
    for x, pack, corners, nc, nb, edge, sign in sides:
        for d in range(1, nc + 1):
            c[edge + sign * d, pl.ds(Y0, NY), :] = x[d - 1]
        for d in range(1, nb + 1):
            b[edge + sign * d, pl.ds(Y0, NY), :] = x[nc + d - 1]
        for field, d, t, by in corners:
            ref = (c, b)[field]
            ref[edge + sign * d, pl.ds(8, 8), :] = turn(pack[t, pl.ds(0, 8), :], -by)
            ref[edge + sign * d, pl.ds(80, 8), :] = turn(pack[t, pl.ds(8, 8), :], by)
    for x in (1, 16):
        c[x + 8, here, :] = c_in[x, here, :]
    for x in (2, 3, 14, 15):
        ua[x + 8, here, :] = ua_in[x, here, :]

    def fill(x):
        for ref, src in ((fx, fx_in), (fy, fy_in), (fz, fz_in), (w, w_in), (b, b_in), (ub, ub_in)):
            ref[x + 8, here, :] = src[x, here, :]

    rows(1, 17, fill)
    for x in range(1, 9):
        c1[x + 4, here1, :] = c1_in[x, here1, :]
        for ref, src in ((gx_, gx_in), (gy_, gy_in), (gz_, gz_in), (gw_, gw_in), (b1, b1_in)):
            ref[x + 4, here1, :] = src[x, here1, :]

    top, mid = levels_down(c, b, fx, fy, fz, w, c1, b1, gx_, gy_, gz_, gw_)
    top.faces(2, 9)
    top.faces(24, 35)
    top.weights(3, 10, ua)
    top.weights(24, 35, ua)
    top.sweep(ua, ub, 4, 11)
    top.sweep(ua, ub, 23, 34)
    top.restrict_c(ctmp, c1, 0, 4, 1, 1)
    top.restrict_c(ctmp, c1, 12, 17, 1, 1)
    top.restrict(ub, tmp, b1, 0, 4, 5, 3)
    top.restrict(ub, tmp, b1, 8, 14, 5, 3)

    mid.faces(1, 5)
    mid.faces(12, 17)
    mid.weights(2, 6)
    mid.weights(12, 17)
    mid.start(ga_, 3, 17)
    mid.sweep(ga_, u1, 4, 16)
    mid.restrict(u1, tmp1, b2, 0, 5, 5, X2)
    mid.restrict_c(tmp1, c2, 0, 8, 1, X2 - 2)

    e0 = Y1 + (1 - oy) * 28
    e1 = Y1 + oy * 28
    f0 = pl.multiple_of(Y2 + (1 - oy) * 8, 8)
    f1 = pl.multiple_of(Y2 + oy * 8, 8)
    for pack, e, f in ((ypack0, e0, f0), (ypack1, e1, f1)):
        for k in range(4):
            x = X1 + 2 * k
            pack[k, pl.ds(0, 4), :] = pack_lanes([u1[x + j, pl.ds(e, 4), :] for j in range(2)])
            pack[k, pl.ds(4, 4), :] = pack_lanes([b1[x + j, pl.ds(e, 4), :] for j in range(2)])
        for k in range(2):
            pack[4 + k] = pack_lanes([b2[X2 + min(4 * k + j, 4), pl.ds(f, 8), :] for j in range(4)])
            pack[6 + k] = pack_lanes([c2[X2 - 2 + 4 * k + j, pl.ds(f, 8), :] for j in range(4)])


def set_y1(ref, y0, y1, oy, part):
    a0 = Y1 - 4 + (1 - oy) * 36
    a1 = Y1 - 4 + oy * 36
    for y, a in ((y0, a0), (y1, a1)):
        for k in range(4):
            for j, v in enumerate(unpack_lanes(y[k], 2)):
                ref[X1 + 2 * k + j, pl.ds(a, 4), :] = v[4 * part : 4 * part + 4]


def set_y2(c2, b2, y0, y1, oy):
    a0 = pl.multiple_of(Y2 - 8 + (1 - oy) * 24, 8)
    a1 = pl.multiple_of(Y2 - 8 + oy * 24, 8)
    for y, a in ((y0, a0), (y1, a1)):
        for k in range(2):
            for j, v in enumerate(unpack_lanes(y[4 + k], 4)):
                if 4 * k + j < 5:
                    b2[X2 + 4 * k + j, pl.ds(a, 8), :] = v
            for j, v in enumerate(unpack_lanes(y[6 + k], 4)):
                c2[X2 - 2 + 4 * k + j, pl.ds(a, 8), :] = v


def copy_rows(pairs, lo, hi):
    def body(x):
        for src, dst in pairs:
            dst[x] = src[x]

    rows(lo, hi, body)


def edge2_kernel(u1_in, b1_in, c2_in, b2_in, y0, y1, high, low, u1, b1, c2, b2):
    oy = odd("gy")
    copy_rows([(u1_in, u1), (b1_in, b1)], X1, X1 + 8)
    copy_rows([(c2_in, c2)], X2 - 2, X2 + 6)
    copy_rows([(b2_in, b2)], X2, X2 + 5)
    set_y1(u1, y0, y1, oy, 0)
    set_y1(b1, y0, y1, oy, 1)
    set_y2(c2, b2, y0, y1, oy)
    for pack, edge1, edge2, sign in ((high, X1 + 7, X2 + 3, -1), (low, X1, X2, 1)):
        for k in range(2):
            t = [u1[edge1 + sign * (2 * k + j), pl.ds(12, 40), :] for j in range(2)]
            pack[pl.ds(k * 40, 40), :] = pack_lanes(t)
        t = [c2[edge2 + sign * d, pl.ds(10, 28), :] for d in range(6)]
        t += [b2[edge2 + sign * d, pl.ds(10, 28), :] for d in range(5 if sign == 1 else 4)]
        t += t[:1] * (12 - len(t))
        for k in range(3):
            pack[pl.ds(80 + k * 28, 28), :] = pack_lanes(t[4 * k : 4 * k + 4])
        for n, y in enumerate((12, 48)):
            t = [b1[edge1 + sign * j, pl.ds(y, 4), :] for j in range(2)]
            pack[pl.ds(164 + 4 * n, 4), :] = pack_lanes(t)
        t = [b1[edge1 + sign * 2, pl.ds(16 + 16 * j, 16), :] for j in range(2)]
        pack[pl.ds(172, 16), :] = pack_lanes(t)


def one_hot(shape, f):
    i = lax.broadcasted_iota(jnp.int32, shape, 0)
    j = lax.broadcasted_iota(jnp.int32, shape, 1)
    return jnp.where(f(i, j), 1.0, 0.0).astype(F32)


def halves(v):
    high = v.astype(jnp.bfloat16)
    return high, (v - high.astype(F32)).astype(jnp.bfloat16)


def pick_dot(a, b):
    a1, rest = halves(a)[0], a - halves(a)[0].astype(F32)
    a2, a3 = halves(rest)
    b = b.astype(jnp.bfloat16)
    return jnp.dot(jnp.concatenate([a1, a2, a3], 1), jnp.concatenate([b, b, b], 0), preferred_element_type=F32)


def split_dot(a, b):
    (a1, a2), (b1, b2) = halves(a), halves(b)
    return jnp.dot(jnp.concatenate([a1, a2, a1], 1), jnp.concatenate([b1, b1, b2], 0), preferred_element_type=F32)


def level2_kernel(
    u1_in, c2_in, b2_in, y0, y1, x0, x1,
    fx, fy, fz, w, b2, u2, u1, gather,
    c2, ua, tmp, b3, c3,
):
    ox, oy = odd("gx"), odd("gy")
    copy_rows([(u1_in, u1)], X1, X1 + 8)
    copy_rows([(c2_in, c2)], X2 - 2, X2 + 6)
    copy_rows([(b2_in, b2)], X2, X2 + 5)
    set_y1(u1, y0, y1, oy, 0)
    set_y2(c2, b2, y0, y1, oy)
    for pack, edge1, edge2, sign in ((x0, X1 + 7, X2 + 3, 1), (x1, X1, X2, -1)):
        for k in range(2):
            for j, v in enumerate(unpack_lanes(pack[pl.ds(k * 40, 40), :], 2)):
                u1[edge1 + sign * (2 * k + j + 1), pl.ds(12, 40), :] = v
        t = []
        for k in range(3):
            t += unpack_lanes(pack[pl.ds(80 + k * 28, 28), :], 4)
        for d in range(6):
            c2[edge2 + sign * (d + 1), pl.ds(10, 28), :] = t[d]
        for d in range(5 if sign == -1 else 4):
            b2[edge2 + sign * (d + 1), pl.ds(10, 28), :] = t[6 + d]

    low = Level(2, c2, b2, fx, fy, fz, w, 8, 40)
    low.faces(0, 15)
    low.weights(1, 15, ua)
    low.sweep(ua, u2, 2, 14)
    low.restrict(u2, tmp, b3, 0, 2, X2, 0)
    low.restrict_c(tmp, c3, 0, 2, X2, 0)
    both = jnp.concatenate(
        [b3[0, pl.ds(16, 8), :], b3[1, pl.ds(16, 8), :], c3[0, pl.ds(16, 8), :], c3[1, pl.ds(16, 8), :]], 0
    )
    spread = pick_dot(both, one_hot((NZ, NZ), lambda i, j: i == 8 * (j % 16)))
    shape = (8, NZ)
    mine = lane(shape) // 16 == lax.broadcasted_iota(jnp.int32, shape, 0)
    packed = [
        jnp.sum(jnp.where(mine, spread[8 * k : 8 * k + 8], 0.0), axis=0, keepdims=True) for k in range(4)
    ]
    packed = [jnp.where(ox == 1, packed[k ^ 1], packed[k]) for k in range(4)]
    eight = jnp.concatenate(packed + packed, 0)

    def body(k):
        gather[pl.ds(pl.multiple_of(8 * k, 8), 8), :] = eight

    rows(0, 64, body, 8)


class Whole:
    def __init__(self, depth, b, c):
        self.h = H0 * 4.0**depth
        self.s = 2 ** (depth - 3)
        self.st = 16 * self.s
        self.b = b
        n = c.shape[0]
        sub = lax.broadcasted_iota(jnp.int32, (1,) + c.shape[1:], 2)
        up = self.xp(c)
        end = jnp.where(sub == 7, 0.0, up[n - 1 :])
        up = jnp.concatenate([up[: n - 1], end], 0) if n > 1 else end
        self.fxp = harmonic(c, up)
        up = self.yp(c)
        last = up[:, 3:]
        last = jnp.where(lane(last.shape) >= 128 - self.st, 0.0, last)
        self.fyp = harmonic(c, jnp.concatenate([up[:, :3], last], 1))
        self.fzp = harmonic(c, self.zp(c))
        self.fxm, self.fym, self.fzm = self.xm(self.fxp), self.ym(self.fyp), self.zm(self.fzp)
        d = self.h + self.fxp + self.fxm + self.fyp + self.fym + self.fzp + self.fzm
        self.w = DAMP * recip(d)

    def xp(self, v):
        wrap = pltpu.roll(v[:1], 7, 2)
        return jnp.concatenate([v[1:], wrap], 0) if v.shape[0] > 1 else wrap

    def xm(self, v):
        n = v.shape[0]
        wrap = pltpu.roll(v[n - 1 :], 1, 2)
        return jnp.concatenate([wrap, v[: n - 1]], 0) if n > 1 else wrap

    def yp(self, v):
        w = v if self.st == 128 else lroll(v, -self.st)
        far = jnp.concatenate([w[:, 1:], w[:, :1]], 1)
        return far if self.st == 128 else jnp.where(lane(v.shape) < 128 - self.st, w, far)

    def ym(self, v):
        w = v if self.st == 128 else lroll(v, self.st)
        far = jnp.concatenate([w[:, 3:], w[:, :3]], 1)
        return far if self.st == 128 else jnp.where(lane(v.shape) >= self.st, w, far)

    def zp(self, v):
        s = self.s
        return jnp.where(lane(v.shape) % 16 < 16 - s, lroll(v, -s), lroll(v, 16 - s))

    def zm(self, v):
        s = self.s
        return self.zp(v) if s == 8 else jnp.where(lane(v.shape) % 16 >= s, lroll(v, s), lroll(v, s - 16))

    def flux(self, v):
        acc = self.fxp * self.xp(v) + self.fxm * self.xm(v)
        acc = acc + self.fyp * self.yp(v) + self.fym * self.ym(v)
        return acc + self.fzp * self.zp(v) + self.fzm * self.zm(v)

    def sweep(self, v):
        return KEEP * v + self.w * (self.b + self.flux(v))

    def residual(self, v):
        r = self.b - self.h * v
        r = r + self.fxp * (self.xp(v) - v) + self.fxm * (self.xm(v) - v)
        r = r + self.fyp * (self.yp(v) - v) + self.fym * (self.ym(v) - v)
        return r + self.fzp * (self.zp(v) - v) + self.fzm * (self.zm(v) - v)

    def coarse(self, v, scale):
        v = jnp.concatenate([v[2 * k : 2 * k + 1] + v[2 * k + 1 : 2 * k + 2] for k in range(v.shape[0] // 2)], 0)
        return scale * pair_lanes(pair_lanes(v, self.s), self.st)


def coarsest(level, g):
    def column(v):
        v = v.reshape(32, NZ)
        low = lane(v.shape) % 16 < 8
        return jnp.concatenate([jnp.where(low, v, lroll(v, 8)), jnp.where(low, lroll(v, -8), v)], 0)

    shape = (64, NZ)
    i, j = lax.broadcasted_iota(jnp.int32, shape, 0), lane(shape)

    def pad(v):
        return jnp.concatenate([v, jnp.zeros(shape, F32)], 0)

    m = jnp.where(i == j, KEEP, 0.0)
    w = level.w
    for coef, at in (
        (w * level.fxp, i + 1),
        (w * level.fxm, i - 1),
        (w * level.fyp, i + 8),
        (w * level.fym, i - 8),
        (w * (level.fzp + level.fzm), i ^ 32),
    ):
        m = m + jnp.where(j == at, column(coef), 0.0)
    total = m + jnp.where(i == j, 1.0, 0.0)
    for _ in range(3):
        m = split_dot(m, pad(m))
        total = total + split_dot(m, pad(total))
    u = split_dot(total, pad(column(g)))
    low = lane((32, NZ)) % 16 < 8
    return jnp.where(low, u[:32], u[32:]).reshape(g.shape)


def whole_cycle(depth, b, c):
    level = Whole(depth, b, c)
    v = level.w * b
    if depth == 6:
        return coarsest(level, v)
    v = level.sweep(v)
    below = whole_cycle(depth + 1, level.coarse(level.residual(v), 0.5), level.coarse(c, 0.125))
    v = v + jnp.concatenate([below[k // 2 : k // 2 + 1] for k in range(v.shape[0])], 0)
    return level.sweep(level.sweep(v))


def up_kernel(
    gather, y0, y1, x1, far,
    hx, hy, hz, hw, b2, u2,
    gx_, gy_, gz_, gw_, b1_in, u1,
    fx, fy, fz, w, b, u0,
    out, res,
    s3, e2, e1, e0, ha, hb, b1, ga_, gb_, ua, ub,
):
    ix, iy = lax.axis_index("gx"), lax.axis_index("gy")
    ox, oy = ix % 2, iy % 2
    low = Level(2, None, b2, hx, hy, hz, hw, 12, 36)
    wide = pl.ds(8, 32)
    low.start(ha, X2 + 6, X2 + 8)
    ha[X2 + 8, pl.ds(10, 28), :] = hw[X2 + 8, pl.ds(10, 28), :] * unpack_lanes(far[pl.ds(108, 28), :], 4)[2]
    low.sweep(ha, hb, X2 + 7, X2 + 8)

    def field(k):
        return jnp.stack(
            [
                jnp.stack([gather[pl.ds(xq * 16 + g * 4 + k + xl, 8, stride=64), :] for g in range(4)], 0)
                for xq in range(4)
                for xl in range(2)
            ],
            0,
        )

    u3 = whole_cycle(3, field(0), field(2))
    s3[...] = jnp.zeros(s3.shape, F32)
    for xlo in range(8):
        for g in range(4):
            s3[g + 1, pl.ds(8 + xlo, 8, stride=8), :] = u3[xlo, g]
    shape = (8, NZ)
    mine = lane(shape) // 16 == lax.broadcasted_iota(jnp.int32, shape, 0)
    tiles = []
    for k in range(6):
        for g in range(3):
            row = s3[iy + g, pl.ds(2 * ix + 6 + 5 * ox + (1 - 2 * ox) * k, 1), :]
            tiles.append(jnp.where(mine, jnp.broadcast_to(row, shape), 0.0))
    spread = pick_dot(jnp.concatenate(tiles, 0), one_hot((NZ, NZ), lambda i, j: i % 16 == j // 8))
    for k in range(6):
        t = spread[24 * k : 24 * k + 24]
        e2[k, pl.ds(0, 24, stride=2), :] = t
        e2[k, pl.ds(1, 24, stride=2), :] = t

    for x in range(2, 14):
        ha[x, wide, :] = (hb if x == X2 + 7 else u2)[x, wide, :] + e2[(x - 2) // 2, wide, :]
    low.sweep(ha, hb, 3, 13)
    low.sweep(hb, ha, 4, 12)

    def grow1(k):
        t = ha[4 + k, pl.ds(8, 32), :]
        e1[k, pl.ds(0, 32, stride=2), :] = t
        e1[k, pl.ds(1, 32, stride=2), :] = t

    rows(0, 8, grow1)

    copy_rows([(b1_in, b1)], 2, 18)
    set_y1(b1, y0, y1, oy, 1)
    for j, v in enumerate(unpack_lanes(x1[pl.ds(164, 8), :], 2)):
        b1[X1 - 1 - j, pl.ds(12, 4), :] = v[0:4]
        b1[X1 - 1 - j, pl.ds(48, 4), :] = v[4:8]
    for j, v in enumerate(unpack_lanes(x1[pl.ds(172, 16), :], 2)):
        b1[X1 - 3, pl.ds(16 + 16 * j, 16), :] = v

    def add1(k):
        for j in range(2):
            ga_[1 + 2 * k + j] = u1[1 + 2 * k + j] + e1[k]

    rows(0, 8, add1)
    mid = Level(1, None, b1, gx_, gy_, gz_, gw_, 12, 52)
    mid.sweep(ga_, gb_, 2, 16)
    mid.sweep(gb_, ga_, 3, 15)

    def grow0(k):
        t = ga_[3 + k, pl.ds(8, 48), :]
        e0[k, pl.ds(0, 48, stride=2), :] = t
        e0[k, pl.ds(1, 48, stride=2), :] = t

    def add0(k):
        for j in range(2):
            ua[5 + 2 * k + j] = u0[5 + 2 * k + j] + e0[k]

    rows(0, 12, grow0, 4)
    rows(0, 12, add0, 4)
    top = Level(0, None, b, fx, fy, fz, w, 12, 84)
    top.sweep(ua, ub, 7, 27)
    top.sweep(ub, ua, 8, 26)

    def finish(x):
        to = stored(x)
        out[to] = ua[X0 + x, pl.ds(Y0, NY), :]
        res[to] = top.residual(ua, X0 + x, Y0, NY)

    rows(0, NX, finish)


def swaps(axis, first, second=None):
    count = lax.axis_size(axis)

    def pairs(start):
        return [p for i in range(start, count - 1, 2) for p in ((i, i + 1), (i + 1, i))]

    if second is None:
        return lax.ppermute(first, axis, pairs(0))
    late = lax.ppermute(second, axis, pairs(1))
    return lax.ppermute(first, axis, pairs(0)), late


def per_device(source, density, drag, porous_rows):
    sems = [pltpu.SemaphoreType.DMA((3, PARTS)), pltpu.SemaphoreType.DMA]
    block = (NX, NY, NZ)
    cond, source, p0, p1 = call(
        begin_kernel,
        [block, block, (32, 8, NZ), (32, 8, NZ)],
        [block] * 3 + [pltpu.VMEM((NY,), jnp.int32)] + sems,
        (source, density, drag, porous_rows),
        "begin",
        16,
        4,
    )
    y0, y1 = swaps("gy", p0, p1)
    q0, q1 = call(edge_kernel, [(HIGH_C + HIGH_B, NY, NZ), (LOW_C + LOW_B, NY, NZ)], [], (cond, source), "edges", 16, 0, 10**9)
    x0, x1 = swaps("gx", q0, q1)
    p0, p1 = call(corner_kernel, [(HIGH_TILES, 16, NZ), (LOW_TILES, 16, NZ)], [], (y0, y1), "corners", 16)
    k0, k1 = swaps("gx", p0, p1)
    zero, one, two = (36, 96, NZ), (18, 64, NZ), (16, 48, NZ)
    small, small1 = (18, 96, NZ), (10, 64, NZ)
    inner = call(
        inner_kernel, [small] * 8 + [small1] * 6, [(8, 96, NZ)], (cond, source, y0, y1), "inner", 16, 0, 10**10
    )
    down = call(
        down_kernel,
        [zero] * 6 + [one] * 6 + [two] * 2 + [(8, 8, NZ)] * 2,
        [zero] * 2 + [one] * 2 + [(14, 96, NZ), (17, 96, NZ), (8, 64, NZ)],
        (x0, x1, k0, k1, *inner),
        "down",
        24,
    )
    level0, level1 = down[:6], down[6:12]
    u1, c2, b2, p0, p1 = down[11:]
    y0, y1 = swaps("gy", p0, p1)
    p0, p1 = call(edge2_kernel, [(192, NZ)] * 2, [one, one, two, two], (u1, level1[4], c2, b2, y0, y1), "edges2", 16)
    x0, x1 = swaps("gx", p0, p1)
    far = swaps("gx", x1)
    *level2, u1, packed = call(
        level2_kernel,
        [two] * 6 + [one, (512, NZ)],
        [two] * 2 + [(2, 48, NZ)] * 3,
        (u1, c2, b2, y0, y1, x0, x1),
        "level2",
        16,
    )
    packed, far = lax.optimization_barrier((packed, far))
    whole = lax.all_to_all(packed, ("gx", "gy"), 0, 0, tiled=True)
    out, res = call(
        up_kernel,
        [block] * 2,
        [(6, 80, NZ), (6, 48, NZ), (8, 64, NZ), (12, 96, NZ)] + [two] * 2 + [one] * 3 + [zero] * 2,
        (whole, y0, y1, x1, far, *level2, *level1[:5], u1, *level0),
        "up",
        24,
    )
    return out, res


def solution(mesh):
    return jax.shard_map(
        per_device,
        mesh=mesh,
        in_specs=(P("gx", "gy", None), P("gx", "gy", None), P("gx", "gy", None), P("gy")),
        out_specs=(P("gx", "gy", None), P("gx", "gy", None)),
        check_vma=False,
    )
```

```python
import functools

import jax
import jax.numpy as jnp
from jax import lax
from jax.experimental import pallas as pl
from jax.experimental.pallas import tpu as pltpu
from jax.sharding import PartitionSpec as P

SWEEPS_COARSE = 16
DAMP = 0.8
KEEP = 1.0 - DAMP
H0 = 0.0002

NX, NY, NZ = 16, 64, 128
F32 = jnp.float32
VMEM = pl.BlockSpec(memory_space=pltpu.VMEM)
HBM = pl.BlockSpec(memory_space=pltpu.HBM)


def call(body, outs, scratch, args, name, vmem, hbm=0, cost=0):
    args = [pltpu.with_memory_space_constraint(a, pltpu.HBM) for a in args[:hbm]] + list(args[hbm:])
    return pl.pallas_call(
        body,
        out_shape=[jax.ShapeDtypeStruct(s, F32) for s in outs],
        in_specs=[HBM] * hbm + [VMEM] * (len(args) - hbm),
        out_specs=[VMEM] * len(outs),
        scratch_shapes=[pltpu.VMEM(s, F32) if isinstance(s, tuple) else s for s in scratch],
        compiler_params=pltpu.CompilerParams(vmem_limit_bytes=vmem * 2**20),
        name=name,
        cost_estimate=pl.CostEstimate(flops=cost, bytes_accessed=0, transcendentals=0) if cost else None,
    )(*args)


def recip(t):
    return 1.0 / t


def harmonic(a, b):
    return (2.0 * a) * b / jnp.maximum(a + b, 1e-30)


def lane(shape):
    return lax.broadcasted_iota(jnp.int32, shape, len(shape) - 1)


def lroll(v, shift):
    return pltpu.roll(v, shift % 128, v.ndim - 1)


def pair_lanes(v, s):
    first = (lane(v.shape) // s) % 2 == 0
    return v + jnp.where(first, lroll(v, -s), lroll(v, s))


def pack_lanes(tiles):
    n = len(tiles)
    out = tiles[0]
    for k in range(1, n):
        out = jnp.where(lane(out.shape) % n == k, tiles[k], out)
    return out


def unpack_lanes(p, n):
    at = lane(p.shape) % n
    moved = {d: p if d == 0 else lroll(p, -d) for d in range(1 - n, n)}
    tiles = []
    for k in range(n):
        out = moved[k]
        for m in range(1, n):
            out = jnp.where(at == m, moved[k - m], out)
        tiles.append(out)
    return tiles


def rows(lo, hi, body, unroll=8):
    whole = (hi - lo) // unroll

    def step(k, carry):
        for j in range(unroll):
            body(lo + k * unroll + j)
        return carry

    if whole > 1:
        lax.fori_loop(0, whole, step, 0)
        lo = lo + whole * unroll
    for x in range(lo, hi):
        body(x)


class Level:
    def __init__(self, depth, c, b, fx, fy, fz, w, ys, ye):
        self.h = H0 * 4.0**depth
        self.s = 2**depth
        self.c, self.b, self.fx, self.fy, self.fz, self.w = c, b, fx, fy, fz, w
        self.ys, self.n = ys, ye - ys

    def faces(self, lo, hi):
        here, above = pl.ds(self.ys, self.n), pl.ds(self.ys + 1, self.n)

        def body(x):
            c = self.c[x, here, :]
            twice, safe = c + c, c + 1e-30

            def face(other):
                return twice * other / (safe + other)

            self.fx[x, here, :] = face(self.c[x + 1, here, :])
            self.fy[x, here, :] = face(self.c[x, above, :])
            self.fz[x, here, :] = face(lroll(c, -self.s))

        rows(lo, hi, body)

    def weights(self, lo, hi, start=None):
        here, below = pl.ds(self.ys, self.n), pl.ds(self.ys - 1, self.n)

        def body(x):
            fz = self.fz[x, here, :]
            d = self.fx[x, here, :] + self.fx[x - 1, here, :]
            d = d + (self.fy[x, here, :] + self.fy[x, below, :])
            d = d + (fz + lroll(fz, self.s))
            w = DAMP * recip(self.h + d)
            self.w[x, here, :] = w
            if start is not None:
                start[x, here, :] = w * self.b[x, here, :]

        rows(lo, hi, body)

    def start(self, out, lo, hi):
        here = pl.ds(self.ys, self.n)

        def body(x):
            out[x, here, :] = self.w[x, here, :] * self.b[x, here, :]

        rows(lo, hi, body)

    def sweep(self, u, out, lo, hi):
        here = pl.ds(self.ys, self.n)
        above, below = pl.ds(self.ys + 1, self.n), pl.ds(self.ys - 1, self.n)

        def body(x):
            v = u[x, here, :]
            fz = self.fz[x, here, :]
            acc = fz * lroll(v, -self.s) + lroll(fz * v, self.s)
            acc = acc + (self.fx[x, here, :] * u[x + 1, here, :] + self.fx[x - 1, here, :] * u[x - 1, here, :])
            acc = acc + (self.fy[x, here, :] * u[x, above, :] + self.fy[x, below, :] * u[x, below, :])
            out[x, here, :] = KEEP * v + self.w[x, here, :] * (self.b[x, here, :] + acc)

        rows(lo, hi, body)

    def residual(self, u, x, y, n):
        here, above, below = pl.ds(y, n), pl.ds(y + 1, n), pl.ds(y - 1, n)
        v = u[x, here, :]
        flow = self.fz[x, here, :] * (lroll(v, -self.s) - v)
        r = self.b[x, here, :] - self.h * v
        r = r + (flow - lroll(flow, self.s))
        r = r + self.fx[x, here, :] * (u[x + 1, here, :] - v)
        r = r + self.fx[x - 1, here, :] * (u[x - 1, here, :] - v)
        r = r + self.fy[x, here, :] * (u[x, above, :] - v)
        return r + self.fy[x, below, :] * (u[x, below, :] - v)

    def halve(self, tmp, out, lo, hi, x_to, scale):
        half = tmp.shape[1] // 2

        def body(k):
            t = tmp[k, pl.ds(0, half, stride=2), :] + tmp[k, pl.ds(1, half, stride=2), :]
            out[x_to + k, pl.ds(8, half), :] = scale * pair_lanes(t, self.s)

        rows(lo, hi, body)

    def restrict(self, u, tmp, out, lo, hi, x_from, x_to):
        def body(k):
            x = x_from + 2 * k
            both = self.residual(u, x, self.ys, self.n) + self.residual(u, x + 1, self.ys, self.n)
            tmp[k, pl.ds(self.ys, self.n), :] = both

        rows(lo, hi, body, 4)
        self.halve(tmp, out, lo, hi, x_to, 0.5)

    def restrict_c(self, tmp, out, lo, hi, x_from, x_to):
        def body(k):
            x = x_from + 2 * k
            tmp[k] = self.c[x] + self.c[x + 1]

        rows(lo, hi, body)
        self.halve(tmp, out, lo, hi, x_to, 0.125)


def odd(axis):
    return lax.axis_index(axis) % 2


PARTS = 2


def stored(x):
    o = odd("gx")
    return o * (NX - 1) + (1 - 2 * o) * x


def begin_kernel(source, density, drag, porous, cond, rhs, ypack0, ypack1, dens, dra, src, por, sem, psem):
    o = odd("gy")
    at0 = pl.multiple_of((1 - o) * (NY - 8), 8)
    at1 = pl.multiple_of(o * (NY - 8), 8)
    part = NX // PARTS
    loads = []
    first = pltpu.make_async_copy(porous, por, psem)
    first.start()
    for k in range(PARTS):
        here = pl.ds(k * part, part)
        for j, (ref, dst) in enumerate(((density, dens), (drag, dra), (source, src))):
            loads.append(pltpu.make_async_copy(ref.at[here], dst.at[here], sem.at[j, k]))
            loads[-1].start()
    first.wait()
    line = jnp.broadcast_to(por[...].astype(F32)[None], (NY, NY))
    same = lax.broadcasted_iota(jnp.int32, (NY, NY), 0) == lax.broadcasted_iota(jnp.int32, (NY, NY), 1)
    mask = jnp.broadcast_to(jnp.sum(jnp.where(same, line, 0.0), axis=1, keepdims=True), (NY, NZ))
    for k in range(PARTS):
        for load in loads[3 * k : 3 * k + 3]:
            load.wait()
        for x in range(k * part, k * part + part):
            to = stored(x)
            cond[to] = recip(dens[x] * (1.0 + dra[x] * mask))
            rhs[to] = src[x]
            for pack, at in ((ypack0, at0), (ypack1, at1)):
                pack[to] = cond[to, pl.ds(at, 8), :]
                pack[NX + to] = src[x, pl.ds(at, 8), :]


HIGH_C, HIGH_B, LOW_C, LOW_B = 11, 10, 8, 6


def edge_kernel(cond, source, high, low):
    for d in range(HIGH_C):
        high[d] = cond[NX - 1 - d]
    for d in range(HIGH_B):
        high[HIGH_C + d] = source[NX - 1 - d]
    for d in range(LOW_C):
        low[d] = cond[d]
    for d in range(LOW_B):
        low[LOW_C + d] = source[d]


HIGH = (
    [(0, d, d - 1, 0) for d in (1, 2, 3, 4, 5, 6, 7)]
    + [(0, 9, 4, 2), (0, 8, 5, 3), (0, 10, 6, 1)]
    + [(1, d, d + 6, 0) for d in (1, 2, 3, 4, 5, 6)]
    + [(1, 7, 11, 3), (1, 8, 12, 2), (1, 9, 10, 1)]
)
LOW = [(0, 1, 0, 0), (0, 7, 0, 1), (0, 2, 1, 0), (0, 6, 1, 2), (0, 3, 2, 0), (0, 5, 2, 3), (0, 4, 3, 0)]
LOW += [(1, 5, 3, 1), (1, 1, 4, 0), (1, 3, 4, 3), (1, 2, 5, 0), (1, 4, 5, 2)]
HIGH_TILES, LOW_TILES = 13, 6


def turn(v, by):
    return v if by == 0 else pltpu.roll(v, by % 8, 0)


def corner_kernel(y0, y1, high, low):
    oy = odd("gy")
    at0 = pl.multiple_of((1 - oy) * 8, 8)
    at1 = pl.multiple_of(oy * 8, 8)
    row = lax.broadcasted_iota(jnp.int32, (8, NZ), 0)
    for pack, corners, count, side in ((high, HIGH, HIGH_TILES, 1), (low, LOW, LOW_TILES, 0)):
        for y, at, above in ((y0, at0, 1 - oy), (y1, at1, oy)):
            tiles = {}
            for field, d, t, by in corners:
                v = y[field * NX + (NX - d if side else d - 1)]
                if by == 0:
                    tiles[t] = v
                else:
                    under = jnp.where(row < by, turn(v, by), tiles[t])
                    over = jnp.where(row >= 8 - by, turn(v, -by), tiles[t])
                    tiles[t] = jnp.where(above == 1, over, under)
            for t in range(count):
                pack[t, pl.ds(at, 8), :] = tiles[t]


X0, Y0 = 9, 16
X1, Y1 = 5, 16
X2, Y2 = 6, 16


def levels_down(c, b, fx, fy, fz, w, c1, b1, gx_, gy_, gz_, gw_):
    top = Level(0, c, b, fx, fy, fz, w, 8, 88)
    return top, Level(1, c1, b1, gx_, gy_, gz_, gw_, 12, 52)


def inner_kernel(cond, source, y0, y1, c, b, fx, fy, fz, w, ua, ub, c1, b1, gx_, gy_, gz_, gw_, tmp):
    oy = odd("gy")
    at0 = pl.multiple_of(8 + (1 - oy) * (NY + 8), 8)
    at1 = pl.multiple_of(8 + oy * (NY + 8), 8)

    def own(x):
        c[1 + x, pl.ds(Y0, NY), :] = cond[x]
        c[1 + x, pl.ds(at0, 8), :] = y0[x]
        c[1 + x, pl.ds(at1, 8), :] = y1[x]
        b[1 + x, pl.ds(Y0, NY), :] = source[x]
        b[1 + x, pl.ds(at0, 8), :] = y0[NX + x]
        b[1 + x, pl.ds(at1, 8), :] = y1[NX + x]

    rows(0, NX, own)
    top, mid = levels_down(c, b, fx, fy, fz, w, c1, b1, gx_, gy_, gz_, gw_)
    top.faces(1, 17)
    top.weights(2, 16, ua)
    top.sweep(ua, ub, 3, 15)
    top.restrict_c(tmp, c1, 0, 8, 1, 1)
    top.restrict(ub, tmp, b1, 2, 6, 1, 1)
    mid.faces(1, 9)
    mid.weights(2, 8)


def down_kernel(
    x0, x1, k0, k1, c_in, b_in, fx_in, fy_in, fz_in, w_in, ua_in, ub_in, c1_in, b1_in, gx_in, gy_in, gz_in, gw_in,
    fx, fy, fz, w, b, ub, gx_, gy_, gz_, gw_, b1, u1, c2, b2, ypack0, ypack1,
    c, ua, c1, ga_, tmp, ctmp, tmp1,
):
    oy = odd("gy")
    here, here1 = pl.ds(8, 80), pl.ds(8, 48)
    sides = ((x0, k0, HIGH, HIGH_C, HIGH_B, X0 + NX - 1, 1), (x1, k1, LOW, LOW_C, LOW_B, X0, -1))
    for x, pack, corners, nc, nb, edge, sign in sides:
        for d in range(1, nc + 1):
            c[edge + sign * d, pl.ds(Y0, NY), :] = x[d - 1]
        for d in range(1, nb + 1):
            b[edge + sign * d, pl.ds(Y0, NY), :] = x[nc + d - 1]
        for field, d, t, by in corners:
            ref = (c, b)[field]
            ref[edge + sign * d, pl.ds(8, 8), :] = turn(pack[t, pl.ds(0, 8), :], -by)
            ref[edge + sign * d, pl.ds(80, 8), :] = turn(pack[t, pl.ds(8, 8), :], by)
    for x in (1, 16):
        c[x + 8, here, :] = c_in[x, here, :]
    for x in (2, 3, 14, 15):
        ua[x + 8, here, :] = ua_in[x, here, :]

    def fill(x):
        for ref, src in ((fx, fx_in), (fy, fy_in), (fz, fz_in), (w, w_in), (b, b_in), (ub, ub_in)):
            ref[x + 8, here, :] = src[x, here, :]

    rows(1, 17, fill)
    for x in range(1, 9):
        c1[x + 4, here1, :] = c1_in[x, here1, :]
        for ref, src in ((gx_, gx_in), (gy_, gy_in), (gz_, gz_in), (gw_, gw_in), (b1, b1_in)):
            ref[x + 4, here1, :] = src[x, here1, :]

    top, mid = levels_down(c, b, fx, fy, fz, w, c1, b1, gx_, gy_, gz_, gw_)
    top.faces(2, 9)
    top.faces(24, 35)
    top.weights(3, 10, ua)
    top.weights(24, 35, ua)
    top.sweep(ua, ub, 4, 11)
    top.sweep(ua, ub, 23, 34)
    top.restrict_c(ctmp, c1, 0, 4, 1, 1)
    top.restrict_c(ctmp, c1, 12, 17, 1, 1)
    top.restrict(ub, tmp, b1, 0, 4, 5, 3)
    top.restrict(ub, tmp, b1, 8, 14, 5, 3)

    mid.faces(1, 5)
    mid.faces(12, 17)
    mid.weights(2, 6)
    mid.weights(12, 17)
    mid.start(ga_, 3, 17)
    mid.sweep(ga_, u1, 4, 16)
    mid.restrict(u1, tmp1, b2, 0, 5, 5, X2)
    mid.restrict_c(tmp1, c2, 0, 8, 1, X2 - 2)

    e0 = Y1 + (1 - oy) * 28
    e1 = Y1 + oy * 28
    f0 = pl.multiple_of(Y2 + (1 - oy) * 8, 8)
    f1 = pl.multiple_of(Y2 + oy * 8, 8)
    for pack, e, f in ((ypack0, e0, f0), (ypack1, e1, f1)):
        for k in range(4):
            x = X1 + 2 * k
            pack[k, pl.ds(0, 4), :] = pack_lanes([u1[x + j, pl.ds(e, 4), :] for j in range(2)])
            pack[k, pl.ds(4, 4), :] = pack_lanes([b1[x + j, pl.ds(e, 4), :] for j in range(2)])
        for k in range(2):
            pack[4 + k] = pack_lanes([b2[X2 + min(4 * k + j, 4), pl.ds(f, 8), :] for j in range(4)])
            pack[6 + k] = pack_lanes([c2[X2 - 2 + 4 * k + j, pl.ds(f, 8), :] for j in range(4)])


def set_y1(ref, y0, y1, oy, part):
    a0 = Y1 - 4 + (1 - oy) * 36
    a1 = Y1 - 4 + oy * 36
    for y, a in ((y0, a0), (y1, a1)):
        for k in range(4):
            for j, v in enumerate(unpack_lanes(y[k], 2)):
                ref[X1 + 2 * k + j, pl.ds(a, 4), :] = v[4 * part : 4 * part + 4]


def set_y2(c2, b2, y0, y1, oy):
    a0 = pl.multiple_of(Y2 - 8 + (1 - oy) * 24, 8)
    a1 = pl.multiple_of(Y2 - 8 + oy * 24, 8)
    for y, a in ((y0, a0), (y1, a1)):
        for k in range(2):
            for j, v in enumerate(unpack_lanes(y[4 + k], 4)):
                if 4 * k + j < 5:
                    b2[X2 + 4 * k + j, pl.ds(a, 8), :] = v
            for j, v in enumerate(unpack_lanes(y[6 + k], 4)):
                c2[X2 - 2 + 4 * k + j, pl.ds(a, 8), :] = v


def copy_rows(pairs, lo, hi):
    def body(x):
        for src, dst in pairs:
            dst[x] = src[x]

    rows(lo, hi, body)


def edge2_kernel(u1_in, b1_in, c2_in, b2_in, y0, y1, high, low, u1, b1, c2, b2):
    oy = odd("gy")
    copy_rows([(u1_in, u1), (b1_in, b1)], X1, X1 + 8)
    copy_rows([(c2_in, c2)], X2 - 2, X2 + 6)
    copy_rows([(b2_in, b2)], X2, X2 + 5)
    set_y1(u1, y0, y1, oy, 0)
    set_y1(b1, y0, y1, oy, 1)
    set_y2(c2, b2, y0, y1, oy)
    for pack, edge1, edge2, sign in ((high, X1 + 7, X2 + 3, -1), (low, X1, X2, 1)):
        for k in range(2):
            t = [u1[edge1 + sign * (2 * k + j), pl.ds(12, 40), :] for j in range(2)]
            pack[pl.ds(k * 40, 40), :] = pack_lanes(t)
        t = [c2[edge2 + sign * d, pl.ds(10, 28), :] for d in range(6)]
        t += [b2[edge2 + sign * d, pl.ds(10, 28), :] for d in range(5 if sign == 1 else 4)]
        t += t[:1] * (12 - len(t))
        for k in range(3):
            pack[pl.ds(80 + k * 28, 28), :] = pack_lanes(t[4 * k : 4 * k + 4])
        for n, y in enumerate((12, 48)):
            t = [b1[edge1 + sign * j, pl.ds(y, 4), :] for j in range(2)]
            pack[pl.ds(164 + 4 * n, 4), :] = pack_lanes(t)
        t = [b1[edge1 + sign * 2, pl.ds(16 + 16 * j, 16), :] for j in range(2)]
        pack[pl.ds(172, 16), :] = pack_lanes(t)


def one_hot(shape, f):
    i = lax.broadcasted_iota(jnp.int32, shape, 0)
    j = lax.broadcasted_iota(jnp.int32, shape, 1)
    return jnp.where(f(i, j), 1.0, 0.0).astype(F32)


def halves(v):
    high = v.astype(jnp.bfloat16)
    return high, (v - high.astype(F32)).astype(jnp.bfloat16)


def pick_dot(a, b):
    a1, rest = halves(a)[0], a - halves(a)[0].astype(F32)
    a2, a3 = halves(rest)
    b = b.astype(jnp.bfloat16)
    return jnp.dot(jnp.concatenate([a1, a2, a3], 1), jnp.concatenate([b, b, b], 0), preferred_element_type=F32)


def split_dot(a, b):
    (a1, a2), (b1, b2) = halves(a), halves(b)
    return jnp.dot(jnp.concatenate([a1, a2, a1], 1), jnp.concatenate([b1, b1, b2], 0), preferred_element_type=F32)


def level2_kernel(
    u1_in, c2_in, b2_in, y0, y1, x0, x1,
    fx, fy, fz, w, b2, u2, u1, gather,
    c2, ua, tmp, b3, c3,
):
    ox, oy = odd("gx"), odd("gy")
    copy_rows([(u1_in, u1)], X1, X1 + 8)
    copy_rows([(c2_in, c2)], X2 - 2, X2 + 6)
    copy_rows([(b2_in, b2)], X2, X2 + 5)
    set_y1(u1, y0, y1, oy, 0)
    set_y2(c2, b2, y0, y1, oy)
    for pack, edge1, edge2, sign in ((x0, X1 + 7, X2 + 3, 1), (x1, X1, X2, -1)):
        for k in range(2):
            for j, v in enumerate(unpack_lanes(pack[pl.ds(k * 40, 40), :], 2)):
                u1[edge1 + sign * (2 * k + j + 1), pl.ds(12, 40), :] = v
        t = []
        for k in range(3):
            t += unpack_lanes(pack[pl.ds(80 + k * 28, 28), :], 4)
        for d in range(6):
            c2[edge2 + sign * (d + 1), pl.ds(10, 28), :] = t[d]
        for d in range(5 if sign == -1 else 4):
            b2[edge2 + sign * (d + 1), pl.ds(10, 28), :] = t[6 + d]

    low = Level(2, c2, b2, fx, fy, fz, w, 8, 40)
    low.faces(0, 15)
    low.weights(1, 15, ua)
    low.sweep(ua, u2, 2, 14)
    low.restrict(u2, tmp, b3, 0, 2, X2, 0)
    low.restrict_c(tmp, c3, 0, 2, X2, 0)
    both = jnp.concatenate(
        [b3[0, pl.ds(16, 8), :], b3[1, pl.ds(16, 8), :], c3[0, pl.ds(16, 8), :], c3[1, pl.ds(16, 8), :]], 0
    )
    spread = pick_dot(both, one_hot((NZ, NZ), lambda i, j: i == 8 * (j % 16)))
    shape = (8, NZ)
    mine = lane(shape) // 16 == lax.broadcasted_iota(jnp.int32, shape, 0)
    packed = [
        jnp.sum(jnp.where(mine, spread[8 * k : 8 * k + 8], 0.0), axis=0, keepdims=True) for k in range(4)
    ]
    packed = [jnp.where(ox == 1, packed[k ^ 1], packed[k]) for k in range(4)]
    eight = jnp.concatenate(packed + packed, 0)

    def body(k):
        gather[pl.ds(pl.multiple_of(8 * k, 8), 8), :] = eight

    rows(0, 64, body, 8)


class Whole:
    def __init__(self, depth, b, c):
        self.h = H0 * 4.0**depth
        self.s = 2 ** (depth - 3)
        self.st = 16 * self.s
        self.b = b
        n = c.shape[0]
        sub = lax.broadcasted_iota(jnp.int32, (1,) + c.shape[1:], 2)
        up = self.xp(c)
        end = jnp.where(sub == 7, 0.0, up[n - 1 :])
        up = jnp.concatenate([up[: n - 1], end], 0) if n > 1 else end
        self.fxp = harmonic(c, up)
        up = self.yp(c)
        last = up[:, 3:]
        last = jnp.where(lane(last.shape) >= 128 - self.st, 0.0, last)
        self.fyp = harmonic(c, jnp.concatenate([up[:, :3], last], 1))
        self.fzp = harmonic(c, self.zp(c))
        self.fxm, self.fym, self.fzm = self.xm(self.fxp), self.ym(self.fyp), self.zm(self.fzp)
        d = self.h + self.fxp + self.fxm + self.fyp + self.fym + self.fzp + self.fzm
        self.w = DAMP * recip(d)

    def xp(self, v):
        wrap = pltpu.roll(v[:1], 7, 2)
        return jnp.concatenate([v[1:], wrap], 0) if v.shape[0] > 1 else wrap

    def xm(self, v):
        n = v.shape[0]
        wrap = pltpu.roll(v[n - 1 :], 1, 2)
        return jnp.concatenate([wrap, v[: n - 1]], 0) if n > 1 else wrap

    def yp(self, v):
        w = v if self.st == 128 else lroll(v, -self.st)
        far = jnp.concatenate([w[:, 1:], w[:, :1]], 1)
        return far if self.st == 128 else jnp.where(lane(v.shape) < 128 - self.st, w, far)

    def ym(self, v):
        w = v if self.st == 128 else lroll(v, self.st)
        far = jnp.concatenate([w[:, 3:], w[:, :3]], 1)
        return far if self.st == 128 else jnp.where(lane(v.shape) >= self.st, w, far)

    def zp(self, v):
        s = self.s
        return jnp.where(lane(v.shape) % 16 < 16 - s, lroll(v, -s), lroll(v, 16 - s))

    def zm(self, v):
        s = self.s
        return self.zp(v) if s == 8 else jnp.where(lane(v.shape) % 16 >= s, lroll(v, s), lroll(v, s - 16))

    def flux(self, v):
        acc = self.fxp * self.xp(v) + self.fxm * self.xm(v)
        acc = acc + self.fyp * self.yp(v) + self.fym * self.ym(v)
        return acc + self.fzp * self.zp(v) + self.fzm * self.zm(v)

    def sweep(self, v):
        return KEEP * v + self.w * (self.b + self.flux(v))

    def residual(self, v):
        r = self.b - self.h * v
        r = r + self.fxp * (self.xp(v) - v) + self.fxm * (self.xm(v) - v)
        r = r + self.fyp * (self.yp(v) - v) + self.fym * (self.ym(v) - v)
        return r + self.fzp * (self.zp(v) - v) + self.fzm * (self.zm(v) - v)

    def coarse(self, v, scale):
        v = jnp.concatenate([v[2 * k : 2 * k + 1] + v[2 * k + 1 : 2 * k + 2] for k in range(v.shape[0] // 2)], 0)
        return scale * pair_lanes(pair_lanes(v, self.s), self.st)


def coarsest(level, g):
    def column(v):
        v = v.reshape(32, NZ)
        low = lane(v.shape) % 16 < 8
        return jnp.concatenate([jnp.where(low, v, lroll(v, 8)), jnp.where(low, lroll(v, -8), v)], 0)

    shape = (64, NZ)
    i, j = lax.broadcasted_iota(jnp.int32, shape, 0), lane(shape)

    def pad(v):
        return jnp.concatenate([v, jnp.zeros(shape, F32)], 0)

    m = jnp.where(i == j, KEEP, 0.0)
    w = level.w
    for coef, at in (
        (w * level.fxp, i + 1),
        (w * level.fxm, i - 1),
        (w * level.fyp, i + 8),
        (w * level.fym, i - 8),
        (w * (level.fzp + level.fzm), i ^ 32),
    ):
        m = m + jnp.where(j == at, column(coef), 0.0)
    total = m + jnp.where(i == j, 1.0, 0.0)
    for _ in range(3):
        m = split_dot(m, pad(m))
        total = total + split_dot(m, pad(total))
    u = split_dot(total, pad(column(g)))
    low = lane((32, NZ)) % 16 < 8
    return jnp.where(low, u[:32], u[32:]).reshape(g.shape)


def whole_cycle(depth, b, c):
    level = Whole(depth, b, c)
    v = level.w * b
    if depth == 6:
        return coarsest(level, v)
    v = level.sweep(v)
    below = whole_cycle(depth + 1, level.coarse(level.residual(v), 0.5), level.coarse(c, 0.125))
    v = v + jnp.concatenate([below[k // 2 : k // 2 + 1] for k in range(v.shape[0])], 0)
    return level.sweep(level.sweep(v))


def up_kernel(
    gather, y0, y1, x1, far,
    hx, hy, hz, hw, b2, u2,
    gx_, gy_, gz_, gw_, b1_in, u1,
    fx, fy, fz, w, b, u0,
    out, res,
    s3, e2, e1, e0, ha, hb, b1, ga_, gb_, ua, ub,
):
    ix, iy = lax.axis_index("gx"), lax.axis_index("gy")
    ox, oy = ix % 2, iy % 2
    low = Level(2, None, b2, hx, hy, hz, hw, 12, 36)
    wide = pl.ds(8, 32)
    low.start(ha, X2 + 6, X2 + 8)
    ha[X2 + 8, pl.ds(10, 28), :] = hw[X2 + 8, pl.ds(10, 28), :] * unpack_lanes(far[pl.ds(108, 28), :], 4)[2]
    low.sweep(ha, hb, X2 + 7, X2 + 8)

    def field(k):
        return jnp.stack(
            [
                jnp.stack([gather[pl.ds(xq * 16 + g * 4 + k + xl, 8, stride=64), :] for g in range(4)], 0)
                for xq in range(4)
                for xl in range(2)
            ],
            0,
        )

    u3 = whole_cycle(3, field(0), field(2))
    s3[...] = jnp.zeros(s3.shape, F32)
    for xlo in range(8):
        for g in range(4):
            s3[g + 1, pl.ds(8 + xlo, 8, stride=8), :] = u3[xlo, g]
    shape = (8, NZ)
    mine = lane(shape) // 16 == lax.broadcasted_iota(jnp.int32, shape, 0)
    tiles = []
    for k in range(6):
        for g in range(3):
            row = s3[iy + g, pl.ds(2 * ix + 6 + 5 * ox + (1 - 2 * ox) * k, 1), :]
            tiles.append(jnp.where(mine, jnp.broadcast_to(row, shape), 0.0))
    spread = pick_dot(jnp.concatenate(tiles, 0), one_hot((NZ, NZ), lambda i, j: i % 16 == j // 8))
    for k in range(6):
        t = spread[24 * k : 24 * k + 24]
        e2[k, pl.ds(0, 24, stride=2), :] = t
        e2[k, pl.ds(1, 24, stride=2), :] = t

    for x in range(2, 14):
        ha[x, wide, :] = (hb if x == X2 + 7 else u2)[x, wide, :] + e2[(x - 2) // 2, wide, :]
    low.sweep(ha, hb, 3, 13)
    low.sweep(hb, ha, 4, 12)

    def grow1(k):
        t = ha[4 + k, pl.ds(8, 32), :]
        e1[k, pl.ds(0, 32, stride=2), :] = t
        e1[k, pl.ds(1, 32, stride=2), :] = t

    rows(0, 8, grow1)

    copy_rows([(b1_in, b1)], 2, 18)
    set_y1(b1, y0, y1, oy, 1)
    for j, v in enumerate(unpack_lanes(x1[pl.ds(164, 8), :], 2)):
        b1[X1 - 1 - j, pl.ds(12, 4), :] = v[0:4]
        b1[X1 - 1 - j, pl.ds(48, 4), :] = v[4:8]
    for j, v in enumerate(unpack_lanes(x1[pl.ds(172, 16), :], 2)):
        b1[X1 - 3, pl.ds(16 + 16 * j, 16), :] = v

    def add1(k):
        for j in range(2):
            ga_[1 + 2 * k + j] = u1[1 + 2 * k + j] + e1[k]

    rows(0, 8, add1)
    mid = Level(1, None, b1, gx_, gy_, gz_, gw_, 12, 52)
    mid.sweep(ga_, gb_, 2, 16)
    mid.sweep(gb_, ga_, 3, 15)

    def grow0(k):
        t = ga_[3 + k, pl.ds(8, 48), :]
        e0[k, pl.ds(0, 48, stride=2), :] = t
        e0[k, pl.ds(1, 48, stride=2), :] = t

    def add0(k):
        for j in range(2):
            ua[5 + 2 * k + j] = u0[5 + 2 * k + j] + e0[k]

    rows(0, 12, grow0, 4)
    rows(0, 12, add0, 4)
    top = Level(0, None, b, fx, fy, fz, w, 12, 84)
    top.sweep(ua, ub, 7, 27)
    top.sweep(ub, ua, 8, 26)

    def finish(x):
        to = stored(x)
        out[to] = ua[X0 + x, pl.ds(Y0, NY), :]
        res[to] = top.residual(ua, X0 + x, Y0, NY)

    rows(0, NX, finish)


def swaps(axis, first, second=None):
    count = lax.axis_size(axis)

    def pairs(start):
        return [p for i in range(start, count - 1, 2) for p in ((i, i + 1), (i + 1, i))]

    if second is None:
        return lax.ppermute(first, axis, pairs(0))
    late = lax.ppermute(second, axis, pairs(1))
    return lax.ppermute(first, axis, pairs(0)), late


def per_device(source, density, drag, porous_rows):
    sems = [pltpu.SemaphoreType.DMA((3, PARTS)), pltpu.SemaphoreType.DMA]
    block = (NX, NY, NZ)
    cond, source, p0, p1 = call(
        begin_kernel,
        [block, block, (32, 8, NZ), (32, 8, NZ)],
        [block] * 3 + [pltpu.VMEM((NY,), jnp.int32)] + sems,
        (source, density, drag, porous_rows),
        "begin",
        16,
        4,
    )
    y0, y1 = swaps("gy", p0, p1)
    q0, q1 = call(edge_kernel, [(HIGH_C + HIGH_B, NY, NZ), (LOW_C + LOW_B, NY, NZ)], [], (cond, source), "edges", 16, 0, 10**9)
    x0, x1 = swaps("gx", q0, q1)
    p0, p1 = call(corner_kernel, [(HIGH_TILES, 16, NZ), (LOW_TILES, 16, NZ)], [], (y0, y1), "corners", 16)
    k0, k1 = swaps("gx", p0, p1)
    zero, one, two = (36, 96, NZ), (18, 64, NZ), (16, 48, NZ)
    small, small1 = (18, 96, NZ), (10, 64, NZ)
    inner = call(
        inner_kernel, [small] * 8 + [small1] * 6, [(8, 96, NZ)], (cond, source, y0, y1), "inner", 16, 0, 10**10
    )
    down = call(
        down_kernel,
        [zero] * 6 + [one] * 6 + [two] * 2 + [(8, 8, NZ)] * 2,
        [zero] * 2 + [one] * 2 + [(14, 96, NZ), (17, 96, NZ), (8, 64, NZ)],
        (x0, x1, k0, k1, *inner),
        "down",
        24,
    )
    level0, level1 = down[:6], down[6:12]
    u1, c2, b2, p0, p1 = down[11:]
    y0, y1 = swaps("gy", p0, p1)
    p0, p1 = call(edge2_kernel, [(192, NZ)] * 2, [one, one, two, two], (u1, level1[4], c2, b2, y0, y1), "edges2", 16)
    x0, x1 = swaps("gx", p0, p1)
    far = swaps("gx", x1)
    *level2, u1, packed = call(
        level2_kernel,
        [two] * 6 + [one, (512, NZ)],
        [two] * 2 + [(2, 48, NZ)] * 3,
        (u1, c2, b2, y0, y1, x0, x1),
        "level2",
        16,
    )
    packed, far = lax.optimization_barrier((packed, far))
    whole = lax.all_to_all(packed, ("gx", "gy"), 0, 0, tiled=True)
    out, res = call(
        up_kernel,
        [block] * 2,
        [(6, 88, NZ), (6, 48, NZ), (8, 64, NZ), (12, 96, NZ)] + [two] * 2 + [one] * 3 + [zero] * 2,
        (whole, y0, y1, x1, far, *level2, *level1[:5], u1, *level0),
        "up",
        24,
    )
    return out, res


def solution(mesh):
    return jax.shard_map(
        per_device,
        mesh=mesh,
        in_specs=(P("gx", "gy", None), P("gx", "gy", None), P("gx", "gy", None), P("gy")),
        out_specs=(P("gx", "gy", None), P("gx", "gy", None)),
        check_vma=False,
    )
```

```python
import functools

import jax
import jax.numpy as jnp
from jax import lax
from jax.experimental import pallas as pl
from jax.experimental.pallas import tpu as pltpu
from jax.sharding import PartitionSpec as P

SWEEPS_COARSE = 16
DAMP = 0.8
KEEP = 1.0 - DAMP
H0 = 0.0002

NX, NY, NZ = 16, 64, 128
F32 = jnp.float32
VMEM = pl.BlockSpec(memory_space=pltpu.VMEM)
HBM = pl.BlockSpec(memory_space=pltpu.HBM)


def call(body, outs, scratch, args, name, vmem, hbm=0, cost=0):
    args = [pltpu.with_memory_space_constraint(a, pltpu.HBM) for a in args[:hbm]] + list(args[hbm:])
    return pl.pallas_call(
        body,
        out_shape=[jax.ShapeDtypeStruct(s, F32) for s in outs],
        in_specs=[HBM] * hbm + [VMEM] * (len(args) - hbm),
        out_specs=[VMEM] * len(outs),
        scratch_shapes=[pltpu.VMEM(s, F32) if isinstance(s, tuple) else s for s in scratch],
        compiler_params=pltpu.CompilerParams(vmem_limit_bytes=vmem * 2**20),
        name=name,
        cost_estimate=pl.CostEstimate(flops=cost, bytes_accessed=0, transcendentals=0) if cost else None,
    )(*args)


def recip(t):
    return 1.0 / t


def harmonic(a, b):
    return (2.0 * a) * b / jnp.maximum(a + b, 1e-30)


def lane(shape):
    return lax.broadcasted_iota(jnp.int32, shape, len(shape) - 1)


def lroll(v, shift):
    return pltpu.roll(v, shift % 128, v.ndim - 1)


def pair_lanes(v, s):
    first = (lane(v.shape) // s) % 2 == 0
    return v + jnp.where(first, lroll(v, -s), lroll(v, s))


def pack_lanes(tiles):
    n = len(tiles)
    out = tiles[0]
    for k in range(1, n):
        out = jnp.where(lane(out.shape) % n == k, tiles[k], out)
    return out


def unpack_lanes(p, n):
    at = lane(p.shape) % n
    moved = {d: p if d == 0 else lroll(p, -d) for d in range(1 - n, n)}
    tiles = []
    for k in range(n):
        out = moved[k]
        for m in range(1, n):
            out = jnp.where(at == m, moved[k - m], out)
        tiles.append(out)
    return tiles


def rows(lo, hi, body, unroll=8):
    whole = (hi - lo) // unroll

    def step(k, carry):
        for j in range(unroll):
            body(lo + k * unroll + j)
        return carry

    if whole > 1:
        lax.fori_loop(0, whole, step, 0)
        lo = lo + whole * unroll
    for x in range(lo, hi):
        body(x)


class Level:
    def __init__(self, depth, c, b, fx, fy, fz, w, ys, ye):
        self.h = H0 * 4.0**depth
        self.s = 2**depth
        self.c, self.b, self.fx, self.fy, self.fz, self.w = c, b, fx, fy, fz, w
        self.ys, self.n = ys, ye - ys

    def faces(self, lo, hi):
        here, above = pl.ds(self.ys, self.n), pl.ds(self.ys + 1, self.n)

        def body(x):
            c = self.c[x, here, :]
            twice, safe = c + c, c + 1e-30

            def face(other):
                return twice * other / (safe + other)

            self.fx[x, here, :] = face(self.c[x + 1, here, :])
            self.fy[x, here, :] = face(self.c[x, above, :])
            self.fz[x, here, :] = face(lroll(c, -self.s))

        rows(lo, hi, body)

    def weights(self, lo, hi, start=None):
        here, below = pl.ds(self.ys, self.n), pl.ds(self.ys - 1, self.n)

        def body(x):
            fz = self.fz[x, here, :]
            d = self.fx[x, here, :] + self.fx[x - 1, here, :]
            d = d + (self.fy[x, here, :] + self.fy[x, below, :])
            d = d + (fz + lroll(fz, self.s))
            w = DAMP * recip(self.h + d)
            self.w[x, here, :] = w
            if start is not None:
                start[x, here, :] = w * self.b[x, here, :]

        rows(lo, hi, body)

    def start(self, out, lo, hi):
        here = pl.ds(self.ys, self.n)

        def body(x):
            out[x, here, :] = self.w[x, here, :] * self.b[x, here, :]

        rows(lo, hi, body)

    def sweep(self, u, out, lo, hi):
        here = pl.ds(self.ys, self.n)
        above, below = pl.ds(self.ys + 1, self.n), pl.ds(self.ys - 1, self.n)

        def body(x):
            v = u[x, here, :]
            fz = self.fz[x, here, :]
            acc = fz * lroll(v, -self.s) + lroll(fz * v, self.s)
            acc = acc + (self.fx[x, here, :] * u[x + 1, here, :] + self.fx[x - 1, here, :] * u[x - 1, here, :])
            acc = acc + (self.fy[x, here, :] * u[x, above, :] + self.fy[x, below, :] * u[x, below, :])
            out[x, here, :] = KEEP * v + self.w[x, here, :] * (self.b[x, here, :] + acc)

        rows(lo, hi, body)

    def residual(self, u, x, y, n):
        here, above, below = pl.ds(y, n), pl.ds(y + 1, n), pl.ds(y - 1, n)
        v = u[x, here, :]
        flow = self.fz[x, here, :] * (lroll(v, -self.s) - v)
        r = self.b[x, here, :] - self.h * v
        r = r + (flow - lroll(flow, self.s))
        r = r + self.fx[x, here, :] * (u[x + 1, here, :] - v)
        r = r + self.fx[x - 1, here, :] * (u[x - 1, here, :] - v)
        r = r + self.fy[x, here, :] * (u[x, above, :] - v)
        return r + self.fy[x, below, :] * (u[x, below, :] - v)

    def halve(self, tmp, out, lo, hi, x_to, scale):
        half = tmp.shape[1] // 2

        def body(k):
            t = tmp[k, pl.ds(0, half, stride=2), :] + tmp[k, pl.ds(1, half, stride=2), :]
            out[x_to + k, pl.ds(8, half), :] = scale * pair_lanes(t, self.s)

        rows(lo, hi, body)

    def restrict(self, u, tmp, out, lo, hi, x_from, x_to):
        def body(k):
            x = x_from + 2 * k
            both = self.residual(u, x, self.ys, self.n) + self.residual(u, x + 1, self.ys, self.n)
            tmp[k, pl.ds(self.ys, self.n), :] = both

        rows(lo, hi, body, 4)
        self.halve(tmp, out, lo, hi, x_to, 0.5)

    def restrict_c(self, tmp, out, lo, hi, x_from, x_to):
        def body(k):
            x = x_from + 2 * k
            tmp[k] = self.c[x] + self.c[x + 1]

        rows(lo, hi, body)
        self.halve(tmp, out, lo, hi, x_to, 0.125)


def odd(axis):
    return lax.axis_index(axis) % 2


PARTS = 2


def stored(x):
    o = odd("gx")
    return o * (NX - 1) + (1 - 2 * o) * x


def begin_kernel(source, density, drag, porous, cond, rhs, ypack0, ypack1, dens, dra, src, por, sem, psem):
    o = odd("gy")
    at0 = pl.multiple_of((1 - o) * (NY - 8), 8)
    at1 = pl.multiple_of(o * (NY - 8), 8)
    part = NX // PARTS
    loads = []
    first = pltpu.make_async_copy(porous, por, psem)
    first.start()
    for k in range(PARTS):
        here = pl.ds(k * part, part)
        for j, (ref, dst) in enumerate(((density, dens), (drag, dra), (source, src))):
            loads.append(pltpu.make_async_copy(ref.at[here], dst.at[here], sem.at[j, k]))
            loads[-1].start()
    first.wait()
    line = jnp.broadcast_to(por[...].astype(F32)[None], (NY, NY))
    same = lax.broadcasted_iota(jnp.int32, (NY, NY), 0) == lax.broadcasted_iota(jnp.int32, (NY, NY), 1)
    mask = jnp.broadcast_to(jnp.sum(jnp.where(same, line, 0.0), axis=1, keepdims=True), (NY, NZ))
    for k in range(PARTS):
        for load in loads[3 * k : 3 * k + 3]:
            load.wait()
        for x in range(k * part, k * part + part):
            to = stored(x)
            cond[to] = recip(dens[x] * (1.0 + dra[x] * mask))
            rhs[to] = src[x]
            for pack, at in ((ypack0, at0), (ypack1, at1)):
                pack[to] = cond[to, pl.ds(at, 8), :]
                pack[NX + to] = src[x, pl.ds(at, 8), :]


HIGH_C, HIGH_B, LOW_C, LOW_B = 11, 10, 8, 6


def edge_kernel(cond, source, high, low):
    for d in range(HIGH_C):
        high[d] = cond[NX - 1 - d]
    for d in range(HIGH_B):
        high[HIGH_C + d] = source[NX - 1 - d]
    for d in range(LOW_C):
        low[d] = cond[d]
    for d in range(LOW_B):
        low[LOW_C + d] = source[d]


HIGH = (
    [(0, d, d - 1, 0) for d in (1, 2, 3, 4, 5, 6, 7)]
    + [(0, 9, 4, 2), (0, 8, 5, 3), (0, 10, 6, 1)]
    + [(1, d, d + 6, 0) for d in (1, 2, 3, 4, 5, 6)]
    + [(1, 7, 11, 3), (1, 8, 12, 2), (1, 9, 10, 1)]
)
LOW = [(0, 1, 0, 0), (0, 7, 0, 1), (0, 2, 1, 0), (0, 6, 1, 2), (0, 3, 2, 0), (0, 5, 2, 3), (0, 4, 3, 0)]
LOW += [(1, 5, 3, 1), (1, 1, 4, 0), (1, 3, 4, 3), (1, 2, 5, 0), (1, 4, 5, 2)]
HIGH_TILES, LOW_TILES = 13, 6


def turn(v, by):
    return v if by == 0 else pltpu.roll(v, by % 8, 0)


def corner_kernel(y0, y1, high, low):
    oy = odd("gy")
    at0 = pl.multiple_of((1 - oy) * 8, 8)
    at1 = pl.multiple_of(oy * 8, 8)
    row = lax.broadcasted_iota(jnp.int32, (8, NZ), 0)
    for pack, corners, count, side in ((high, HIGH, HIGH_TILES, 1), (low, LOW, LOW_TILES, 0)):
        for y, at, above in ((y0, at0, 1 - oy), (y1, at1, oy)):
            tiles = {}
            for field, d, t, by in corners:
                v = y[field * NX + (NX - d if side else d - 1)]
                if by == 0:
                    tiles[t] = v
                else:
                    under = jnp.where(row < by, turn(v, by), tiles[t])
                    over = jnp.where(row >= 8 - by, turn(v, -by), tiles[t])
                    tiles[t] = jnp.where(above == 1, over, under)
            for t in range(count):
                pack[t, pl.ds(at, 8), :] = tiles[t]


X0, Y0 = 9, 16
X1, Y1 = 5, 16
X2, Y2 = 6, 16


def levels_down(c, b, fx, fy, fz, w, c1, b1, gx_, gy_, gz_, gw_):
    top = Level(0, c, b, fx, fy, fz, w, 8, 88)
    return top, Level(1, c1, b1, gx_, gy_, gz_, gw_, 12, 52)


def inner_kernel(cond, source, y0, y1, c, b, fx, fy, fz, w, ua, ub, c1, b1, gx_, gy_, gz_, gw_, tmp):
    oy = odd("gy")
    at0 = pl.multiple_of(8 + (1 - oy) * (NY + 8), 8)
    at1 = pl.multiple_of(8 + oy * (NY + 8), 8)

    def own(x):
        c[1 + x, pl.ds(Y0, NY), :] = cond[x]
        c[1 + x, pl.ds(at0, 8), :] = y0[x]
        c[1 + x, pl.ds(at1, 8), :] = y1[x]
        b[1 + x, pl.ds(Y0, NY), :] = source[x]
        b[1 + x, pl.ds(at0, 8), :] = y0[NX + x]
        b[1 + x, pl.ds(at1, 8), :] = y1[NX + x]

    rows(0, NX, own)
    top, mid = levels_down(c, b, fx, fy, fz, w, c1, b1, gx_, gy_, gz_, gw_)
    top.faces(1, 17)
    top.weights(2, 16, ua)
    top.sweep(ua, ub, 3, 15)
    top.restrict_c(tmp, c1, 0, 8, 1, 1)
    top.restrict(ub, tmp, b1, 2, 6, 1, 1)
    mid.faces(1, 9)
    mid.weights(2, 8)


def down_kernel(
    x0, x1, k0, k1, c_in, b_in, fx_in, fy_in, fz_in, w_in, ua_in, ub_in, c1_in, b1_in, gx_in, gy_in, gz_in, gw_in,
    fx, fy, fz, w, b, ub, gx_, gy_, gz_, gw_, b1, u1, c2, b2, ypack0, ypack1,
    c, ua, c1, ga_, tmp, ctmp, tmp1,
):
    oy = odd("gy")
    here, here1 = pl.ds(8, 80), pl.ds(12, 40)
    sides = ((x0, k0, HIGH, HIGH_C, HIGH_B, X0 + NX - 1, 1), (x1, k1, LOW, LOW_C, LOW_B, X0, -1))
    for x, pack, corners, nc, nb, edge, sign in sides:
        for d in range(1, nc + 1):
            c[edge + sign * d, pl.ds(Y0, NY), :] = x[d - 1]
        for d in range(1, nb + 1):
            b[edge + sign * d, pl.ds(Y0, NY), :] = x[nc + d - 1]
        for field, d, t, by in corners:
            ref = (c, b)[field]
            ref[edge + sign * d, pl.ds(8, 8), :] = turn(pack[t, pl.ds(0, 8), :], -by)
            ref[edge + sign * d, pl.ds(80, 8), :] = turn(pack[t, pl.ds(8, 8), :], by)
    for x in (1, 16):
        c[x + 8, here, :] = c_in[x, here, :]
    for x in (2, 3, 14, 15):
        ua[x + 8, here, :] = ua_in[x, here, :]

    def fill(x):
        for ref, src in ((fx, fx_in), (fy, fy_in), (fz, fz_in), (w, w_in), (b, b_in), (ub, ub_in)):
            ref[x + 8, here, :] = src[x, here, :]

    rows(1, 17, fill)
    for x in range(1, 9):
        c1[x + 4, here1, :] = c1_in[x, here1, :]
        for ref, src in ((gx_, gx_in), (gy_, gy_in), (gz_, gz_in), (gw_, gw_in), (b1, b1_in)):
            ref[x + 4, here1, :] = src[x, here1, :]

    top, mid = levels_down(c, b, fx, fy, fz, w, c1, b1, gx_, gy_, gz_, gw_)
    top.faces(2, 9)
    top.faces(24, 35)
    top.weights(3, 10, ua)
    top.weights(24, 35, ua)
    top.sweep(ua, ub, 4, 11)
    top.sweep(ua, ub, 23, 34)
    top.restrict_c(ctmp, c1, 0, 4, 1, 1)
    top.restrict_c(ctmp, c1, 12, 17, 1, 1)
    top.restrict(ub, tmp, b1, 0, 4, 5, 3)
    top.restrict(ub, tmp, b1, 8, 14, 5, 3)

    mid.faces(1, 5)
    mid.faces(12, 17)
    mid.weights(2, 6)
    mid.weights(12, 17)
    mid.start(ga_, 3, 17)
    mid.sweep(ga_, u1, 4, 16)
    mid.restrict(u1, tmp1, b2, 0, 5, 5, X2)
    mid.restrict_c(tmp1, c2, 0, 8, 1, X2 - 2)

    e0 = Y1 + (1 - oy) * 28
    e1 = Y1 + oy * 28
    f0 = pl.multiple_of(Y2 + (1 - oy) * 8, 8)
    f1 = pl.multiple_of(Y2 + oy * 8, 8)
    for pack, e, f in ((ypack0, e0, f0), (ypack1, e1, f1)):
        for k in range(4):
            x = X1 + 2 * k
            pack[k, pl.ds(0, 4), :] = pack_lanes([u1[x + j, pl.ds(e, 4), :] for j in range(2)])
            pack[k, pl.ds(4, 4), :] = pack_lanes([b1[x + j, pl.ds(e, 4), :] for j in range(2)])
        for k in range(2):
            pack[4 + k] = pack_lanes([b2[X2 + min(4 * k + j, 4), pl.ds(f, 8), :] for j in range(4)])
            pack[6 + k] = pack_lanes([c2[X2 - 2 + 4 * k + j, pl.ds(f, 8), :] for j in range(4)])


def set_y1(ref, y0, y1, oy, part):
    a0 = Y1 - 4 + (1 - oy) * 36
    a1 = Y1 - 4 + oy * 36
    for y, a in ((y0, a0), (y1, a1)):
        for k in range(4):
            for j, v in enumerate(unpack_lanes(y[k], 2)):
                ref[X1 + 2 * k + j, pl.ds(a, 4), :] = v[4 * part : 4 * part + 4]


def set_y2(c2, b2, y0, y1, oy):
    a0 = pl.multiple_of(Y2 - 8 + (1 - oy) * 24, 8)
    a1 = pl.multiple_of(Y2 - 8 + oy * 24, 8)
    for y, a in ((y0, a0), (y1, a1)):
        for k in range(2):
            for j, v in enumerate(unpack_lanes(y[4 + k], 4)):
                if 4 * k + j < 5:
                    b2[X2 + 4 * k + j, pl.ds(a, 8), :] = v
            for j, v in enumerate(unpack_lanes(y[6 + k], 4)):
                c2[X2 - 2 + 4 * k + j, pl.ds(a, 8), :] = v


def copy_rows(pairs, lo, hi, y, n):
    here = pl.ds(y, n)

    def body(x):
        for src, dst in pairs:
            dst[x, here, :] = src[x, here, :]

    rows(lo, hi, body)


def edge2_kernel(u1_in, b1_in, c2_in, b2_in, y0, y1, high, low, u1, b1, c2, b2):
    oy = odd("gy")
    copy_rows([(u1_in, u1), (b1_in, b1)], X1, X1 + 8, Y1, 32)
    copy_rows([(c2_in, c2)], X2 - 2, X2 + 6, Y2, 16)
    copy_rows([(b2_in, b2)], X2, X2 + 5, Y2, 16)
    set_y1(u1, y0, y1, oy, 0)
    set_y1(b1, y0, y1, oy, 1)
    set_y2(c2, b2, y0, y1, oy)
    for pack, edge1, edge2, sign in ((high, X1 + 7, X2 + 3, -1), (low, X1, X2, 1)):
        for k in range(2):
            t = [u1[edge1 + sign * (2 * k + j), pl.ds(12, 40), :] for j in range(2)]
            pack[pl.ds(k * 40, 40), :] = pack_lanes(t)
        t = [c2[edge2 + sign * d, pl.ds(10, 28), :] for d in range(6)]
        t += [b2[edge2 + sign * d, pl.ds(10, 28), :] for d in range(5 if sign == 1 else 4)]
        t += t[:1] * (12 - len(t))
        for k in range(3):
            pack[pl.ds(80 + k * 28, 28), :] = pack_lanes(t[4 * k : 4 * k + 4])
        for n, y in enumerate((12, 48)):
            t = [b1[edge1 + sign * j, pl.ds(y, 4), :] for j in range(2)]
            pack[pl.ds(164 + 4 * n, 4), :] = pack_lanes(t)
        t = [b1[edge1 + sign * 2, pl.ds(16 + 16 * j, 16), :] for j in range(2)]
        pack[pl.ds(172, 16), :] = pack_lanes(t)


def one_hot(shape, f):
    i = lax.broadcasted_iota(jnp.int32, shape, 0)
    j = lax.broadcasted_iota(jnp.int32, shape, 1)
    return jnp.where(f(i, j), 1.0, 0.0).astype(F32)


def halves(v):
    high = v.astype(jnp.bfloat16)
    return high, (v - high.astype(F32)).astype(jnp.bfloat16)


def pick_dot(a, b):
    a1, rest = halves(a)[0], a - halves(a)[0].astype(F32)
    a2, a3 = halves(rest)
    b = b.astype(jnp.bfloat16)
    return jnp.dot(jnp.concatenate([a1, a2, a3], 1), jnp.concatenate([b, b, b], 0), preferred_element_type=F32)


def split_dot(a, b):
    (a1, a2), (b1, b2) = halves(a), halves(b)
    return jnp.dot(jnp.concatenate([a1, a2, a1], 1), jnp.concatenate([b1, b1, b2], 0), preferred_element_type=F32)


def level2_kernel(
    u1_in, c2_in, b2_in, y0, y1, x0, x1,
    fx, fy, fz, w, b2, u2, u1, gather,
    c2, ua, tmp, b3, c3,
):
    ox, oy = odd("gx"), odd("gy")
    copy_rows([(u1_in, u1)], X1, X1 + 8, Y1, 32)
    copy_rows([(c2_in, c2)], X2 - 2, X2 + 6, Y2, 16)
    copy_rows([(b2_in, b2)], X2, X2 + 5, Y2, 16)
    set_y1(u1, y0, y1, oy, 0)
    set_y2(c2, b2, y0, y1, oy)
    for pack, edge1, edge2, sign in ((x0, X1 + 7, X2 + 3, 1), (x1, X1, X2, -1)):
        for k in range(2):
            for j, v in enumerate(unpack_lanes(pack[pl.ds(k * 40, 40), :], 2)):
                u1[edge1 + sign * (2 * k + j + 1), pl.ds(12, 40), :] = v
        t = []
        for k in range(3):
            t += unpack_lanes(pack[pl.ds(80 + k * 28, 28), :], 4)
        for d in range(6):
            c2[edge2 + sign * (d + 1), pl.ds(10, 28), :] = t[d]
        for d in range(5 if sign == -1 else 4):
            b2[edge2 + sign * (d + 1), pl.ds(10, 28), :] = t[6 + d]

    low = Level(2, c2, b2, fx, fy, fz, w, 8, 40)
    low.faces(0, 15)
    low.weights(1, 15, ua)
    low.sweep(ua, u2, 2, 14)
    low.restrict(u2, tmp, b3, 0, 2, X2, 0)
    low.restrict_c(tmp, c3, 0, 2, X2, 0)
    both = jnp.concatenate(
        [b3[0, pl.ds(16, 8), :], b3[1, pl.ds(16, 8), :], c3[0, pl.ds(16, 8), :], c3[1, pl.ds(16, 8), :]], 0
    )
    spread = pick_dot(both, one_hot((NZ, NZ), lambda i, j: i == 8 * (j % 16)))
    shape = (8, NZ)
    mine = lane(shape) // 16 == lax.broadcasted_iota(jnp.int32, shape, 0)
    packed = [
        jnp.sum(jnp.where(mine, spread[8 * k : 8 * k + 8], 0.0), axis=0, keepdims=True) for k in range(4)
    ]
    packed = [jnp.where(ox == 1, packed[k ^ 1], packed[k]) for k in range(4)]
    eight = jnp.concatenate(packed + packed, 0)

    def body(k):
        gather[pl.ds(pl.multiple_of(8 * k, 8), 8), :] = eight

    rows(0, 64, body, 8)


class Whole:
    def __init__(self, depth, b, c):
        self.h = H0 * 4.0**depth
        self.s = 2 ** (depth - 3)
        self.st = 16 * self.s
        self.b = b
        n = c.shape[0]
        sub = lax.broadcasted_iota(jnp.int32, (1,) + c.shape[1:], 2)
        up = self.xp(c)
        end = jnp.where(sub == 7, 0.0, up[n - 1 :])
        up = jnp.concatenate([up[: n - 1], end], 0) if n > 1 else end
        self.fxp = harmonic(c, up)
        up = self.yp(c)
        last = up[:, 3:]
        last = jnp.where(lane(last.shape) >= 128 - self.st, 0.0, last)
        self.fyp = harmonic(c, jnp.concatenate([up[:, :3], last], 1))
        self.fzp = harmonic(c, self.zp(c))
        self.fxm, self.fym, self.fzm = self.xm(self.fxp), self.ym(self.fyp), self.zm(self.fzp)
        d = self.h + self.fxp + self.fxm + self.fyp + self.fym + self.fzp + self.fzm
        self.w = DAMP * recip(d)

    def xp(self, v):
        wrap = pltpu.roll(v[:1], 7, 2)
        return jnp.concatenate([v[1:], wrap], 0) if v.shape[0] > 1 else wrap

    def xm(self, v):
        n = v.shape[0]
        wrap = pltpu.roll(v[n - 1 :], 1, 2)
        return jnp.concatenate([wrap, v[: n - 1]], 0) if n > 1 else wrap

    def yp(self, v):
        w = v if self.st == 128 else lroll(v, -self.st)
        far = jnp.concatenate([w[:, 1:], w[:, :1]], 1)
        return far if self.st == 128 else jnp.where(lane(v.shape) < 128 - self.st, w, far)

    def ym(self, v):
        w = v if self.st == 128 else lroll(v, self.st)
        far = jnp.concatenate([w[:, 3:], w[:, :3]], 1)
        return far if self.st == 128 else jnp.where(lane(v.shape) >= self.st, w, far)

    def zp(self, v):
        s = self.s
        return jnp.where(lane(v.shape) % 16 < 16 - s, lroll(v, -s), lroll(v, 16 - s))

    def zm(self, v):
        s = self.s
        return self.zp(v) if s == 8 else jnp.where(lane(v.shape) % 16 >= s, lroll(v, s), lroll(v, s - 16))

    def flux(self, v):
        acc = self.fxp * self.xp(v) + self.fxm * self.xm(v)
        acc = acc + self.fyp * self.yp(v) + self.fym * self.ym(v)
        return acc + self.fzp * self.zp(v) + self.fzm * self.zm(v)

    def sweep(self, v):
        return KEEP * v + self.w * (self.b + self.flux(v))

    def residual(self, v):
        r = self.b - self.h * v
        r = r + self.fxp * (self.xp(v) - v) + self.fxm * (self.xm(v) - v)
        r = r + self.fyp * (self.yp(v) - v) + self.fym * (self.ym(v) - v)
        return r + self.fzp * (self.zp(v) - v) + self.fzm * (self.zm(v) - v)

    def coarse(self, v, scale):
        v = jnp.concatenate([v[2 * k : 2 * k + 1] + v[2 * k + 1 : 2 * k + 2] for k in range(v.shape[0] // 2)], 0)
        return scale * pair_lanes(pair_lanes(v, self.s), self.st)


def coarsest(level, g):
    def column(v):
        v = v.reshape(32, NZ)
        low = lane(v.shape) % 16 < 8
        return jnp.concatenate([jnp.where(low, v, lroll(v, 8)), jnp.where(low, lroll(v, -8), v)], 0)

    shape = (64, NZ)
    i, j = lax.broadcasted_iota(jnp.int32, shape, 0), lane(shape)

    def pad(v):
        return jnp.concatenate([v, jnp.zeros(shape, F32)], 0)

    m = jnp.where(i == j, KEEP, 0.0)
    w = level.w
    for coef, at in (
        (w * level.fxp, i + 1),
        (w * level.fxm, i - 1),
        (w * level.fyp, i + 8),
        (w * level.fym, i - 8),
        (w * (level.fzp + level.fzm), i ^ 32),
    ):
        m = m + jnp.where(j == at, column(coef), 0.0)
    total = m + jnp.where(i == j, 1.0, 0.0)
    for _ in range(3):
        m = split_dot(m, pad(m))
        total = total + split_dot(m, pad(total))
    u = split_dot(total, pad(column(g)))
    low = lane((32, NZ)) % 16 < 8
    return jnp.where(low, u[:32], u[32:]).reshape(g.shape)


def whole_cycle(depth, b, c):
    level = Whole(depth, b, c)
    v = level.w * b
    if depth == 6:
        return coarsest(level, v)
    v = level.sweep(v)
    below = whole_cycle(depth + 1, level.coarse(level.residual(v), 0.5), level.coarse(c, 0.125))
    v = v + jnp.concatenate([below[k // 2 : k // 2 + 1] for k in range(v.shape[0])], 0)
    return level.sweep(level.sweep(v))


def up_kernel(
    gather, y0, y1, x1, far,
    hx, hy, hz, hw, b2, u2,
    gx_, gy_, gz_, gw_, b1_in, u1,
    fx, fy, fz, w, b, u0,
    out, res,
    s3, e2, e1, e0, ha, hb, b1, ga_, gb_, ua, ub,
):
    ix, iy = lax.axis_index("gx"), lax.axis_index("gy")
    ox, oy = ix % 2, iy % 2
    low = Level(2, None, b2, hx, hy, hz, hw, 12, 36)
    wide = pl.ds(8, 32)
    low.start(ha, X2 + 6, X2 + 8)
    ha[X2 + 8, pl.ds(10, 28), :] = hw[X2 + 8, pl.ds(10, 28), :] * unpack_lanes(far[pl.ds(108, 28), :], 4)[2]
    low.sweep(ha, hb, X2 + 7, X2 + 8)

    def field(k):
        return jnp.stack(
            [
                jnp.stack([gather[pl.ds(xq * 16 + g * 4 + k + xl, 8, stride=64), :] for g in range(4)], 0)
                for xq in range(4)
                for xl in range(2)
            ],
            0,
        )

    u3 = whole_cycle(3, field(0), field(2))
    s3[...] = jnp.zeros(s3.shape, F32)
    for xlo in range(8):
        for g in range(4):
            s3[g + 1, pl.ds(8 + xlo, 8, stride=8), :] = u3[xlo, g]
    shape = (8, NZ)
    mine = lane(shape) // 16 == lax.broadcasted_iota(jnp.int32, shape, 0)
    tiles = []
    for k in range(6):
        for g in range(3):
            row = s3[iy + g, pl.ds(2 * ix + 6 + 5 * ox + (1 - 2 * ox) * k, 1), :]
            tiles.append(jnp.where(mine, jnp.broadcast_to(row, shape), 0.0))
    spread = pick_dot(jnp.concatenate(tiles, 0), one_hot((NZ, NZ), lambda i, j: i % 16 == j // 8))
    for k in range(6):
        t = spread[24 * k : 24 * k + 24]
        e2[k, pl.ds(0, 24, stride=2), :] = t
        e2[k, pl.ds(1, 24, stride=2), :] = t

    for x in range(2, 14):
        ha[x, wide, :] = (hb if x == X2 + 7 else u2)[x, wide, :] + e2[(x - 2) // 2, wide, :]
    low.sweep(ha, hb, 3, 13)
    low.sweep(hb, ha, 4, 12)

    def grow1(k):
        t = ha[4 + k, pl.ds(8, 32), :]
        e1[k, pl.ds(0, 32, stride=2), :] = t
        e1[k, pl.ds(1, 32, stride=2), :] = t

    rows(0, 8, grow1)

    copy_rows([(b1_in, b1)], 2, 18, 8, 48)
    set_y1(b1, y0, y1, oy, 1)
    for j, v in enumerate(unpack_lanes(x1[pl.ds(164, 8), :], 2)):
        b1[X1 - 1 - j, pl.ds(12, 4), :] = v[0:4]
        b1[X1 - 1 - j, pl.ds(48, 4), :] = v[4:8]
    for j, v in enumerate(unpack_lanes(x1[pl.ds(172, 16), :], 2)):
        b1[X1 - 3, pl.ds(16 + 16 * j, 16), :] = v

    def add1(k):
        for j in range(2):
            ga_[1 + 2 * k + j] = u1[1 + 2 * k + j] + e1[k]

    rows(0, 8, add1)
    mid = Level(1, None, b1, gx_, gy_, gz_, gw_, 12, 52)
    mid.sweep(ga_, gb_, 2, 16)
    mid.sweep(gb_, ga_, 3, 15)

    def grow0(k):
        t = ga_[3 + k, pl.ds(8, 48), :]
        e0[k, pl.ds(0, 48, stride=2), :] = t
        e0[k, pl.ds(1, 48, stride=2), :] = t

    def add0(k):
        for j in range(2):
            ua[5 + 2 * k + j] = u0[5 + 2 * k + j] + e0[k]

    rows(0, 12, grow0, 4)
    rows(0, 12, add0, 4)
    top = Level(0, None, b, fx, fy, fz, w, 12, 84)
    top.sweep(ua, ub, 7, 27)
    top.sweep(ub, ua, 8, 26)

    def finish(x):
        to = stored(x)
        out[to] = ua[X0 + x, pl.ds(Y0, NY), :]
        res[to] = top.residual(ua, X0 + x, Y0, NY)

    rows(0, NX, finish)


def swaps(axis, first, second=None):
    count = lax.axis_size(axis)

    def pairs(start):
        return [p for i in range(start, count - 1, 2) for p in ((i, i + 1), (i + 1, i))]

    if second is None:
        return lax.ppermute(first, axis, pairs(0))
    late = lax.ppermute(second, axis, pairs(1))
    return lax.ppermute(first, axis, pairs(0)), late


def per_device(source, density, drag, porous_rows):
    sems = [pltpu.SemaphoreType.DMA((3, PARTS)), pltpu.SemaphoreType.DMA]
    block = (NX, NY, NZ)
    cond, source, p0, p1 = call(
        begin_kernel,
        [block, block, (32, 8, NZ), (32, 8, NZ)],
        [block] * 3 + [pltpu.VMEM((NY,), jnp.int32)] + sems,
        (source, density, drag, porous_rows),
        "begin",
        16,
        4,
    )
    y0, y1 = swaps("gy", p0, p1)
    q0, q1 = call(edge_kernel, [(HIGH_C + HIGH_B, NY, NZ), (LOW_C + LOW_B, NY, NZ)], [], (cond, source), "edges", 16, 0, 10**9)
    x0, x1 = swaps("gx", q0, q1)
    p0, p1 = call(corner_kernel, [(HIGH_TILES, 16, NZ), (LOW_TILES, 16, NZ)], [], (y0, y1), "corners", 16)
    k0, k1 = swaps("gx", p0, p1)
    zero, one, two = (36, 96, NZ), (18, 64, NZ), (16, 48, NZ)
    small, small1 = (18, 96, NZ), (10, 64, NZ)
    inner = call(
        inner_kernel, [small] * 8 + [small1] * 6, [(8, 96, NZ)], (cond, source, y0, y1), "inner", 16, 0, 10**10
    )
    down = call(
        down_kernel,
        [zero] * 6 + [one] * 6 + [two] * 2 + [(8, 8, NZ)] * 2,
        [zero] * 2 + [one] * 2 + [(14, 96, NZ), (17, 96, NZ), (8, 64, NZ)],
        (x0, x1, k0, k1, *inner),
        "down",
        24,
    )
    level0, level1 = down[:6], down[6:12]
    u1, c2, b2, p0, p1 = down[11:]
    y0, y1 = swaps("gy", p0, p1)
    p0, p1 = call(edge2_kernel, [(192, NZ)] * 2, [one, one, two, two], (u1, level1[4], c2, b2, y0, y1), "edges2", 16)
    x0, x1 = swaps("gx", p0, p1)
    far = swaps("gx", x1)
    *level2, u1, packed = call(
        level2_kernel,
        [two] * 6 + [one, (512, NZ)],
        [two] * 2 + [(2, 48, NZ)] * 3,
        (u1, c2, b2, y0, y1, x0, x1),
        "level2",
        16,
    )
    packed, far = lax.optimization_barrier((packed, far))
    whole = lax.all_to_all(packed, ("gx", "gy"), 0, 0, tiled=True)
    out, res = call(
        up_kernel,
        [block] * 2,
        [(6, 88, NZ), (6, 48, NZ), (8, 64, NZ), (12, 96, NZ)] + [two] * 2 + [one] * 3 + [zero] * 2,
        (whole, y0, y1, x1, far, *level2, *level1[:5], u1, *level0),
        "up",
        24,
    )
    return out, res


def solution(mesh):
    return jax.shard_map(
        per_device,
        mesh=mesh,
        in_specs=(P("gx", "gy", None), P("gx", "gy", None), P("gx", "gy", None), P("gy")),
        out_specs=(P("gx", "gy", None), P("gx", "gy", None)),
        check_vma=False,
    )
```
